32 devices in a mesh: dp: 2 (over x), slab: 16 (over z, y, core).
Axes of the slice: x: 2, y: 2, z: 4, core: 2. Of those that a mesh axis runs over, the one named last changes fastest.
Arguments:
- field: float32 [2, 32, 128, 128, 128], P('dp', None, 'slab'), may hold values from -6 to 6
- cotangent: float32 [2, 32, 128, 128, 128], P('dp', None, 'slab'), may hold values from -6 to 6
- spec_weight: float32 [2, 32, 512, 1024], P(None, None, 'slab'), may hold values from -8 to 8
- bypass_weight: float32 [32, 32], replicated, may hold values from -1 to 1
Outputs:
- layer_out: float32 [2, 32, 128, 128, 128], P('dp', None, 'slab')
- grad_field: float32 [2, 32, 128, 128, 128], P('dp', None, 'slab')
- grad_spec: float32 [2, 32, 512, 1024], P(None, None, 'slab')
The draws below stay inside these ranges and needn't reach their ends.
All inputs are finite; a program needn't handle non-finite values.
Results may differ from the reference program's by a relative error of at most 0.0001.
Values sent between devices are 32-bit elements; how exact they have to be, the bound alone decides.
No kernel may reach another device: no remote copies, remote signals or barrier semaphores. Data moves between devices by JAX's collectives and lax.ppermute only.
A program may use at most 384 MiB of HBM per device.

```python
import math
import jax
import jax.numpy as jnp
from jax import lax

GX = 128
GY = 128
GZ = 128
CHANNELS = 32
KX = 32
KY = 32
KZ = 16
SAMPLES = 2
MODES_YZ = 512


def level_of(key, extent, cuts, low, high):
    def one(position, shards_of):
        heights = jax.random.uniform(jax.random.fold_in(jax.random.fold_in(key, 6), position), (shards_of,), jnp.float32, low / len(cuts), high / len(cuts))
        return jnp.repeat(jnp.exp(heights), extent[position] // shards_of).reshape((-1,) + (1,) * (len(extent) - position - 1))

    factor_of = one(*cuts[0])
    for cut in cuts[1:]:
        factor_of = factor_of * one(*cut)
    return factor_of


def gaussian(own_key, dims, deviation, limit, split=(), held_as=jnp.bfloat16):
    factor_of = level_of(own_key, dims, split, -0.22, 0.18) if split else 1.0
    values = jax.random.normal(own_key, dims, jnp.float32) * deviation * factor_of
    return jnp.minimum(jnp.maximum(values, -limit), limit).astype(held_as)


def setup_inputs(seed: int = 0) -> dict:
    arg_keys = jax.random.split(jax.random.key(seed), 5)
    field = gaussian(arg_keys[0], (SAMPLES, CHANNELS, GX, GY, GZ), 1.0, 6.0, ((0, 2), (2, 16)), jnp.float32)
    cotangent = gaussian(arg_keys[1], (SAMPLES, CHANNELS, GX, GY, GZ), 1.0, 6.0, ((0, 2), (2, 16)), jnp.float32)
    spec_weight = gaussian(arg_keys[2], (2, CHANNELS, MODES_YZ, KX * CHANNELS), 1.4, 8.0, ((2, 16),), jnp.float32)
    bypass_weight = gaussian(arg_keys[3], (CHANNELS, CHANNELS), CHANNELS ** -0.5, 1.0, (), jnp.float32)
    return dict(field=field, cotangent=cotangent, spec_weight=spec_weight, bypass_weight=bypass_weight)


precise = lax.Precision.HIGHEST

def wave_tables(length, count, signed):
    positions = jnp.arange(length, dtype=jnp.int32)
    indices = jnp.arange(count, dtype=jnp.int32)
    if signed:
        freqs = jnp.where(indices < count // 2, indices, indices - count).astype(jnp.int32)
    else:
        freqs = indices
    phase = positions[:, None] * freqs[None, :] % length
    angle = phase.astype(jnp.float32) * (2.0 * math.pi / length)
    return (jnp.cos(angle), jnp.sin(angle))

def gelu_exact(values):
    return jax.nn.gelu(values, approximate=False)

def forward_spectrum(data, tables):
    z_cos, z_sin, y_cos, y_sin, x_cos, x_sin = tables
    part_re = jnp.einsum('cxyz,zk->cxyk', data, z_cos, precision=precise)
    part_im = -jnp.einsum('cxyz,zk->cxyk', data, z_sin, precision=precise)
    mid_re = jnp.einsum('cxyk,yj->cxjk', part_re, y_cos, precision=precise) + jnp.einsum('cxyk,yj->cxjk', part_im, y_sin, precision=precise)
    mid_im = jnp.einsum('cxyk,yj->cxjk', part_im, y_cos, precision=precise) - jnp.einsum('cxyk,yj->cxjk', part_re, y_sin, precision=precise)
    full_re = jnp.einsum('cxjk,xi->cijk', mid_re, x_cos, precision=precise) + jnp.einsum('cxjk,xi->cijk', mid_im, x_sin, precision=precise)
    full_im = jnp.einsum('cxjk,xi->cijk', mid_im, x_cos, precision=precise) - jnp.einsum('cxjk,xi->cijk', mid_re, x_sin, precision=precise)
    return (full_re, full_im)

def inverse_spectrum(spec_re, spec_im, weight, tables):
    z_cos, z_sin, y_cos, y_sin, x_cos, x_sin = tables
    wide_re = jnp.einsum('cijk,xi->cxjk', spec_re, x_cos, precision=precise) - jnp.einsum('cijk,xi->cxjk', spec_im, x_sin, precision=precise)
    wide_im = jnp.einsum('cijk,xi->cxjk', spec_re, x_sin, precision=precise) + jnp.einsum('cijk,xi->cxjk', spec_im, x_cos, precision=precise)
    plane_re = jnp.einsum('cxjk,yj->cxyk', wide_re, y_cos, precision=precise) - jnp.einsum('cxjk,yj->cxyk', wide_im, y_sin, precision=precise)
    plane_im = jnp.einsum('cxjk,yj->cxyk', wide_re, y_sin, precision=precise) + jnp.einsum('cxjk,yj->cxyk', wide_im, y_cos, precision=precise)
    plane_re = plane_re * weight
    plane_im = plane_im * weight
    return jnp.einsum('cxyk,zk->cxyz', plane_re, z_cos, precision=precise) - jnp.einsum('cxyk,zk->cxyz', plane_im, z_sin, precision=precise)

def reference(field, cotangent, spec_weight, bypass_weight):
    z_cos, z_sin = wave_tables(GZ, KZ, False)
    y_cos, y_sin = wave_tables(GY, KY, True)
    x_cos, x_sin = wave_tables(GX, KX, True)
    tables = (z_cos, z_sin, y_cos, y_sin, x_cos, x_sin)
    kz_index = jnp.arange(KZ, dtype=jnp.int32)
    fold = jnp.where(kz_index == 0, 1.0, 2.0).astype(jnp.float32) / float(GX * GY * GZ)
    ones = jnp.ones((KZ,), jnp.float32)
    weights = spec_weight.reshape(2, CHANNELS, KY, KZ, KX, CHANNELS)
    w_real = weights[0]
    w_imag = weights[1]
    grad_real = jnp.zeros((CHANNELS, KY, KZ, KX, CHANNELS), jnp.float32)
    grad_imag = jnp.zeros((CHANNELS, KY, KZ, KX, CHANNELS), jnp.float32)
    outputs = []
    field_grads = []
    for sample in range(SAMPLES):
        source = field[sample]
        hat_re, hat_im = forward_spectrum(source, tables)
        mix_re = jnp.einsum('cijk,cjkio->oijk', hat_re, w_real, precision=precise) - jnp.einsum('cijk,cjkio->oijk', hat_im, w_imag, precision=precise)
        mix_im = jnp.einsum('cijk,cjkio->oijk', hat_re, w_imag, precision=precise) + jnp.einsum('cijk,cjkio->oijk', hat_im, w_real, precision=precise)
        spectral = inverse_spectrum(mix_re, mix_im, fold, tables)
        pre = spectral + jnp.einsum('co,cxyz->oxyz', bypass_weight, source, precision=precise)
        result, pullback = jax.vjp(gelu_exact, pre)
        grad_pre = pullback(cotangent[sample])[0]
        grad_re, grad_im = forward_spectrum(grad_pre, tables)
        grad_re = grad_re * fold
        grad_im = grad_im * fold
        grad_real = grad_real + jnp.einsum('cijk,oijk->cjkio', hat_re, grad_re, precision=precise) + jnp.einsum('cijk,oijk->cjkio', hat_im, grad_im, precision=precise)
        grad_imag = grad_imag + jnp.einsum('cijk,oijk->cjkio', hat_re, grad_im, precision=precise) - jnp.einsum('cijk,oijk->cjkio', hat_im, grad_re, precision=precise)
        input_re = jnp.einsum('oijk,cjkio->cijk', grad_re, w_real, precision=precise) + jnp.einsum('oijk,cjkio->cijk', grad_im, w_imag, precision=precise)
        input_im = jnp.einsum('oijk,cjkio->cijk', grad_im, w_real, precision=precise) - jnp.einsum('oijk,cjkio->cijk', grad_re, w_imag, precision=precise)
        back_field = inverse_spectrum(input_re, input_im, ones, tables)
        back_field = back_field + jnp.einsum('co,oxyz->cxyz', bypass_weight, grad_pre, precision=precise)
        outputs.append(result)
        field_grads.append(back_field)
    grad_spec = jnp.stack([grad_real, grad_imag]).reshape(2, CHANNELS, KY * KZ, KX * CHANNELS)
    return (jnp.stack(outputs), jnp.stack(field_grads), grad_spec)
```

```python
import functools
import math

import jax
import jax.numpy as jnp
import ml_dtypes
import numpy as np
from jax import lax
from jax.experimental import pallas as pl
from jax.experimental.pallas import tpu as pltpu
from jax.sharding import PartitionSpec as P

GX = 128
GY = 128
GZ = 128
KX = 32
KY = 32
KZ = 16


precise = lax.Precision.HIGHEST


def wave_tables(length, count, signed):
    positions = jnp.arange(length, dtype=jnp.int32)
    indices = jnp.arange(count, dtype=jnp.int32)
    if signed:
        freqs = jnp.where(indices < count // 2, indices, indices - count)
    else:
        freqs = indices
    phase = positions[:, None] * freqs[None, :] % length
    angle = phase.astype(jnp.float32) * (2.0 * math.pi / length)
    return (jnp.cos(angle), jnp.sin(angle))


def gelu_exact(values):
    return jax.nn.gelu(values, approximate=False)


def plane_spectrum(data, weight, z_cos, z_sin, y_cos, y_sin):
    chans, planes = (data.shape[0], data.shape[1])
    part_re = jnp.einsum("cxyz,zk->cxky", data, z_cos, precision=precise)
    part_im = -jnp.einsum("cxyz,zk->cxky", data, z_sin, precision=precise)
    mid_re = jnp.einsum("cxky,yj->cxjk", part_re, y_cos, precision=precise) + jnp.einsum(
        "cxky,yj->cxjk", part_im, y_sin, precision=precise
    )
    mid_im = jnp.einsum("cxky,yj->cxjk", part_im, y_cos, precision=precise) - jnp.einsum(
        "cxky,yj->cxjk", part_re, y_sin, precision=precise
    )
    stacked = jnp.stack([mid_re * weight, mid_im * weight])
    return stacked.reshape(2, chans, planes, KY * KZ)


def along_first(moved, x_cos, x_sin):
    line_re, line_im = (moved[0], moved[1])
    full_re = jnp.einsum("cxp,xi->cpi", line_re, x_cos, precision=precise) + jnp.einsum(
        "cxp,xi->cpi", line_im, x_sin, precision=precise
    )
    full_im = jnp.einsum("cxp,xi->cpi", line_im, x_cos, precision=precise) - jnp.einsum(
        "cxp,xi->cpi", line_re, x_sin, precision=precise
    )
    return (full_re, full_im)


def back_first(spec_re, spec_im, x_cos, x_sin):
    wide_re = jnp.einsum("cpi,xi->cxp", spec_re, x_cos, precision=precise) - jnp.einsum(
        "cpi,xi->cxp", spec_im, x_sin, precision=precise
    )
    wide_im = jnp.einsum("cpi,xi->cxp", spec_re, x_sin, precision=precise) + jnp.einsum(
        "cpi,xi->cxp", spec_im, x_cos, precision=precise
    )
    return jnp.stack([wide_re, wide_im])


def plane_inverse(arrived, weight, z_cos, z_sin, y_cos, y_sin):
    chans, planes = (arrived.shape[1], arrived.shape[2])
    shaped = arrived.reshape(2, chans, planes, KY, KZ)
    wide_re, wide_im = (shaped[0], shaped[1])
    plane_re = jnp.einsum("cxjk,yj->cxky", wide_re, y_cos, precision=precise) - jnp.einsum(
        "cxjk,yj->cxky", wide_im, y_sin, precision=precise
    )
    plane_im = jnp.einsum("cxjk,yj->cxky", wide_re, y_sin, precision=precise) + jnp.einsum(
        "cxjk,yj->cxky", wide_im, y_cos, precision=precise
    )
    plane_re = plane_re * weight[:, None]
    plane_im = plane_im * weight[:, None]
    return jnp.einsum("cxky,zk->cxyz", plane_re, z_cos, precision=precise) - jnp.einsum(
        "cxky,zk->cxyz", plane_im, z_sin, precision=precise
    )


def on_device_any(field, cotangent, spec_weight, bypass_weight):
    count = lax.axis_size("slab")
    pairs = KY * KZ // count
    chans = field.shape[1]
    z_cos, z_sin = wave_tables(GZ, KZ, False)
    y_cos, y_sin = wave_tables(GY, KY, True)
    x_cos, x_sin = wave_tables(GX, KX, True)
    kz_index = jnp.arange(KZ, dtype=jnp.int32)
    fold = jnp.where(kz_index == 0, 1.0, 2.0).astype(jnp.float32) / float(GX * GY * GZ)
    ones = jnp.ones((KZ,), jnp.float32)
    weights = spec_weight.reshape(2, chans, pairs, KX, chans)
    w_real = weights[0]
    w_imag = weights[1]
    source = field[0]
    local_spec = plane_spectrum(source, ones, z_cos, z_sin, y_cos, y_sin)
    moved = lax.all_to_all(local_spec, "slab", split_axis=3, concat_axis=2, tiled=True)
    hat_re, hat_im = along_first(moved, x_cos, x_sin)
    mix_re = jnp.einsum("cpi,cpio->opi", hat_re, w_real, precision=precise) - jnp.einsum(
        "cpi,cpio->opi", hat_im, w_imag, precision=precise
    )
    mix_im = jnp.einsum("cpi,cpio->opi", hat_re, w_imag, precision=precise) + jnp.einsum(
        "cpi,cpio->opi", hat_im, w_real, precision=precise
    )
    outgoing = back_first(mix_re, mix_im, x_cos, x_sin)
    arrived = lax.all_to_all(outgoing, "slab", split_axis=2, concat_axis=3, tiled=True)
    spectral = plane_inverse(arrived, fold, z_cos, z_sin, y_cos, y_sin)
    pre = spectral + jnp.einsum("co,cxyz->oxyz", bypass_weight, source, precision=precise)
    result, pullback = jax.vjp(gelu_exact, pre)
    grad_pre = pullback(cotangent[0])[0]
    fold_grid = jnp.broadcast_to(fold, (KY, KZ))
    cot_spec = plane_spectrum(grad_pre, fold_grid, z_cos, z_sin, y_cos, y_sin)
    cot_moved = lax.all_to_all(cot_spec, "slab", split_axis=3, concat_axis=2, tiled=True)
    grad_re, grad_im = along_first(cot_moved, x_cos, x_sin)
    own_real = jnp.einsum("cpi,opi->cpio", hat_re, grad_re, precision=precise) + jnp.einsum(
        "cpi,opi->cpio", hat_im, grad_im, precision=precise
    )
    own_imag = jnp.einsum("cpi,opi->cpio", hat_re, grad_im, precision=precise) - jnp.einsum(
        "cpi,opi->cpio", hat_im, grad_re, precision=precise
    )
    summed = lax.psum(jnp.stack([own_real, own_imag]), "dp")
    grad_spec = summed.reshape(2, chans, pairs, KX * chans)
    input_re = jnp.einsum("opi,cpio->cpi", grad_re, w_real, precision=precise) + jnp.einsum(
        "opi,cpio->cpi", grad_im, w_imag, precision=precise
    )
    input_im = jnp.einsum("opi,cpio->cpi", grad_im, w_real, precision=precise) - jnp.einsum(
        "opi,cpio->cpi", grad_re, w_imag, precision=precise
    )
    grad_out = back_first(input_re, input_im, x_cos, x_sin)
    grad_arrived = lax.all_to_all(grad_out, "slab", split_axis=2, concat_axis=3, tiled=True)
    back_field = plane_inverse(grad_arrived, ones, z_cos, z_sin, y_cos, y_sin)
    back_field = back_field + jnp.einsum(
        "co,oxyz->cxyz", bypass_weight, grad_pre, precision=precise
    )
    return (result[None], back_field[None], grad_spec)


CH = 32
PLANES = 8
PAIRS = 32
PEERS = 16
KYL = PAIRS // KZ
KYH = KY // KYL
QUAD = 4
GROUPS = CH // QUAD
TILE = QUAD * PAIRS
WIDE = QUAD * KYL * 2 * GZ
MODES_O = KX * CH

BF = jnp.bfloat16
F32 = jnp.float32


def split_table(table):
    high = table.astype(ml_dtypes.bfloat16)
    low = (table - high.astype(np.float64)).astype(ml_dtypes.bfloat16)
    return high, low


def phases(length, count, signed):
    freqs = np.arange(count)
    if signed:
        freqs = np.where(freqs < count // 2, freqs, freqs - count)
    phase = (np.arange(length)[:, None] * freqs[None, :]) % length
    angle = phase * (2.0 * np.pi / length)
    return np.cos(angle), np.sin(angle)


@functools.lru_cache(maxsize=None)
def host_tables():
    zc, zs = phases(GZ, KZ, False)
    yc, ys = phases(GY, KY, True)
    xc, xs = phases(GX, KX, True)
    fold = np.where(np.arange(KZ) == 0, 1.0, 2.0) / float(GX * GY * GZ)
    out = {}
    ycr = yc.T.reshape(KYH, KYL, GY).transpose(1, 0, 2)
    ysr = ys.T.reshape(KYH, KYL, GY).transpose(1, 0, 2)
    fwd = np.stack([ycr, -ysr], axis=1).reshape(2 * KY, GY)
    high, low = split_table(fwd)
    out["yf"] = np.block([[high, high], [low, low]])
    inv = np.stack([ycr, -ysr], axis=1).reshape(2 * KY, GY).T
    high, low = split_table(inv)
    out["yi"] = np.concatenate([high, high, low], axis=1)
    core = np.stack([np.stack([zc, -zs]), np.stack([zs, zc])])
    for name, scale in (("zf", np.ones(KZ)), ("zg", fold)):
        table = np.zeros((QUAD, KYL, 2, GZ, 2, QUAD, KYL, KZ))
        for q in range(QUAD):
            for k in range(KYL):
                table[q, k, :, :, :, q, k, :] = (core * scale).transpose(0, 2, 1, 3)
        out[name + "h"], out[name + "l"] = split_table(table.reshape(WIDE, 2 * TILE))
    core = np.stack([np.stack([zc, zs]), np.stack([-zs, zc])])
    for name, scale in (("zi", fold), ("zj", np.ones(KZ))):
        table = np.zeros((2, QUAD, KYL, KZ, QUAD, KYL, 2, GZ))
        for q in range(QUAD):
            for k in range(KYL):
                table[:, q, k, :, q, k, :, :] = (core * scale).transpose(0, 3, 1, 2)
        out[name + "h"], out[name + "l"] = split_table(table.reshape(2 * TILE, WIDE))
    core = np.stack([np.stack([xc, xs]), np.stack([-xs, xc])])
    table = core.reshape(2, 2, PEERS, PLANES, KX).transpose(0, 4, 2, 1, 3).reshape(2 * KX, 2 * GX)
    high, low = split_table(table)
    out["xfh"], out["xfl"] = high, low
    core = np.stack([np.stack([xc, -xs]), np.stack([xs, xc])])
    table = core.reshape(2, 2, PEERS, PLANES, KX).transpose(2, 0, 3, 1, 4).reshape(2 * GX, 2 * KX)
    high, low = split_table(table)
    out["xi"] = np.concatenate([high, high, low], axis=1)
    spread = np.repeat(np.eye(2 * KX), CH, axis=1).astype(ml_dtypes.bfloat16)
    out["spread"] = np.concatenate([spread, spread], axis=0)
    out["gather"] = np.concatenate([spread, spread], axis=0).T.copy()
    return out


def halves(values):
    high = values.astype(BF)
    return high, (values - high.astype(F32)).astype(BF)


def dot(left, right):
    return jnp.dot(left, right, preferred_element_type=F32)


def dot3(high, low, table_high, table_low):
    rows = high.shape[0]
    both = dot(jnp.concatenate([high, low], axis=0), table_high)
    return both[:rows] + both[rows:] + dot(high, table_low)


def lines_to_modes(pair, yf):
    high, low = halves(pair)
    both = dot(yf, jnp.concatenate([high, low], axis=0))
    return halves(both[: 2 * KY] + both[2 * KY :])


def call(body, grid, ins, outs, shapes, scratch, vmem=56):
    return pl.pallas_call(
        body,
        grid=grid,
        in_specs=ins,
        out_specs=outs,
        out_shape=shapes,
        scratch_shapes=scratch,
        compiler_params=pltpu.CompilerParams(
            dimension_semantics=("arbitrary",), vmem_limit_bytes=vmem * 1024 * 1024
        ),
    )


def whole(array):
    zeros = (0,) * array.ndim
    return pl.BlockSpec(array.shape, lambda step: zeros)


def spectrum_body(f_ref, yf_ref, th_ref, tl_ref, out_ref, high_s, low_s):
    yf = yf_ref[...]
    for x in range(PLANES):
        for half in range(2):
            pair = jnp.concatenate([f_ref[2 * half, x], f_ref[2 * half + 1, x]], axis=1)
            high, low = lines_to_modes(pair, yf)
            for j in range(2):
                for part in range(2 * KYL):
                    lanes = ((2 * half + j) * 2 * KYL + part) * GZ
                    rows = slice(part * KYH, (part + 1) * KYH)
                    to = (slice(x * KYH, (x + 1) * KYH), slice(lanes, lanes + GZ))
                    high_s[to] = high[rows, j * GZ : (j + 1) * GZ]
                    low_s[to] = low[rows, j * GZ : (j + 1) * GZ]
    sums = dot3(high_s[...], low_s[...], th_ref[...], tl_ref[...])
    for part in range(2):
        block = sums[:, part * TILE : (part + 1) * TILE].reshape(PLANES, KYH, TILE)
        out_ref[:, part * PLANES : (part + 1) * PLANES, :] = jnp.swapaxes(block, 0, 1)


def spectrum(field, t):
    tables = (t["yf"], t["zfh"], t["zfl"])
    return call(
        spectrum_body,
        (GROUPS,),
        [pl.BlockSpec((QUAD, PLANES, GY, GZ), lambda g: (g, 0, 0, 0))] + [whole(a) for a in tables],
        pl.BlockSpec((PEERS, 2 * PLANES, TILE), lambda g: (0, 0, g)),
        jax.ShapeDtypeStruct((PEERS, 2 * PLANES, CH * PAIRS), F32),
        [pltpu.VMEM((PLANES * KYH, WIDE), BF), pltpu.VMEM((PLANES * KYH, WIDE), BF)],
    )(field, *tables)


def own_mask():
    rows = lax.broadcasted_iota(jnp.int32, (TILE, TILE), 0) % QUAD
    lanes = lax.broadcasted_iota(jnp.int32, (TILE, TILE), 1) // PAIRS
    return rows == lanes


def x_forward(moved, xfh, xfl):
    high, low = halves(moved)
    both = dot(jnp.concatenate([xfh, xfl], axis=0), high)
    return both[: 2 * KX] + both[2 * KX :] + dot(xfh, low)


def x_inverse(spec, xi):
    high, low = halves(spec)
    return dot(xi, jnp.concatenate([high, low, high], axis=0))


def spread_modes(spec, spread):
    turned = jnp.concatenate([spec, spec], axis=0).T
    high, low = halves(turned)
    lanes = lax.broadcasted_iota(jnp.int32, (TILE, 4 * KX), 1)
    return dot(jnp.where(lanes < 2 * KX, high, low), spread)


def mix_body(moved_ref, w_ref, xfh_ref, xfl_ref, spread_ref, xi_ref, hat_ref, out_ref, acc_s, turn_s):
    step = pl.program_id(0)

    @pl.when(step == 0)
    def _():
        acc_s[...] = jnp.zeros_like(acc_s)

    hat = x_forward(moved_ref[...].reshape(2 * GX, TILE), xfh_ref[...], xfl_ref[...])
    hat_ref[...] = hat
    wide = spread_modes(hat, spread_ref[...])
    acc_re, acc_im = acc_s[0], acc_s[1]
    for q in range(QUAD):
        h_re = wide[q * PAIRS : (q + 1) * PAIRS, :MODES_O]
        h_im = wide[q * PAIRS : (q + 1) * PAIRS, MODES_O:]
        w_re, w_im = w_ref[0, q], w_ref[1, q]
        acc_re = acc_re + h_re * w_re - h_im * w_im
        acc_im = acc_im + h_re * w_im + h_im * w_re
    acc_s[0] = acc_re
    acc_s[1] = acc_im

    @pl.when(step == GROUPS - 1)
    def _():
        mask = own_mask()
        for part in range(2):
            full = jnp.concatenate([acc_s[part]] * QUAD, axis=0)
            for k in range(MODES_O // TILE):
                turned = full[:, k * TILE : (k + 1) * TILE].T
                turn_s[pl.ds(part * MODES_O + k * TILE, TILE), :] = jnp.where(mask, turned, 0.0)
        xi = xi_ref[...]
        for g in range(0, GROUPS, 2):
            tiles = []
            for h in range(g, g + 2):
                parts = []
                for part in range(2):
                    total = None
                    for q in range(QUAD):
                        rows = turn_s[pl.ds(part * MODES_O + h * QUAD + q, KX, stride=CH), :]
                        total = rows if total is None else total + rows
                    parts.append(total)
                tiles.append(jnp.concatenate(parts, axis=0))
            wave = x_inverse(jnp.concatenate(tiles, axis=1), xi)
            out_ref[:, :, g * TILE : (g + 2) * TILE] = wave.reshape(PEERS, 2 * PLANES, 2 * TILE)


def mix(moved, weights, t):
    tables = (t["xfh"], t["xfl"], t["spread"], t["xi"])
    return call(
        mix_body,
        (GROUPS,),
        [
            pl.BlockSpec((PEERS, 2 * PLANES, TILE), lambda g: (0, 0, g)),
            pl.BlockSpec((2, QUAD, PAIRS, MODES_O), lambda g: (0, g, 0, 0)),
        ]
        + [whole(a) for a in tables],
        [
            pl.BlockSpec((2 * KX, TILE), lambda g: (0, g)),
            pl.BlockSpec((PEERS, 2 * PLANES, CH * PAIRS), lambda g: (0, 0, 0)),
        ],
        [
            jax.ShapeDtypeStruct((2 * KX, CH * PAIRS), F32),
            jax.ShapeDtypeStruct((PEERS, 2 * PLANES, CH * PAIRS), F32),
        ],
        [pltpu.VMEM((2, PAIRS, MODES_O), F32), pltpu.VMEM((2 * MODES_O, TILE), F32)],
    )(moved, weights, *tables)


def input_body(moved_ref, w_ref, xfh_ref, xfl_ref, gather_ref, xi_ref, g_ref, out_ref, turn_s):
    step = pl.program_id(0)

    @pl.when(step == 0)
    def _():
        lanes = lax.broadcasted_iota(jnp.int32, (KX, TILE), 1) // PAIRS
        for h in range(GROUPS):
            tile = moved_ref[:, :, h * TILE : (h + 1) * TILE].reshape(2 * GX, TILE)
            hat = x_forward(tile, xfh_ref[...], xfl_ref[...])
            for part in range(2):
                rows = hat[part * KX : (part + 1) * KX]
                for q in range(QUAD):
                    to = pl.ds(part * MODES_O + h * QUAD + q, KX, stride=CH)
                    turn_s[to, :] = jnp.where(lanes == q, rows, 0.0)
        for part in range(2):
            for k in range(MODES_O // TILE):
                turned = turn_s[pl.ds(part * MODES_O + k * TILE, TILE), :].T
                total = turned[:PAIRS]
                for q in range(1, QUAD):
                    total = total + turned[q * PAIRS : (q + 1) * PAIRS]
                g_ref[part, :, k * TILE : (k + 1) * TILE] = total

    g_re, g_im = g_ref[0], g_ref[1]
    rows_high, rows_low = [], []
    for q in range(QUAD):
        w_re, w_im = w_ref[0, q], w_ref[1, q]
        full = jnp.concatenate([g_re * w_re + g_im * w_im, g_im * w_re - g_re * w_im], axis=1)
        high, low = halves(full)
        rows_high.append(high)
        rows_low.append(low)
    both = dot(jnp.concatenate(rows_high + rows_low, axis=0), gather_ref[...])
    spec = (both[:TILE] + both[TILE:]).T[: 2 * KX]
    out_ref[...] = x_inverse(spec, xi_ref[...]).reshape(PEERS, 2 * PLANES, TILE)


def input_modes(moved, weights, t):
    tables = (t["xfh"], t["xfl"], t["gather"], t["xi"])
    return call(
        input_body,
        (GROUPS,),
        [
            whole(moved),
            pl.BlockSpec((2, QUAD, PAIRS, MODES_O), lambda g: (0, g, 0, 0)),
        ]
        + [whole(a) for a in tables],
        [
            pl.BlockSpec((2, PAIRS, MODES_O), lambda g: (0, 0, 0)),
            pl.BlockSpec((PEERS, 2 * PLANES, TILE), lambda g: (0, 0, g)),
        ],
        [
            jax.ShapeDtypeStruct((2, PAIRS, MODES_O), F32),
            jax.ShapeDtypeStruct((PEERS, 2 * PLANES, CH * PAIRS), F32),
        ],
        [pltpu.VMEM((2 * MODES_O, TILE), F32)],
    )(moved, weights, *tables)


def weight_grad_body(hat_ref, far_hat_ref, g_ref, far_g_ref, spread_ref, out_ref):
    spread = spread_ref[...]
    near = spread_modes(hat_ref[...], spread)
    far = spread_modes(far_hat_ref[...], spread)
    for q in range(QUAD):
        rows = slice(q * PAIRS, (q + 1) * PAIRS)
        n_re, n_im = near[rows, :MODES_O], near[rows, MODES_O:]
        f_re, f_im = far[rows, :MODES_O], far[rows, MODES_O:]
        out_ref[0, q] = n_re * g_ref[0] + n_im * g_ref[1] + f_re * far_g_ref[0] + f_im * far_g_ref[1]
        out_ref[1, q] = n_re * g_ref[1] - n_im * g_ref[0] + f_re * far_g_ref[1] - f_im * far_g_ref[0]


def weight_grad(hat, far_hat, grad, far_grad, t):
    tile = pl.BlockSpec((2 * KX, TILE), lambda g: (0, g))
    return call(
        weight_grad_body,
        (GROUPS,),
        [tile, tile, whole(grad), whole(far_grad), whole(t["spread"])],
        pl.BlockSpec((2, QUAD, PAIRS, MODES_O), lambda g: (0, g, 0, 0)),
        jax.ShapeDtypeStruct((2, CH, PAIRS, MODES_O), F32),
        [],
    )(hat, far_hat, grad, far_grad, t["spread"])


def gelu_parts(pre):
    bell = jnp.exp(pre * pre * -0.5)
    t = 1.0 / (1.0 + (0.3275911 * math.sqrt(0.5)) * jnp.abs(pre))
    poly = 1.061405429 * 0.5
    for coefficient in (-1.453152027, 1.421413741, -0.284496736, 0.254829592):
        poly = poly * t + coefficient * 0.5
    tail = poly * t * bell
    share = jnp.where(pre >= 0.0, 1.0 - tail, tail)
    return share, pre * bell * (1.0 / math.sqrt(2.0 * math.pi))


def sort_planes(arrived_ref, planes_s):
    for part in range(2):
        block = arrived_ref[:, part * PLANES : (part + 1) * PLANES, :]
        lanes = slice(part * CH * PAIRS, (part + 1) * CH * PAIRS)
        planes_s[:, :, lanes] = jnp.swapaxes(block, 0, 1)


def inverse_plane(x, planes_s, yi, zih, zil, high_s, low_s, spec_s):
    rows = []
    for g in range(GROUPS):
        parts = [planes_s[x, :, (part * GROUPS + g) * TILE : (part * GROUPS + g + 1) * TILE] for part in range(2)]
        rows.append(jnp.concatenate(parts, axis=1))
    high, low = halves(jnp.concatenate(rows, axis=0))
    high, low = halves(dot3(high, low, zih, zil))
    high_s[...] = high
    low_s[...] = low

    def one(g, carry):
        rows = pl.ds(pl.multiple_of(g * KYH, KYH), KYH)
        for half in range(2):
            stacks = []
            for source in (high_s, low_s):
                sides = []
                for j in range(2):
                    lanes = (2 * half + j) * 2 * KYL * GZ
                    sides.append(
                        jnp.concatenate(
                            [source[rows, lanes + k * GZ : lanes + (k + 1) * GZ] for k in range(2 * KYL)], axis=0
                        )
                    )
                stacks.append(jnp.concatenate(sides, axis=1))
            waves = dot(yi, jnp.concatenate([stacks[0], stacks[1], stacks[0]], axis=0))
            for j in range(2):
                spec_s[g * QUAD + 2 * half + j] = waves[:, j * GZ : (j + 1) * GZ]
        return carry

    lax.fori_loop(0, GROUPS, one, 0)


def channel_sum(data_ref, y, kron_ref):
    tiles = [data_ref[:, 0, pl.ds(y + 8 * j, 8), :].reshape(8 * CH, GZ) for j in range(2)]
    high, low = halves(jnp.concatenate(tiles, axis=1))
    both = dot(kron_ref[...], high)
    return both[: 8 * CH] + both[8 * CH :] + dot(kron_ref[: 8 * CH], low)


def middle_body(
    arrived_ref, f_ref, cot_ref, kron_ref, yi_ref, zih_ref, zil_ref, yf_ref, zgh_ref, zgl_ref,
    out_ref, grad_ref, spec_ref, planes_s, high_s, low_s, wave_s, sent_s,
):
    x = pl.program_id(0)

    @pl.when(x == 0)
    def _():
        sort_planes(arrived_ref, planes_s)

    inverse_plane(x, planes_s, yi_ref[...], zih_ref[...], zil_ref[...], high_s, low_s, wave_s)

    def rows(i, carry):
        y = pl.multiple_of(i * 16, 16)
        sums = channel_sum(f_ref, y, kron_ref)
        for j in range(2):
            at = pl.ds(y + 8 * j, 8)
            pre = sums[:, j * GZ : (j + 1) * GZ].reshape(CH, 8, GZ) + wave_s[:, at, :]
            share, slope = gelu_parts(pre)
            out_ref[:, 0, at, :] = pre * share
            grad_ref[:, 0, at, :] = cot_ref[:, 0, at, :] * (share + slope)
        return carry

    lax.fori_loop(0, GY // 16, rows, 0)

    def lines(g, carry):
        at = pl.ds(pl.multiple_of(g * KYH, KYH), KYH)
        for half in range(2):
            c = g * QUAD + 2 * half
            high, low = lines_to_modes(jnp.concatenate([grad_ref[c, 0], grad_ref[c + 1, 0]], axis=1), yf_ref[...])
            for j in range(2):
                for part in range(2 * KYL):
                    lanes = ((2 * half + j) * 2 * KYL + part) * GZ
                    take = slice(part * KYH, (part + 1) * KYH)
                    high_s[at, lanes : lanes + GZ] = high[take, j * GZ : (j + 1) * GZ]
                    low_s[at, lanes : lanes + GZ] = low[take, j * GZ : (j + 1) * GZ]
        return carry

    lax.fori_loop(0, GROUPS, lines, 0)
    sums = dot3(high_s[...], low_s[...], zgh_ref[...], zgl_ref[...])
    for g in range(GROUPS):
        for part in range(2):
            lanes = (part * GROUPS + g) * TILE
            sent_s[x, :, lanes : lanes + TILE] = sums[g * KYH : (g + 1) * KYH, part * TILE : (part + 1) * TILE]

    @pl.when(x == PLANES - 1)
    def _():
        for part in range(2):
            block = sent_s[:, :, part * CH * PAIRS : (part + 1) * CH * PAIRS]
            spec_ref[:, part * PLANES : (part + 1) * PLANES, :] = jnp.swapaxes(block, 0, 1)


def plane_block():
    return pl.BlockSpec((CH, 1, GY, GZ), lambda x: (0, x, 0, 0))


def middle(arrived, field, cotangent, kron, t):
    tables = (kron, t["yi"], t["zih"], t["zil"], t["yf"], t["zgh"], t["zgl"])
    return call(
        middle_body,
        (PLANES,),
        [whole(arrived), plane_block(), plane_block()] + [whole(a) for a in tables],
        [plane_block(), plane_block(), whole(arrived)],
        [
            jax.ShapeDtypeStruct(field.shape, F32),
            jax.ShapeDtypeStruct(field.shape, F32),
            jax.ShapeDtypeStruct(arrived.shape, F32),
        ],
        [
            pltpu.VMEM((PLANES, KYH, 2 * CH * PAIRS), F32),
            pltpu.VMEM((GROUPS * KYH, WIDE), BF),
            pltpu.VMEM((GROUPS * KYH, WIDE), BF),
            pltpu.VMEM((CH, GY, GZ), F32),
            pltpu.VMEM((PLANES, KYH, 2 * CH * PAIRS), F32),
        ],
    )(arrived, field, cotangent, *tables)


def last_body(arrived_ref, grad_ref, kron_ref, yi_ref, zjh_ref, zjl_ref, out_ref, planes_s, high_s, low_s, wave_s):
    x = pl.program_id(0)

    @pl.when(x == 0)
    def _():
        sort_planes(arrived_ref, planes_s)

    inverse_plane(x, planes_s, yi_ref[...], zjh_ref[...], zjl_ref[...], high_s, low_s, wave_s)

    def rows(i, carry):
        y = pl.multiple_of(i * 16, 16)
        sums = channel_sum(grad_ref, y, kron_ref)
        for j in range(2):
            at = pl.ds(y + 8 * j, 8)
            out_ref[:, 0, at, :] = sums[:, j * GZ : (j + 1) * GZ].reshape(CH, 8, GZ) + wave_s[:, at, :]
        return carry

    lax.fori_loop(0, GY // 16, rows, 0)


def last(arrived, grad_pre, kron, t):
    tables = (kron, t["yi"], t["zjh"], t["zjl"])
    return call(
        last_body,
        (PLANES,),
        [whole(arrived), plane_block()] + [whole(a) for a in tables],
        plane_block(),
        jax.ShapeDtypeStruct(grad_pre.shape, F32),
        [
            pltpu.VMEM((PLANES, KYH, 2 * CH * PAIRS), F32),
            pltpu.VMEM((GROUPS * KYH, WIDE), BF),
            pltpu.VMEM((GROUPS * KYH, WIDE), BF),
            pltpu.VMEM((CH, GY, GZ), F32),
        ],
    )(arrived, grad_pre, *tables)


def kron_halves(matrix):
    high = lax.reduce_precision(matrix, 8, 7)
    eye = jnp.eye(8, dtype=F32)
    stacked = jnp.stack([high, matrix - high])
    wide = stacked[:, :, None, :, None] * eye[None, None, :, None, :]
    return wide.reshape(16 * CH, 8 * CH).astype(BF)


def swap_slabs(array):
    return lax.all_to_all(array, "slab", split_axis=0, concat_axis=0, tiled=True)


def on_device(field, cotangent, spec_weight, bypass_weight):
    shape = (field.shape[1], field.shape[2], spec_weight.shape[2], lax.axis_size("slab"), lax.axis_size("dp"))
    if shape != (CH, PLANES, PAIRS, PEERS, 2):
        return on_device_any(field, cotangent, spec_weight, bypass_weight)
    t = {name: jnp.asarray(table) for name, table in host_tables().items()}
    source, other = field[0], cotangent[0]
    moved = swap_slabs(spectrum(source, t))
    kron_out = kron_halves(bypass_weight.T)
    kron_in = kron_halves(bypass_weight)
    hat, outgoing = mix(moved, spec_weight, t)
    swap_pair = [(0, 1), (1, 0)]
    far_hat = lax.ppermute(hat, "dp", swap_pair)
    result, grad_pre, cot_spec = middle(swap_slabs(outgoing), source, other, kron_out, t)
    grad, grad_out = input_modes(swap_slabs(cot_spec), spec_weight, t)
    far_grad = lax.ppermute(grad, "dp", swap_pair)
    grad_arrived = swap_slabs(grad_out)
    grad_spec = weight_grad(hat, far_hat, grad, far_grad, t)
    back_field = last(grad_arrived, grad_pre, kron_in, t)
    return (result[None], back_field[None], grad_spec)


def solution(mesh):
    in_specs = (
        P("dp", None, "slab", None, None),
        P("dp", None, "slab", None, None),
        P(None, None, "slab", None),
        P(),
    )
    out_specs = (
        P("dp", None, "slab", None, None),
        P("dp", None, "slab", None, None),
        P(None, None, "slab", None),
    )
    return jax.shard_map(
        on_device, mesh=mesh, in_specs=in_specs, out_specs=out_specs, check_vma=False
    )
```

```python
import functools
import math

import jax
import jax.numpy as jnp
import ml_dtypes
import numpy as np
from jax import lax
from jax.experimental import pallas as pl
from jax.experimental.pallas import tpu as pltpu
from jax.sharding import PartitionSpec as P

GX = 128
GY = 128
GZ = 128
KX = 32
KY = 32
KZ = 16


precise = lax.Precision.HIGHEST


def wave_tables(length, count, signed):
    positions = jnp.arange(length, dtype=jnp.int32)
    indices = jnp.arange(count, dtype=jnp.int32)
    if signed:
        freqs = jnp.where(indices < count // 2, indices, indices - count)
    else:
        freqs = indices
    phase = positions[:, None] * freqs[None, :] % length
    angle = phase.astype(jnp.float32) * (2.0 * math.pi / length)
    return (jnp.cos(angle), jnp.sin(angle))


def gelu_exact(values):
    return jax.nn.gelu(values, approximate=False)


def plane_spectrum(data, weight, z_cos, z_sin, y_cos, y_sin):
    chans, planes = (data.shape[0], data.shape[1])
    part_re = jnp.einsum("cxyz,zk->cxky", data, z_cos, precision=precise)
    part_im = -jnp.einsum("cxyz,zk->cxky", data, z_sin, precision=precise)
    mid_re = jnp.einsum("cxky,yj->cxjk", part_re, y_cos, precision=precise) + jnp.einsum(
        "cxky,yj->cxjk", part_im, y_sin, precision=precise
    )
    mid_im = jnp.einsum("cxky,yj->cxjk", part_im, y_cos, precision=precise) - jnp.einsum(
        "cxky,yj->cxjk", part_re, y_sin, precision=precise
    )
    stacked = jnp.stack([mid_re * weight, mid_im * weight])
    return stacked.reshape(2, chans, planes, KY * KZ)


def along_first(moved, x_cos, x_sin):
    line_re, line_im = (moved[0], moved[1])
    full_re = jnp.einsum("cxp,xi->cpi", line_re, x_cos, precision=precise) + jnp.einsum(
        "cxp,xi->cpi", line_im, x_sin, precision=precise
    )
    full_im = jnp.einsum("cxp,xi->cpi", line_im, x_cos, precision=precise) - jnp.einsum(
        "cxp,xi->cpi", line_re, x_sin, precision=precise
    )
    return (full_re, full_im)


def back_first(spec_re, spec_im, x_cos, x_sin):
    wide_re = jnp.einsum("cpi,xi->cxp", spec_re, x_cos, precision=precise) - jnp.einsum(
        "cpi,xi->cxp", spec_im, x_sin, precision=precise
    )
    wide_im = jnp.einsum("cpi,xi->cxp", spec_re, x_sin, precision=precise) + jnp.einsum(
        "cpi,xi->cxp", spec_im, x_cos, precision=precise
    )
    return jnp.stack([wide_re, wide_im])


def plane_inverse(arrived, weight, z_cos, z_sin, y_cos, y_sin):
    chans, planes = (arrived.shape[1], arrived.shape[2])
    shaped = arrived.reshape(2, chans, planes, KY, KZ)
    wide_re, wide_im = (shaped[0], shaped[1])
    plane_re = jnp.einsum("cxjk,yj->cxky", wide_re, y_cos, precision=precise) - jnp.einsum(
        "cxjk,yj->cxky", wide_im, y_sin, precision=precise
    )
    plane_im = jnp.einsum("cxjk,yj->cxky", wide_re, y_sin, precision=precise) + jnp.einsum(
        "cxjk,yj->cxky", wide_im, y_cos, precision=precise
    )
    plane_re = plane_re * weight[:, None]
    plane_im = plane_im * weight[:, None]
    return jnp.einsum("cxky,zk->cxyz", plane_re, z_cos, precision=precise) - jnp.einsum(
        "cxky,zk->cxyz", plane_im, z_sin, precision=precise
    )


def on_device_any(field, cotangent, spec_weight, bypass_weight):
    count = lax.axis_size("slab")
    pairs = KY * KZ // count
    chans = field.shape[1]
    z_cos, z_sin = wave_tables(GZ, KZ, False)
    y_cos, y_sin = wave_tables(GY, KY, True)
    x_cos, x_sin = wave_tables(GX, KX, True)
    kz_index = jnp.arange(KZ, dtype=jnp.int32)
    fold = jnp.where(kz_index == 0, 1.0, 2.0).astype(jnp.float32) / float(GX * GY * GZ)
    ones = jnp.ones((KZ,), jnp.float32)
    weights = spec_weight.reshape(2, chans, pairs, KX, chans)
    w_real = weights[0]
    w_imag = weights[1]
    source = field[0]
    local_spec = plane_spectrum(source, ones, z_cos, z_sin, y_cos, y_sin)
    moved = lax.all_to_all(local_spec, "slab", split_axis=3, concat_axis=2, tiled=True)
    hat_re, hat_im = along_first(moved, x_cos, x_sin)
    mix_re = jnp.einsum("cpi,cpio->opi", hat_re, w_real, precision=precise) - jnp.einsum(
        "cpi,cpio->opi", hat_im, w_imag, precision=precise
    )
    mix_im = jnp.einsum("cpi,cpio->opi", hat_re, w_imag, precision=precise) + jnp.einsum(
        "cpi,cpio->opi", hat_im, w_real, precision=precise
    )
    outgoing = back_first(mix_re, mix_im, x_cos, x_sin)
    arrived = lax.all_to_all(outgoing, "slab", split_axis=2, concat_axis=3, tiled=True)
    spectral = plane_inverse(arrived, fold, z_cos, z_sin, y_cos, y_sin)
    pre = spectral + jnp.einsum("co,cxyz->oxyz", bypass_weight, source, precision=precise)
    result, pullback = jax.vjp(gelu_exact, pre)
    grad_pre = pullback(cotangent[0])[0]
    fold_grid = jnp.broadcast_to(fold, (KY, KZ))
    cot_spec = plane_spectrum(grad_pre, fold_grid, z_cos, z_sin, y_cos, y_sin)
    cot_moved = lax.all_to_all(cot_spec, "slab", split_axis=3, concat_axis=2, tiled=True)
    grad_re, grad_im = along_first(cot_moved, x_cos, x_sin)
    own_real = jnp.einsum("cpi,opi->cpio", hat_re, grad_re, precision=precise) + jnp.einsum(
        "cpi,opi->cpio", hat_im, grad_im, precision=precise
    )
    own_imag = jnp.einsum("cpi,opi->cpio", hat_re, grad_im, precision=precise) - jnp.einsum(
        "cpi,opi->cpio", hat_im, grad_re, precision=precise
    )
    summed = lax.psum(jnp.stack([own_real, own_imag]), "dp")
    grad_spec = summed.reshape(2, chans, pairs, KX * chans)
    input_re = jnp.einsum("opi,cpio->cpi", grad_re, w_real, precision=precise) + jnp.einsum(
        "opi,cpio->cpi", grad_im, w_imag, precision=precise
    )
    input_im = jnp.einsum("opi,cpio->cpi", grad_im, w_real, precision=precise) - jnp.einsum(
        "opi,cpio->cpi", grad_re, w_imag, precision=precise
    )
    grad_out = back_first(input_re, input_im, x_cos, x_sin)
    grad_arrived = lax.all_to_all(grad_out, "slab", split_axis=2, concat_axis=3, tiled=True)
    back_field = plane_inverse(grad_arrived, ones, z_cos, z_sin, y_cos, y_sin)
    back_field = back_field + jnp.einsum(
        "co,oxyz->cxyz", bypass_weight, grad_pre, precision=precise
    )
    return (result[None], back_field[None], grad_spec)


CH = 32
PLANES = 8
PAIRS = 32
PEERS = 16
KYL = PAIRS // KZ
KYH = KY // KYL
QUAD = 4
GROUPS = CH // QUAD
TILE = QUAD * PAIRS
BLOCKS = QUAD * KYL
WIDE = BLOCKS * 2 * GZ
ROWS = PLANES * KYH
MODES_O = KX * CH

VMEM = 56 * 1024 * 1024

BF = jnp.bfloat16
F32 = jnp.float32


def split_table(table):
    high = table.astype(ml_dtypes.bfloat16)
    low = (table - high.astype(np.float64)).astype(ml_dtypes.bfloat16)
    return high, low


def phases(length, count, signed):
    freqs = np.arange(count)
    if signed:
        freqs = np.where(freqs < count // 2, freqs, freqs - count)
    phase = (np.arange(length)[:, None] * freqs[None, :]) % length
    angle = phase * (2.0 * np.pi / length)
    return np.cos(angle), np.sin(angle)


@functools.lru_cache(maxsize=None)
def host_tables():
    zc, zs = phases(GZ, KZ, False)
    yc, ys = phases(GY, KY, True)
    xc, xs = phases(GX, KX, True)
    fold = np.where(np.arange(KZ) == 0, 1.0, 2.0) / float(GX * GY * GZ)
    out = {}
    ycr = yc.T.reshape(KYH, KYL, GY).transpose(1, 0, 2)
    ysr = ys.T.reshape(KYH, KYL, GY).transpose(1, 0, 2)
    fwd = np.stack([ycr, -ysr], axis=1).reshape(2 * KY, GY)
    high, low = split_table(fwd)
    out["yf"] = np.block([[high, high], [low, low]])
    inv = np.stack([ycr, -ysr], axis=1).reshape(2 * KY, GY).T
    high, low = split_table(inv)
    out["yi"] = np.concatenate([high, high, low], axis=1)
    core = np.stack([np.stack([zc, -zs]), np.stack([zs, zc])])
    for name, scale in (("zf", np.ones(KZ)), ("zg", fold)):
        table = (core * scale).transpose(0, 2, 1, 3)[:, :, :, None, :]
        table = np.broadcast_to(table, (2, GZ, 2, BLOCKS, KZ))
        high, low = split_table(table.reshape(2 * GZ, 2 * TILE))
        out[name] = np.stack([high, low])
    core = np.stack([np.stack([zc, zs]), np.stack([-zs, zc])])
    for name, scale in (("zi", fold), ("zj", np.ones(KZ))):
        table = np.zeros((2, QUAD, KYL, KZ, QUAD, KYL, 2, GZ))
        for q in range(QUAD):
            for k in range(KYL):
                table[:, q, k, :, q, k, :, :] = (core * scale).transpose(0, 3, 1, 2)
        out[name + "h"], out[name + "l"] = split_table(table.reshape(2 * TILE, WIDE))
    core = np.stack([np.stack([xc, xs]), np.stack([-xs, xc])])
    table = core.reshape(2, 2, PEERS, PLANES, KX).transpose(0, 4, 2, 1, 3).reshape(2 * KX, 2 * GX)
    high, low = split_table(table)
    out["xfh"], out["xfl"] = high, low
    core = np.stack([np.stack([xc, -xs]), np.stack([xs, xc])])
    table = core.reshape(2, 2, PEERS, PLANES, KX).transpose(2, 0, 3, 1, 4).reshape(2 * GX, 2 * KX)
    high, low = split_table(table)
    out["xi"] = np.concatenate([high, high, low], axis=1)
    spread = np.repeat(np.eye(2 * KX), CH, axis=1).astype(ml_dtypes.bfloat16)
    out["spread"] = np.concatenate([spread, spread], axis=0)
    out["rep"] = np.repeat(np.eye(CH), 8, axis=0).astype(ml_dtypes.bfloat16)
    out["gather"] = np.concatenate([spread, spread], axis=0).T.copy()
    return out


def halves(values):
    high = values.astype(BF)
    return high, (values - high.astype(F32)).astype(BF)


def dot(left, right):
    return jnp.dot(left, right, preferred_element_type=F32)


def dot3(high, low, table_high, table_low):
    rows = high.shape[0]
    both = dot(jnp.concatenate([high, low], axis=0), table_high)
    return both[:rows] + both[rows:] + dot(high, table_low)


def lines_to_modes(pair, yf):
    high, low = halves(pair)
    both = dot(yf, jnp.concatenate([high, low], axis=0))
    return halves(both[: 2 * KY] + both[2 * KY :])


def call(body, us, grid, ins, outs, shapes, scratch, aliases=None):
    return pl.pallas_call(
        body,
        grid=grid,
        in_specs=ins,
        out_specs=outs,
        out_shape=shapes,
        scratch_shapes=scratch,
        input_output_aliases=aliases or {},
        cost_estimate=pl.CostEstimate(flops=int(us * 1e9), bytes_accessed=int(us * 3e6), transcendentals=0),
        compiler_params=pltpu.CompilerParams(
            dimension_semantics=("arbitrary",), vmem_limit_bytes=VMEM
        ),
    )


def whole(array):
    zeros = (0,) * array.ndim
    return pl.BlockSpec(array.shape, lambda step: zeros)


def store_modes(high, low, x, half, high_s, low_s):
    for j in range(2):
        for k in range(KYL):
            to = ((2 * half + j) * KYL + k) * ROWS + x * KYH
            for part in range(2):
                rows = slice((2 * k + part) * KYH, (2 * k + part + 1) * KYH)
                take = (rows, slice(j * GZ, (j + 1) * GZ))
                put = (slice(to, to + KYH), slice(part * GZ, (part + 1) * GZ))
                high_s[put] = high[take]
                low_s[put] = low[take]


def send_modes(high_s, low_s, table_ref, out_ref):
    full = dot3(high_s[...], low_s[...], table_ref[0], table_ref[1])
    owner = lax.broadcasted_iota(jnp.int32, (ROWS, 2 * TILE), 1) % TILE // KZ
    sums = full[:ROWS]
    for i in range(1, BLOCKS):
        sums = jnp.where(owner == i, full[i * ROWS : (i + 1) * ROWS], sums)
    for part in range(2):
        block = sums[:, part * TILE : (part + 1) * TILE].reshape(PLANES, KYH, TILE)
        out_ref[:, part * PLANES : (part + 1) * PLANES, :] = jnp.swapaxes(block, 0, 1)


def spectrum_body(f_ref, yf_ref, table_ref, out_ref, high_s, low_s):
    yf = yf_ref[...]
    for x in range(PLANES):
        for half in range(2):
            pair = jnp.concatenate([f_ref[2 * half, x], f_ref[2 * half + 1, x]], axis=1)
            high, low = lines_to_modes(pair, yf)
            store_modes(high, low, x, half, high_s, low_s)
    send_modes(high_s, low_s, table_ref, out_ref)


def channel_block(first):
    return pl.BlockSpec((QUAD, PLANES, GY, GZ), lambda g: (g + first, 0, 0, 0))


def moved_block():
    return pl.BlockSpec((PEERS, 2 * PLANES, TILE), lambda g: (0, 0, g))


def moved_shape(groups):
    return jax.ShapeDtypeStruct((PEERS, 2 * PLANES, groups * TILE), F32)


def mode_scratch():
    return [pltpu.VMEM((BLOCKS * ROWS, 2 * GZ), BF), pltpu.VMEM((BLOCKS * ROWS, 2 * GZ), BF)]


def spectrum(field, first, count, t):
    tables = (t["yf"], t["zf"])
    return call(
        spectrum_body,
        2 * count,
        (count,),
        [channel_block(first)] + [whole(a) for a in tables],
        moved_block(),
        moved_shape(count),
        mode_scratch(),
    )(field, *tables)


def own_mask():
    rows = lax.broadcasted_iota(jnp.int32, (TILE, TILE), 0) % QUAD
    lanes = lax.broadcasted_iota(jnp.int32, (TILE, TILE), 1) // PAIRS
    return rows == lanes


def x_forward(moved, xfh, xfl):
    high, low = halves(moved)
    both = dot(jnp.concatenate([xfh, xfl], axis=0), high)
    return both[: 2 * KX] + both[2 * KX :] + dot(xfh, low)


def x_inverse(spec, xi):
    high, low = halves(spec)
    return dot(xi, jnp.concatenate([high, low, high], axis=0))


def spread_modes(spec, spread):
    turned = jnp.concatenate([spec, spec], axis=0).T
    high, low = halves(turned)
    lanes = lax.broadcasted_iota(jnp.int32, (TILE, 4 * KX), 1)
    return dot(jnp.where(lanes < 2 * KX, high, low), spread)


def mix_body(first, last, count, *refs):
    moved_ref, w_ref, xfh_ref, xfl_ref, spread_ref, xi_ref = refs[:6]
    refs = refs[6:]
    if not first:
        start_ref, refs = refs[0], refs[1:]
    hat_ref, refs = refs[0], refs[1:]
    if last:
        out_refs, (acc_s, turn_s) = refs[:-2], refs[-2:]
    else:
        (acc_s,) = refs
    step = pl.program_id(0)

    @pl.when(step == 0)
    def _():
        acc_s[...] = jnp.zeros_like(acc_s) if first else start_ref[...]

    hat = x_forward(moved_ref[...].reshape(2 * GX, TILE), xfh_ref[...], xfl_ref[...])
    hat_ref[...] = hat
    wide = spread_modes(hat, spread_ref[...])
    acc_re, acc_im = acc_s[0], acc_s[1]
    for q in range(QUAD):
        h_re = wide[q * PAIRS : (q + 1) * PAIRS, :MODES_O]
        h_im = wide[q * PAIRS : (q + 1) * PAIRS, MODES_O:]
        w_re, w_im = w_ref[0, q], w_ref[1, q]
        acc_re = acc_re + (h_re * w_re - h_im * w_im)
        acc_im = acc_im + (h_re * w_im + h_im * w_re)
    acc_s[0] = acc_re
    acc_s[1] = acc_im

    if last:

        @pl.when(step == count - 1)
        def _():
            mask = own_mask()
            for part in range(2):
                full = jnp.concatenate([acc_s[part]] * QUAD, axis=0)
                for k in range(MODES_O // TILE):
                    turned = full[:, k * TILE : (k + 1) * TILE].T
                    turn_s[pl.ds(part * MODES_O + k * TILE, TILE), :] = jnp.where(mask, turned, 0.0)
            xi = xi_ref[...]
            per = GROUPS // len(out_refs)
            for g in range(0, GROUPS, 2):
                tiles = []
                for h in range(g, g + 2):
                    parts = []
                    for part in range(2):
                        total = None
                        for q in range(QUAD):
                            rows = turn_s[pl.ds(part * MODES_O + h * QUAD + q, KX, stride=CH), :]
                            total = rows if total is None else total + rows
                        parts.append(total)
                    tiles.append(jnp.concatenate(parts, axis=0))
                wave = x_inverse(jnp.concatenate(tiles, axis=1), xi).reshape(PEERS, 2 * PLANES, 2 * TILE)
                for h in range(g, g + 2):
                    to = (h % per) * TILE
                    out_refs[h // per][:, :, to : to + TILE] = wave[:, :, (h - g) * TILE : (h - g + 1) * TILE]


def mix(moved, weights, start, at, count, chunks, t):
    first, last = start is None, at + count == GROUPS
    tables = (t["xfh"], t["xfl"], t["spread"], t["xi"])
    operands = (moved, weights) + tables + (() if first else (start,))
    acc = jax.ShapeDtypeStruct((2, PAIRS, MODES_O), F32)
    outs = [moved_shape(n) for n in chunks] if last else [acc]
    scratch = [pltpu.VMEM(acc.shape, F32), pltpu.VMEM((2 * MODES_O, TILE), F32)] if last else []
    return call(
        functools.partial(mix_body, first, last, count),
        6,
        (count,),
        [moved_block(), pl.BlockSpec((2, QUAD, PAIRS, MODES_O), lambda g: (0, g + at, 0, 0))]
        + [whole(a) for a in operands[2:]],
        [pl.BlockSpec((2 * KX, TILE), lambda g: (0, g))] + [whole(a) for a in outs],
        [jax.ShapeDtypeStruct((2 * KX, count * TILE), F32)] + outs,
        scratch,
    )(*operands)


def input_body(first, moved_refs, g_ref, w_ref, xfh_ref, xfl_ref, gather_ref, xi_ref, out_ref, turn_s):
    if first:

        @pl.when(pl.program_id(0) == 0)
        def _():
            lanes = lax.broadcasted_iota(jnp.int32, (KX, TILE), 1) // PAIRS
            per = GROUPS // len(moved_refs)
            for h in range(GROUPS):
                at = (h % per) * TILE
                tile = moved_refs[h // per][:, :, at : at + TILE].reshape(2 * GX, TILE)
                hat = x_forward(tile, xfh_ref[...], xfl_ref[...])
                for part in range(2):
                    rows = hat[part * KX : (part + 1) * KX]
                    for q in range(QUAD):
                        to = pl.ds(part * MODES_O + h * QUAD + q, KX, stride=CH)
                        turn_s[to, :] = jnp.where(lanes == q, rows, 0.0)
            for part in range(2):
                for k in range(MODES_O // TILE):
                    turned = turn_s[pl.ds(part * MODES_O + k * TILE, TILE), :].T
                    total = turned[:PAIRS]
                    for q in range(1, QUAD):
                        total = total + turned[q * PAIRS : (q + 1) * PAIRS]
                    g_ref[part, :, k * TILE : (k + 1) * TILE] = total

    g_re, g_im = g_ref[0], g_ref[1]
    rows_high, rows_low = [], []
    for q in range(QUAD):
        w_re, w_im = w_ref[0, q], w_ref[1, q]
        full = jnp.concatenate([g_re * w_re + g_im * w_im, g_im * w_re - g_re * w_im], axis=1)
        high, low = halves(full)
        rows_high.append(high)
        rows_low.append(low)
    both = dot(jnp.concatenate(rows_high + rows_low, axis=0), gather_ref[...])
    spec = (both[:TILE] + both[TILE:]).T[: 2 * KX]
    out_ref[...] = x_inverse(spec, xi_ref[...]).reshape(PEERS, 2 * PLANES, TILE)


def input_modes(moved, grad, weights, at, count, t):
    tables = (t["xfh"], t["xfl"], t["gather"], t["xi"])
    shape = jax.ShapeDtypeStruct((2, PAIRS, MODES_O), F32)
    weight_spec = pl.BlockSpec((2, QUAD, PAIRS, MODES_O), lambda g: (0, g + at, 0, 0))
    first = grad is None
    if first:

        def body(*refs):
            n = len(moved)
            w, xfh, xfl, gather, xi, g, out, turn = refs[n:]
            input_body(True, refs[:n], g, w, xfh, xfl, gather, xi, out, turn)

        return call(
            body,
            7,
            (count,),
            [whole(a) for a in moved] + [weight_spec] + [whole(a) for a in tables],
            [whole(shape), moved_block()],
            [shape, moved_shape(count)],
            [pltpu.VMEM((2 * MODES_O, TILE), F32)],
        )(*moved, weights, *tables)

    def body(g, w, xfh, xfl, gather, xi, out):
        input_body(False, None, g, w, xfh, xfl, gather, xi, out, None)

    out = call(
        body,
        6,
        (count,),
        [whole(shape), weight_spec] + [whole(a) for a in tables],
        moved_block(),
        moved_shape(count),
        [],
    )(grad, weights, *tables)
    return grad, out


def weight_grad_body(hat_ref, far_hat_ref, g_ref, far_g_ref, spread_ref, out_ref):
    spread = spread_ref[...]
    near = spread_modes(hat_ref[...], spread)
    far = spread_modes(far_hat_ref[...], spread)
    for q in range(QUAD):
        rows = slice(q * PAIRS, (q + 1) * PAIRS)
        n_re, n_im = near[rows, :MODES_O], near[rows, MODES_O:]
        f_re, f_im = far[rows, :MODES_O], far[rows, MODES_O:]
        out_ref[0, q] = n_re * g_ref[0] + n_im * g_ref[1] + f_re * far_g_ref[0] + f_im * far_g_ref[1]
        out_ref[1, q] = n_re * g_ref[1] - n_im * g_ref[0] + f_re * far_g_ref[1] - f_im * far_g_ref[0]


def weight_grad(hat, far_hat, grad, far_grad, t):
    tile = pl.BlockSpec((2 * KX, TILE), lambda g: (0, g))
    return call(
        weight_grad_body,
        8,
        (GROUPS,),
        [tile, tile, whole(grad), whole(far_grad), whole(t["spread"])],
        pl.BlockSpec((2, QUAD, PAIRS, MODES_O), lambda g: (0, g, 0, 0)),
        jax.ShapeDtypeStruct((2, CH, PAIRS, MODES_O), F32),
        [],
    )(hat, far_hat, grad, far_grad, t["spread"])


def gelu_parts(pre):
    bell = jnp.exp(pre * pre * -0.5)
    t = 1.0 / (1.0 + (0.3275911 * math.sqrt(0.5)) * jnp.abs(pre))
    poly = 1.061405429 * 0.5
    for coefficient in (-1.453152027, 1.421413741, -0.284496736, 0.254829592):
        poly = poly * t + coefficient * 0.5
    tail = poly * t * bell
    share = jnp.where(pre >= 0.0, 1.0 - tail, tail)
    return share, pre * bell * (1.0 / math.sqrt(2.0 * math.pi))


def arrive(arrived_ref, zih, zil):
    parts = []
    for part in range(2):
        block = arrived_ref[:, part * PLANES : (part + 1) * PLANES, :]
        parts.append(jnp.swapaxes(block, 0, 1).reshape(PLANES * KYH, TILE))
    high, low = halves(jnp.concatenate(parts, axis=1))
    return halves(dot3(high, low, zih, zil))


def inverse_pair(high, low, x, half, yi):
    stacks = []
    for source in (high, low):
        sides = []
        for j in range(2):
            lanes = (2 * half + j) * 2 * KYL * GZ
            pieces = [
                source[x * KYH : (x + 1) * KYH, lanes + k * GZ : lanes + (k + 1) * GZ] for k in range(2 * KYL)
            ]
            sides.append(jnp.concatenate(pieces, axis=0))
        stacks.append(jnp.concatenate(sides, axis=1))
    return dot(yi, jnp.concatenate([stacks[0], stacks[1], stacks[0]], axis=0))


def kron_halves(matrix, rep):
    rows = lax.broadcasted_iota(jnp.int32, (8 * CH, 8 * CH), 0) % 8
    lanes = lax.broadcasted_iota(jnp.int32, (8 * CH, 8 * CH), 1) % 8
    wide = []
    for half in halves(matrix):
        tall = dot(rep, half).astype(BF)
        full = lax.dot_general(tall, rep, (((1,), (1,)), ((), ())), preferred_element_type=F32)
        wide.append(jnp.where(rows == lanes, full, 0.0).astype(BF))
    return jnp.concatenate(wide, axis=0)


def channel_sum_body(data_ref, matrix_ref, rep_ref, *refs):
    out_ref, kron_s = refs[-2:]

    @pl.when(pl.program_id(0) == 0)
    def _():
        kron_s[...] = kron_halves(matrix_ref[...], rep_ref[...])

    for x in range(data_ref.shape[1]):
        for i in range(GY // 16):
            tiles = [data_ref[:, x, i * 16 + 8 * j : i * 16 + 8 * j + 8, :].reshape(8 * CH, GZ) for j in range(2)]
            high, low = halves(jnp.concatenate(tiles, axis=1))
            both = dot(kron_s[...], high)
            sums = both[: 8 * CH] + both[8 * CH :] + dot(kron_s[: 8 * CH], low)
            for j in range(2):
                at = slice(i * 16 + 8 * j, i * 16 + 8 * j + 8)
                out_ref[:, x, at, :] = sums[:, j * GZ : (j + 1) * GZ].reshape(CH, 8, GZ)


def channel_sum(data, matrix, first, count, step, so_far, t):
    block = pl.BlockSpec((CH, step, GY, GZ), lambda x: (0, x + first // step, 0, 0))
    return call(
        channel_sum_body,
        2 * count,
        (count // step,),
        [block, whole(matrix), whole(t["rep"])] + [pl.BlockSpec(memory_space=pl.ANY)] * len(so_far),
        block,
        jax.ShapeDtypeStruct(data.shape, F32),
        [pltpu.VMEM((16 * CH, 8 * CH), BF)],
        aliases={3 + i: i for i in range(len(so_far))},
    )(data, matrix, t["rep"], *so_far)


def middle_body(
    arrived_ref, sum_ref, cot_ref, yi_ref, zih_ref, zil_ref, yf_ref, zg_ref, *refs
):
    out_ref, grad_ref, spec_ref, high_s, low_s = refs[-5:]
    high, low = arrive(arrived_ref, zih_ref[...], zil_ref[...])
    yi, yf = yi_ref[...], yf_ref[...]
    for x in range(PLANES):
        for half in range(2):
            waves = inverse_pair(high, low, x, half, yi)
            grads = []
            for j in range(2):
                c = 2 * half + j
                pre = waves[:, j * GZ : (j + 1) * GZ] + sum_ref[c, x]
                share, slope = gelu_parts(pre)
                out_ref[c, x] = pre * share
                grad = cot_ref[c, x] * (share + slope)
                grad_ref[c, x] = grad
                grads.append(grad)
            store_modes(*lines_to_modes(jnp.concatenate(grads, axis=1), yf), x, half, high_s, low_s)
    send_modes(high_s, low_s, zg_ref, spec_ref)


def middle(arrived, sums, cotangent, first, count, so_far, t):
    tables = (t["yi"], t["zih"], t["zil"], t["yf"], t["zg"])
    block = channel_block(first)
    shape = jax.ShapeDtypeStruct(sums.shape, F32)
    n = 3 + len(tables)
    return call(
        middle_body,
        5 * count,
        (count,),
        [moved_block(), block, block] + [whole(a) for a in tables] + [pl.BlockSpec(memory_space=pl.ANY)] * len(so_far),
        [block, block, moved_block()],
        [shape, shape, moved_shape(count)],
        mode_scratch(),
        aliases={n + i: i for i in range(len(so_far))},
    )(arrived, sums, cotangent, *tables, *so_far)


def last_body(arrived_ref, sum_ref, yi_ref, zjh_ref, zjl_ref, *refs):
    out_ref = refs[-1]
    high, low = arrive(arrived_ref, zjh_ref[...], zjl_ref[...])
    yi = yi_ref[...]
    for x in range(PLANES):
        for half in range(2):
            waves = inverse_pair(high, low, x, half, yi)
            for j in range(2):
                c = 2 * half + j
                out_ref[c, x] = waves[:, j * GZ : (j + 1) * GZ] + sum_ref[c, x]


def last(arrived, sums, first, count, so_far, t):
    tables = (t["yi"], t["zjh"], t["zjl"])
    block = channel_block(first)
    n = 2 + len(tables)
    return call(
        last_body,
        2.5 * count,
        (count,),
        [moved_block(), block] + [whole(a) for a in tables] + [pl.BlockSpec(memory_space=pl.ANY)] * len(so_far),
        block,
        jax.ShapeDtypeStruct(sums.shape, F32),
        [],
        aliases={n + i: i for i in range(len(so_far))},
    )(arrived, sums, *tables, *so_far)


def swap_slabs(array):
    return lax.all_to_all(array, "slab", split_axis=0, concat_axis=0, tiled=True)


CHUNKS = (4, 4)
STARTS = tuple(sum(CHUNKS[:k]) for k in range(len(CHUNKS)))


def on_device(field, cotangent, spec_weight, bypass_weight):
    shape = (field.shape[1], field.shape[2], spec_weight.shape[2], lax.axis_size("slab"), lax.axis_size("dp"))
    if shape != (CH, PLANES, PAIRS, PEERS, 2):
        return on_device_any(field, cotangent, spec_weight, bypass_weight)
    t = {name: jnp.asarray(table) for name, table in host_tables().items()}
    source, other = field[0], cotangent[0]
    swap_pair = [(0, 1), (1, 0)]
    parts = list(zip(STARTS, CHUNKS))
    ahead = lax.optimization_barrier

    moved = []
    for at, n in parts:
        sent = spectrum(source, at, n, t)
        if moved:
            moved[-1], sent = ahead((moved[-1], sent))
        moved.append(swap_slabs(sent))
    turned = bypass_weight.T
    sums = channel_sum(source, turned, 0, PLANES // 2, 1, (), t)
    moved[-1], sums = ahead((moved[-1], sums))
    hats, state = [], None
    for arrived, (at, n) in zip(moved, parts):
        hat, *state = mix(arrived, spec_weight, state[0] if state else None, at, n, CHUNKS, t)
        hats.append(hat)
    sums = channel_sum(source, turned, PLANES // 2, PLANES // 2, 1, (sums,), t)
    so_far, cot_moved, arrived = (), [], []
    for sent in state:
        if arrived:
            arrived[-1], sums, sent = ahead((arrived[-1], sums, sent))
        arrived.append(swap_slabs(sent))
    for k, (at, n) in enumerate(parts):
        *so_far, sent = middle(arrived[k], sums, other, at, n, so_far, t)
        if k == 0:
            arrived[-1], sent = ahead((arrived[-1], sent))
        else:
            cot_moved[-1], sent = ahead((cot_moved[-1], sent))
        cot_moved.append(swap_slabs(sent))
    result, grad_pre = so_far
    back_sums = channel_sum(grad_pre, bypass_weight, 0, PLANES, 2, (), t)
    hat = jnp.concatenate(hats, axis=1)
    far_hat = lax.ppermute(hat, "dp", swap_pair)
    cot_moved[-1], back_sums, far_hat = ahead((cot_moved[-1], back_sums, far_hat))
    grad, back_arrived = None, []
    for at, n in parts:
        grad, sent = input_modes(cot_moved, grad, spec_weight, at, n, t)
        if back_arrived:
            far_grad = lax.ppermute(grad, "dp", swap_pair)
            grad_spec = weight_grad(hat, far_hat, grad, far_grad, t)
            back_arrived[-1], sent, grad_spec = ahead((back_arrived[-1], sent, grad_spec))
        back_arrived.append(swap_slabs(sent))
    back = ()
    for k, (at, n) in enumerate(parts):
        back = (last(back_arrived[k], back_sums, at, n, back, t),)
    return (result[None], back[0][None], grad_spec)


def solution(mesh):
    in_specs = (
        P("dp", None, "slab", None, None),
        P("dp", None, "slab", None, None),
        P(None, None, "slab", None),
        P(),
    )
    out_specs = (
        P("dp", None, "slab", None, None),
        P("dp", None, "slab", None, None),
        P(None, None, "slab", None),
    )
    return jax.shard_map(
        on_device, mesh=mesh, in_specs=in_specs, out_specs=out_specs, check_vma=False
    )
```

```python
import functools
import math

import jax
import jax.numpy as jnp
import ml_dtypes
import numpy as np
from jax import lax
from jax.experimental import pallas as pl
from jax.experimental.pallas import tpu as pltpu
from jax.sharding import PartitionSpec as P

GX = 128
GY = 128
GZ = 128
KX = 32
KY = 32
KZ = 16


precise = lax.Precision.HIGHEST


def wave_tables(length, count, signed):
    positions = jnp.arange(length, dtype=jnp.int32)
    indices = jnp.arange(count, dtype=jnp.int32)
    if signed:
        freqs = jnp.where(indices < count // 2, indices, indices - count)
    else:
        freqs = indices
    phase = positions[:, None] * freqs[None, :] % length
    angle = phase.astype(jnp.float32) * (2.0 * math.pi / length)
    return (jnp.cos(angle), jnp.sin(angle))


def gelu_exact(values):
    return jax.nn.gelu(values, approximate=False)


def plane_spectrum(data, weight, z_cos, z_sin, y_cos, y_sin):
    chans, planes = (data.shape[0], data.shape[1])
    part_re = jnp.einsum("cxyz,zk->cxky", data, z_cos, precision=precise)
    part_im = -jnp.einsum("cxyz,zk->cxky", data, z_sin, precision=precise)
    mid_re = jnp.einsum("cxky,yj->cxjk", part_re, y_cos, precision=precise) + jnp.einsum(
        "cxky,yj->cxjk", part_im, y_sin, precision=precise
    )
    mid_im = jnp.einsum("cxky,yj->cxjk", part_im, y_cos, precision=precise) - jnp.einsum(
        "cxky,yj->cxjk", part_re, y_sin, precision=precise
    )
    stacked = jnp.stack([mid_re * weight, mid_im * weight])
    return stacked.reshape(2, chans, planes, KY * KZ)


def along_first(moved, x_cos, x_sin):
    line_re, line_im = (moved[0], moved[1])
    full_re = jnp.einsum("cxp,xi->cpi", line_re, x_cos, precision=precise) + jnp.einsum(
        "cxp,xi->cpi", line_im, x_sin, precision=precise
    )
    full_im = jnp.einsum("cxp,xi->cpi", line_im, x_cos, precision=precise) - jnp.einsum(
        "cxp,xi->cpi", line_re, x_sin, precision=precise
    )
    return (full_re, full_im)


def back_first(spec_re, spec_im, x_cos, x_sin):
    wide_re = jnp.einsum("cpi,xi->cxp", spec_re, x_cos, precision=precise) - jnp.einsum(
        "cpi,xi->cxp", spec_im, x_sin, precision=precise
    )
    wide_im = jnp.einsum("cpi,xi->cxp", spec_re, x_sin, precision=precise) + jnp.einsum(
        "cpi,xi->cxp", spec_im, x_cos, precision=precise
    )
    return jnp.stack([wide_re, wide_im])


def plane_inverse(arrived, weight, z_cos, z_sin, y_cos, y_sin):
    chans, planes = (arrived.shape[1], arrived.shape[2])
    shaped = arrived.reshape(2, chans, planes, KY, KZ)
    wide_re, wide_im = (shaped[0], shaped[1])
    plane_re = jnp.einsum("cxjk,yj->cxky", wide_re, y_cos, precision=precise) - jnp.einsum(
        "cxjk,yj->cxky", wide_im, y_sin, precision=precise
    )
    plane_im = jnp.einsum("cxjk,yj->cxky", wide_re, y_sin, precision=precise) + jnp.einsum(
        "cxjk,yj->cxky", wide_im, y_cos, precision=precise
    )
    plane_re = plane_re * weight[:, None]
    plane_im = plane_im * weight[:, None]
    return jnp.einsum("cxky,zk->cxyz", plane_re, z_cos, precision=precise) - jnp.einsum(
        "cxky,zk->cxyz", plane_im, z_sin, precision=precise
    )


def on_device_any(field, cotangent, spec_weight, bypass_weight):
    count = lax.axis_size("slab")
    pairs = KY * KZ // count
    chans = field.shape[1]
    z_cos, z_sin = wave_tables(GZ, KZ, False)
    y_cos, y_sin = wave_tables(GY, KY, True)
    x_cos, x_sin = wave_tables(GX, KX, True)
    kz_index = jnp.arange(KZ, dtype=jnp.int32)
    fold = jnp.where(kz_index == 0, 1.0, 2.0).astype(jnp.float32) / float(GX * GY * GZ)
    ones = jnp.ones((KZ,), jnp.float32)
    weights = spec_weight.reshape(2, chans, pairs, KX, chans)
    w_real = weights[0]
    w_imag = weights[1]
    source = field[0]
    local_spec = plane_spectrum(source, ones, z_cos, z_sin, y_cos, y_sin)
    moved = lax.all_to_all(local_spec, "slab", split_axis=3, concat_axis=2, tiled=True)
    hat_re, hat_im = along_first(moved, x_cos, x_sin)
    mix_re = jnp.einsum("cpi,cpio->opi", hat_re, w_real, precision=precise) - jnp.einsum(
        "cpi,cpio->opi", hat_im, w_imag, precision=precise
    )
    mix_im = jnp.einsum("cpi,cpio->opi", hat_re, w_imag, precision=precise) + jnp.einsum(
        "cpi,cpio->opi", hat_im, w_real, precision=precise
    )
    outgoing = back_first(mix_re, mix_im, x_cos, x_sin)
    arrived = lax.all_to_all(outgoing, "slab", split_axis=2, concat_axis=3, tiled=True)
    spectral = plane_inverse(arrived, fold, z_cos, z_sin, y_cos, y_sin)
    pre = spectral + jnp.einsum("co,cxyz->oxyz", bypass_weight, source, precision=precise)
    result, pullback = jax.vjp(gelu_exact, pre)
    grad_pre = pullback(cotangent[0])[0]
    fold_grid = jnp.broadcast_to(fold, (KY, KZ))
    cot_spec = plane_spectrum(grad_pre, fold_grid, z_cos, z_sin, y_cos, y_sin)
    cot_moved = lax.all_to_all(cot_spec, "slab", split_axis=3, concat_axis=2, tiled=True)
    grad_re, grad_im = along_first(cot_moved, x_cos, x_sin)
    own_real = jnp.einsum("cpi,opi->cpio", hat_re, grad_re, precision=precise) + jnp.einsum(
        "cpi,opi->cpio", hat_im, grad_im, precision=precise
    )
    own_imag = jnp.einsum("cpi,opi->cpio", hat_re, grad_im, precision=precise) - jnp.einsum(
        "cpi,opi->cpio", hat_im, grad_re, precision=precise
    )
    summed = lax.psum(jnp.stack([own_real, own_imag]), "dp")
    grad_spec = summed.reshape(2, chans, pairs, KX * chans)
    input_re = jnp.einsum("opi,cpio->cpi", grad_re, w_real, precision=precise) + jnp.einsum(
        "opi,cpio->cpi", grad_im, w_imag, precision=precise
    )
    input_im = jnp.einsum("opi,cpio->cpi", grad_im, w_real, precision=precise) - jnp.einsum(
        "opi,cpio->cpi", grad_re, w_imag, precision=precise
    )
    grad_out = back_first(input_re, input_im, x_cos, x_sin)
    grad_arrived = lax.all_to_all(grad_out, "slab", split_axis=2, concat_axis=3, tiled=True)
    back_field = plane_inverse(grad_arrived, ones, z_cos, z_sin, y_cos, y_sin)
    back_field = back_field + jnp.einsum(
        "co,oxyz->cxyz", bypass_weight, grad_pre, precision=precise
    )
    return (result[None], back_field[None], grad_spec)


CH = 32
PLANES = 8
PAIRS = 32
PEERS = 16
KYL = PAIRS // KZ
KYH = KY // KYL
QUAD = 4
GROUPS = CH // QUAD
TILE = QUAD * PAIRS
PER = 2
BLOCKS = QUAD * KYL
WIDE = BLOCKS * 2 * GZ
ROWS = PLANES * KYH
MODES_O = KX * CH

VMEM = 52 * 1024 * 1024

BF = jnp.bfloat16
F32 = jnp.float32


def split_table(table):
    high = table.astype(ml_dtypes.bfloat16)
    low = (table - high.astype(np.float64)).astype(ml_dtypes.bfloat16)
    return high, low


def phases(length, count, signed):
    freqs = np.arange(count)
    if signed:
        freqs = np.where(freqs < count // 2, freqs, freqs - count)
    phase = (np.arange(length)[:, None] * freqs[None, :]) % length
    angle = phase * (2.0 * np.pi / length)
    return np.cos(angle), np.sin(angle)


@functools.lru_cache(maxsize=None)
def host_tables():
    zc, zs = phases(GZ, KZ, False)
    yc, ys = phases(GY, KY, True)
    xc, xs = phases(GX, KX, True)
    fold = np.where(np.arange(KZ) == 0, 1.0, 2.0) / float(GX * GY * GZ)
    out = {}
    ycr = yc.T.reshape(KYH, KYL, GY).transpose(1, 0, 2)
    ysr = ys.T.reshape(KYH, KYL, GY).transpose(1, 0, 2)
    fwd = np.stack([ycr, -ysr], axis=1).reshape(2 * KY, GY)
    high, low = split_table(fwd)
    out["yf"] = np.block([[high, high], [low, low]])
    inv = np.stack([ycr, -ysr], axis=1).reshape(2 * KY, GY).T
    high, low = split_table(inv)
    out["yi"] = np.concatenate([high, high, low], axis=1)
    core = np.stack([np.stack([zc, -zs]), np.stack([zs, zc])])
    for name, scale in (("zf", np.ones(KZ)), ("zg", fold)):
        table = (core * scale).transpose(0, 2, 1, 3)[:, :, :, None, :]
        table = np.broadcast_to(table, (2, GZ, 2, BLOCKS, KZ))
        high, low = split_table(table.reshape(2 * GZ, 2 * TILE))
        out[name] = np.stack([high, low])
    core = np.stack([np.stack([zc, zs]), np.stack([-zs, zc])])
    for name, scale in (("zi", fold), ("zj", np.ones(KZ))):
        table = np.zeros((2, QUAD, KYL, KZ, QUAD, KYL, 2, GZ))
        for q in range(QUAD):
            for k in range(KYL):
                table[:, q, k, :, q, k, :, :] = (core * scale).transpose(0, 3, 1, 2)
        out[name + "h"], out[name + "l"] = split_table(table.reshape(2 * TILE, WIDE))
    core = np.stack([np.stack([xc, xs]), np.stack([-xs, xc])])
    table = core.reshape(2, 2, PEERS, PLANES, KX).transpose(0, 4, 2, 1, 3).reshape(2 * KX, 2 * GX)
    high, low = split_table(table)
    out["xfh"], out["xfl"] = high, low
    core = np.stack([np.stack([xc, -xs]), np.stack([xs, xc])])
    table = core.reshape(2, 2, PEERS, PLANES, KX).transpose(2, 0, 3, 1, 4).reshape(2 * GX, 2 * KX)
    high, low = split_table(table)
    out["xi"] = np.concatenate([high, high, low], axis=1)
    spread = np.repeat(np.eye(2 * KX), CH, axis=1).astype(ml_dtypes.bfloat16)
    out["spread"] = np.concatenate([spread, spread], axis=0)
    out["rep"] = np.repeat(np.eye(CH), 8, axis=0).astype(ml_dtypes.bfloat16)
    out["gather"] = np.concatenate([spread, spread], axis=0).T.copy()
    return out


def halves(values):
    high = values.astype(BF)
    return high, (values - high.astype(F32)).astype(BF)


def dot(left, right):
    return jnp.dot(left, right, preferred_element_type=F32)


def dot3(high, low, table_high, table_low):
    rows = high.shape[0]
    both = dot(jnp.concatenate([high, low], axis=0), table_high)
    return both[:rows] + both[rows:] + dot(high, table_low)


def lines_to_modes(pair, yf):
    high, low = halves(pair)
    both = dot(yf, jnp.concatenate([high, low], axis=0))
    return halves(both[: 2 * KY] + both[2 * KY :])


def call(body, us, grid, ins, outs, shapes, scratch, aliases=None):
    return pl.pallas_call(
        body,
        grid=grid,
        in_specs=ins,
        out_specs=outs,
        out_shape=shapes,
        scratch_shapes=scratch,
        input_output_aliases=aliases or {},
        cost_estimate=pl.CostEstimate(flops=int(us * 1e9), bytes_accessed=int(us * 3e6), transcendentals=0),
        compiler_params=pltpu.CompilerParams(
            dimension_semantics=("arbitrary",), vmem_limit_bytes=VMEM
        ),
    )


def whole(array):
    zeros = (0,) * array.ndim
    return pl.BlockSpec(array.shape, lambda step: zeros)


def store_modes(high, low, x, half, high_s, low_s):
    for j in range(2):
        for k in range(KYL):
            to = ((2 * half + j) * KYL + k) * ROWS + x * KYH
            for part in range(2):
                rows = slice((2 * k + part) * KYH, (2 * k + part + 1) * KYH)
                take = (rows, slice(j * GZ, (j + 1) * GZ))
                put = (slice(to, to + KYH), slice(part * GZ, (part + 1) * GZ))
                high_s[put] = high[take]
                low_s[put] = low[take]


def send_modes(high_s, low_s, table_ref, out_ref):
    full = dot3(high_s[...], low_s[...], table_ref[0], table_ref[1])
    owner = lax.broadcasted_iota(jnp.int32, (ROWS, 2 * TILE), 1) % TILE // KZ
    sums = full[:ROWS]
    for i in range(1, BLOCKS):
        sums = jnp.where(owner == i, full[i * ROWS : (i + 1) * ROWS], sums)
    for part in range(2):
        block = sums[:, part * TILE : (part + 1) * TILE].reshape(PLANES, KYH, TILE)
        out_ref[:, part * PLANES : (part + 1) * PLANES, :] = jnp.swapaxes(block, 0, 1)


def spectrum_body(f_ref, yf_ref, table_ref, out_ref, high_s, low_s):
    yf = yf_ref[...]
    for x in range(PLANES):
        for half in range(2):
            pair = jnp.concatenate([f_ref[2 * half, x], f_ref[2 * half + 1, x]], axis=1)
            high, low = lines_to_modes(pair, yf)
            store_modes(high, low, x, half, high_s, low_s)
    send_modes(high_s, low_s, table_ref, out_ref)


def channel_block(first):
    return pl.BlockSpec((QUAD, PLANES, GY, GZ), lambda g: (g + first, 0, 0, 0))


def moved_block(per=1):
    return pl.BlockSpec((PEERS, 2 * PLANES, per * TILE), lambda g: (0, 0, g))


def weight_block(at):
    return pl.BlockSpec((2, PER * QUAD, PAIRS, MODES_O), lambda g: (0, g + at // PER, 0, 0))


def hat_block(at):
    return pl.BlockSpec((2 * KX, PER * TILE), lambda g: (0, g + at // PER))


def moved_shape(groups):
    return jax.ShapeDtypeStruct((PEERS, 2 * PLANES, groups * TILE), F32)


def mode_scratch():
    return [pltpu.VMEM((BLOCKS * ROWS, 2 * GZ), BF), pltpu.VMEM((BLOCKS * ROWS, 2 * GZ), BF)]


def spectrum(field, first, count, t):
    tables = (t["yf"], t["zf"])
    return call(
        spectrum_body,
        2 * count,
        (count,),
        [channel_block(first)] + [whole(a) for a in tables],
        moved_block(),
        moved_shape(count),
        mode_scratch(),
    )(field, *tables)


def own_mask():
    rows = lax.broadcasted_iota(jnp.int32, (TILE, TILE), 0) % QUAD
    lanes = lax.broadcasted_iota(jnp.int32, (TILE, TILE), 1) // PAIRS
    return rows == lanes


def x_forward(moved, xfh, xfl):
    high, low = halves(moved)
    both = dot(jnp.concatenate([xfh, xfl], axis=0), high)
    return both[: 2 * KX] + both[2 * KX :] + dot(xfh, low)


def x_inverse(spec, xi):
    high, low = halves(spec)
    return dot(xi, jnp.concatenate([high, low, high], axis=0))


def spread_modes(spec, spread):
    turned = jnp.concatenate([spec, spec], axis=0).T
    high, low = halves(turned)
    lanes = lax.broadcasted_iota(jnp.int32, (TILE, 4 * KX), 1)
    return dot(jnp.where(lanes < 2 * KX, high, low), spread)


def mix_body(first, last, count, *refs):
    moved_ref, w_ref, xfh_ref, xfl_ref, spread_ref, xi_ref = refs[:6]
    refs = refs[6:]
    if not first:
        start_ref, refs = refs[0], refs[2:]
    hat_ref, refs = refs[0], refs[1:]
    if last:
        out_refs, (acc_s, turn_s) = refs[:-2], refs[-2:]
    else:
        (acc_s,) = refs
    step = pl.program_id(0)

    @pl.when(step == 0)
    def _():
        acc_s[...] = jnp.zeros_like(acc_s) if first else start_ref[...]

    hat = x_forward(moved_ref[...].reshape(2 * GX, PER * TILE), xfh_ref[...], xfl_ref[...])
    hat_ref[...] = hat
    acc_re, acc_im = acc_s[0], acc_s[1]
    for u in range(PER):
        wide = spread_modes(hat[:, u * TILE : (u + 1) * TILE], spread_ref[...])
        for q in range(QUAD):
            h_re = wide[q * PAIRS : (q + 1) * PAIRS, :MODES_O]
            h_im = wide[q * PAIRS : (q + 1) * PAIRS, MODES_O:]
            w_re, w_im = w_ref[0, u * QUAD + q], w_ref[1, u * QUAD + q]
            acc_re = acc_re + (h_re * w_re - h_im * w_im)
            acc_im = acc_im + (h_re * w_im + h_im * w_re)
    acc_s[0] = acc_re
    acc_s[1] = acc_im

    if last:

        @pl.when(step == count - 1)
        def _():
            mask = own_mask()
            for part in range(2):
                full = jnp.concatenate([acc_s[part]] * QUAD, axis=0)
                for k in range(MODES_O // TILE):
                    turned = full[:, k * TILE : (k + 1) * TILE].T
                    turn_s[pl.ds(part * MODES_O + k * TILE, TILE), :] = jnp.where(mask, turned, 0.0)
            xi = xi_ref[...]
            per = GROUPS // len(out_refs)
            for g in range(0, GROUPS, 2):
                tiles = []
                for h in range(g, g + 2):
                    parts = []
                    for part in range(2):
                        total = None
                        for q in range(QUAD):
                            rows = turn_s[pl.ds(part * MODES_O + h * QUAD + q, KX, stride=CH), :]
                            total = rows if total is None else total + rows
                        parts.append(total)
                    tiles.append(jnp.concatenate(parts, axis=0))
                wave = x_inverse(jnp.concatenate(tiles, axis=1), xi).reshape(PEERS, 2 * PLANES, 2 * TILE)
                for h in range(g, g + 2):
                    to = (h % per) * TILE
                    out_refs[h // per][:, :, to : to + TILE] = wave[:, :, (h - g) * TILE : (h - g + 1) * TILE]


def mix(moved, weights, so_far, at, count, chunks, t):
    first, last = not so_far, at + count == GROUPS
    tables = (t["xfh"], t["xfl"], t["spread"], t["xi"])
    hat = jax.ShapeDtypeStruct((2 * KX, CH * PAIRS), F32)
    acc = jax.ShapeDtypeStruct((2, PAIRS, MODES_O), F32)
    outs = [moved_shape(n) for n in chunks] if last else [acc]
    scratch = [pltpu.VMEM(acc.shape, F32), pltpu.VMEM((2 * MODES_O, TILE), F32)] if last else []
    before = [] if first else [whole(acc), pl.BlockSpec(memory_space=pl.ANY)]
    return call(
        functools.partial(mix_body, first, last, count // PER),
        5,
        (count // PER,),
        [moved_block(PER), weight_block(at)] + [whole(a) for a in tables] + before,
        [hat_block(at)] + [whole(a) for a in outs],
        [hat] + outs,
        scratch,
        aliases={} if first else {7: 0},
    )(moved, weights, *tables, *so_far)


def input_body(first, moved_refs, g_ref, w_ref, xfh_ref, xfl_ref, gather_ref, xi_ref, out_ref, turn_s):
    if first:

        @pl.when(pl.program_id(0) == 0)
        def _():
            lanes = lax.broadcasted_iota(jnp.int32, (KX, TILE), 1) // PAIRS
            per = GROUPS // len(moved_refs)
            for h in range(GROUPS):
                at = (h % per) * TILE
                tile = moved_refs[h // per][:, :, at : at + TILE].reshape(2 * GX, TILE)
                hat = x_forward(tile, xfh_ref[...], xfl_ref[...])
                for part in range(2):
                    rows = hat[part * KX : (part + 1) * KX]
                    for q in range(QUAD):
                        to = pl.ds(part * MODES_O + h * QUAD + q, KX, stride=CH)
                        turn_s[to, :] = jnp.where(lanes == q, rows, 0.0)
            for part in range(2):
                for k in range(MODES_O // TILE):
                    turned = turn_s[pl.ds(part * MODES_O + k * TILE, TILE), :].T
                    total = turned[:PAIRS]
                    for q in range(1, QUAD):
                        total = total + turned[q * PAIRS : (q + 1) * PAIRS]
                    g_ref[part, :, k * TILE : (k + 1) * TILE] = total

    g_re, g_im = g_ref[0], g_ref[1]
    rows_high, rows_low = [], []
    for c in range(PER * QUAD):
        w_re, w_im = w_ref[0, c], w_ref[1, c]
        full = jnp.concatenate([g_re * w_re + g_im * w_im, g_im * w_re - g_re * w_im], axis=1)
        high, low = halves(full)
        rows_high.append(high)
        rows_low.append(low)
    both = dot(jnp.concatenate(rows_high + rows_low, axis=0), gather_ref[...])
    both = both[: PER * TILE] + both[PER * TILE :]
    spec = jnp.concatenate([both[u * TILE : (u + 1) * TILE].T[: 2 * KX] for u in range(PER)], axis=1)
    out_ref[...] = x_inverse(spec, xi_ref[...]).reshape(PEERS, 2 * PLANES, PER * TILE)


def input_modes(moved, grad, weights, at, count, t):
    tables = (t["xfh"], t["xfl"], t["gather"], t["xi"])
    shape = jax.ShapeDtypeStruct((2, PAIRS, MODES_O), F32)
    first = grad is None
    if first:

        def body(*refs):
            n = len(moved)
            w, xfh, xfl, gather, xi, g, out, turn = refs[n:]
            input_body(True, refs[:n], g, w, xfh, xfl, gather, xi, out, turn)

        return call(
            body,
            7,
            (count // PER,),
            [whole(a) for a in moved] + [weight_block(at)] + [whole(a) for a in tables],
            [whole(shape), moved_block(PER)],
            [shape, moved_shape(count)],
            [pltpu.VMEM((2 * MODES_O, TILE), F32)],
        )(*moved, weights, *tables)

    def body(g, w, xfh, xfl, gather, xi, out):
        input_body(False, None, g, w, xfh, xfl, gather, xi, out, None)

    out = call(
        body,
        6,
        (count // PER,),
        [whole(shape), weight_block(at)] + [whole(a) for a in tables],
        moved_block(PER),
        moved_shape(count),
        [],
    )(grad, weights, *tables)
    return grad, out


def weight_grad_body(hat_ref, far_hat_ref, g_ref, far_g_ref, spread_ref, *refs):
    out_ref = refs[-1]
    spread = spread_ref[...]
    for u in range(PER):
        lanes = slice(u * TILE, (u + 1) * TILE)
        near = spread_modes(hat_ref[:, lanes], spread)
        far = spread_modes(far_hat_ref[:, lanes], spread)
        for q in range(QUAD):
            rows = slice(q * PAIRS, (q + 1) * PAIRS)
            n_re, n_im = near[rows, :MODES_O], near[rows, MODES_O:]
            f_re, f_im = far[rows, :MODES_O], far[rows, MODES_O:]
            c = u * QUAD + q
            out_ref[0, c] = n_re * g_ref[0] + n_im * g_ref[1] + f_re * far_g_ref[0] + f_im * far_g_ref[1]
            out_ref[1, c] = n_re * g_ref[1] - n_im * g_ref[0] + f_re * far_g_ref[1] - f_im * far_g_ref[0]


def weight_grad(hat, far_hat, grad, far_grad, at, count, so_far, t):
    return call(
        weight_grad_body,
        count,
        (count // PER,),
        [hat_block(at), hat_block(at), whole(grad), whole(far_grad), whole(t["spread"])]
        + [pl.BlockSpec(memory_space=pl.ANY)] * len(so_far),
        weight_block(at),
        jax.ShapeDtypeStruct((2, CH, PAIRS, MODES_O), F32),
        [],
        aliases={5 + i: i for i in range(len(so_far))},
    )(hat, far_hat, grad, far_grad, t["spread"], *so_far)


def gelu_parts(pre):
    bell = jnp.exp(pre * pre * -0.5)
    t = 1.0 / (1.0 + (0.3275911 * math.sqrt(0.5)) * jnp.abs(pre))
    poly = 1.061405429 * 0.5
    for coefficient in (-1.453152027, 1.421413741, -0.284496736, 0.254829592):
        poly = poly * t + coefficient * 0.5
    tail = poly * t * bell
    share = jnp.where(pre >= 0.0, 1.0 - tail, tail)
    return share, pre * bell * (1.0 / math.sqrt(2.0 * math.pi))


def arrive(arrived_ref, zih, zil):
    parts = []
    for part in range(2):
        block = arrived_ref[:, part * PLANES : (part + 1) * PLANES, :]
        parts.append(jnp.swapaxes(block, 0, 1).reshape(PLANES * KYH, TILE))
    high, low = halves(jnp.concatenate(parts, axis=1))
    return halves(dot3(high, low, zih, zil))


def inverse_pair(high, low, x, half, yi):
    stacks = []
    for source in (high, low):
        sides = []
        for j in range(2):
            lanes = (2 * half + j) * 2 * KYL * GZ
            pieces = [
                source[x * KYH : (x + 1) * KYH, lanes + k * GZ : lanes + (k + 1) * GZ] for k in range(2 * KYL)
            ]
            sides.append(jnp.concatenate(pieces, axis=0))
        stacks.append(jnp.concatenate(sides, axis=1))
    return dot(yi, jnp.concatenate([stacks[0], stacks[1], stacks[0]], axis=0))


def kron_halves(matrix, rep):
    rows = lax.broadcasted_iota(jnp.int32, (8 * CH, 8 * CH), 0) % 8
    lanes = lax.broadcasted_iota(jnp.int32, (8 * CH, 8 * CH), 1) % 8
    wide = []
    for half in halves(matrix):
        tall = dot(rep, half).astype(BF)
        full = lax.dot_general(tall, rep, (((1,), (1,)), ((), ())), preferred_element_type=F32)
        wide.append(jnp.where(rows == lanes, full, 0.0).astype(BF))
    return jnp.concatenate(wide, axis=0)


def channel_sum_body(data_ref, matrix_ref, rep_ref, *refs):
    out_ref, kron_s = refs[-2:]

    @pl.when(pl.program_id(0) == 0)
    def _():
        kron_s[...] = kron_halves(matrix_ref[...], rep_ref[...])

    for x in range(data_ref.shape[1]):
        for i in range(GY // 16):
            tiles = [data_ref[:, x, i * 16 + 8 * j : i * 16 + 8 * j + 8, :].reshape(8 * CH, GZ) for j in range(2)]
            high, low = halves(jnp.concatenate(tiles, axis=1))
            both = dot(kron_s[...], high)
            sums = both[: 8 * CH] + both[8 * CH :] + dot(kron_s[: 8 * CH], low)
            for j in range(2):
                at = slice(i * 16 + 8 * j, i * 16 + 8 * j + 8)
                out_ref[:, x, at, :] = sums[:, j * GZ : (j + 1) * GZ].reshape(CH, 8, GZ)


def channel_sum(data, matrix, first, count, step, so_far, t):
    block = pl.BlockSpec((CH, step, GY, GZ), lambda x: (0, x + first // step, 0, 0))
    return call(
        channel_sum_body,
        2 * count,
        (count // step,),
        [block, whole(matrix), whole(t["rep"])] + [pl.BlockSpec(memory_space=pl.ANY)] * len(so_far),
        block,
        jax.ShapeDtypeStruct(data.shape, F32),
        [pltpu.VMEM((16 * CH, 8 * CH), BF)],
        aliases={3 + i: i for i in range(len(so_far))},
    )(data, matrix, t["rep"], *so_far)


def middle_body(
    arrived_ref, sum_ref, cot_ref, yi_ref, zih_ref, zil_ref, yf_ref, zg_ref, *refs
):
    out_ref, grad_ref, spec_ref, high_s, low_s = refs[-5:]
    high, low = arrive(arrived_ref, zih_ref[...], zil_ref[...])
    yi, yf = yi_ref[...], yf_ref[...]
    for x in range(PLANES):
        for half in range(2):
            waves = inverse_pair(high, low, x, half, yi)
            grads = []
            for j in range(2):
                c = 2 * half + j
                pre = waves[:, j * GZ : (j + 1) * GZ] + sum_ref[c, x]
                share, slope = gelu_parts(pre)
                out_ref[c, x] = pre * share
                grad = cot_ref[c, x] * (share + slope)
                grad_ref[c, x] = grad
                grads.append(grad)
            store_modes(*lines_to_modes(jnp.concatenate(grads, axis=1), yf), x, half, high_s, low_s)
    send_modes(high_s, low_s, zg_ref, spec_ref)


def middle(arrived, sums, cotangent, first, count, so_far, t):
    tables = (t["yi"], t["zih"], t["zil"], t["yf"], t["zg"])
    block = channel_block(first)
    shape = jax.ShapeDtypeStruct(sums.shape, F32)
    n = 3 + len(tables)
    return call(
        middle_body,
        5 * count,
        (count,),
        [moved_block(), block, block] + [whole(a) for a in tables] + [pl.BlockSpec(memory_space=pl.ANY)] * len(so_far),
        [block, block, moved_block()],
        [shape, shape, moved_shape(count)],
        mode_scratch(),
        aliases={n + i: i for i in range(len(so_far))},
    )(arrived, sums, cotangent, *tables, *so_far)


def last_body(arrived_ref, sum_ref, yi_ref, zjh_ref, zjl_ref, *refs):
    out_ref = refs[-1]
    high, low = arrive(arrived_ref, zjh_ref[...], zjl_ref[...])
    yi = yi_ref[...]
    for x in range(PLANES):
        for half in range(2):
            waves = inverse_pair(high, low, x, half, yi)
            for j in range(2):
                c = 2 * half + j
                out_ref[c, x] = waves[:, j * GZ : (j + 1) * GZ] + sum_ref[c, x]


def last(arrived, sums, first, count, so_far, t):
    tables = (t["yi"], t["zjh"], t["zjl"])
    block = channel_block(first)
    n = 2 + len(tables)
    return call(
        last_body,
        2.5 * count,
        (count,),
        [moved_block(), block] + [whole(a) for a in tables] + [pl.BlockSpec(memory_space=pl.ANY)] * len(so_far),
        block,
        jax.ShapeDtypeStruct(sums.shape, F32),
        [],
        aliases={n + i: i for i in range(len(so_far))},
    )(arrived, sums, *tables, *so_far)


def swap_slabs(array):
    return lax.all_to_all(array, "slab", split_axis=0, concat_axis=0, tiled=True)


CHUNKS = (4, 4)
STARTS = tuple(sum(CHUNKS[:k]) for k in range(len(CHUNKS)))


def on_device(field, cotangent, spec_weight, bypass_weight):
    shape = (field.shape[1], field.shape[2], spec_weight.shape[2], lax.axis_size("slab"), lax.axis_size("dp"))
    if shape != (CH, PLANES, PAIRS, PEERS, 2):
        return on_device_any(field, cotangent, spec_weight, bypass_weight)
    t = {name: jnp.asarray(table) for name, table in host_tables().items()}
    source, other = field[0], cotangent[0]
    swap_pair = [(0, 1), (1, 0)]
    parts = list(zip(STARTS, CHUNKS))
    ahead = lax.optimization_barrier

    turned = bypass_weight.T
    moved, sums = [], ()
    for at, n in parts:
        sent = spectrum(source, at, n, t)
        if moved:
            sums = (channel_sum(source, turned, 0, 2, 1, (), t),)
            moved[-1], sent, *sums = ahead((moved[-1], sent, *sums))
        moved.append(swap_slabs(sent))
    sums = (channel_sum(source, turned, 2, 4, 1, tuple(sums), t),)
    moved[-1], *sums = ahead((moved[-1], *sums))
    hat, state = None, ()
    for arrived, (at, n) in zip(moved, parts):
        hat, *state = mix(arrived, spec_weight, (*state, hat) if state else (), at, n, CHUNKS, t)
    far_hat = lax.ppermute(hat, "dp", swap_pair)
    sums = channel_sum(source, turned, 6, 2, 1, tuple(sums), t)
    so_far, cot_moved, arrived = (), [], []
    for sent in state:
        if arrived:
            arrived[-1], sums, sent = ahead((arrived[-1], sums, sent))
        arrived.append(swap_slabs(sent))
    for k, (at, n) in enumerate(parts):
        *so_far, sent = middle(arrived[k], sums, other, at, n, so_far, t)
        if k == 0:
            arrived[-1], sent = ahead((arrived[-1], sent))
        else:
            cot_moved[-1], sent = ahead((cot_moved[-1], sent))
        cot_moved.append(swap_slabs(sent))
    result, grad_pre = so_far
    back_sums = channel_sum(grad_pre, bypass_weight, 0, PLANES, 2, (), t)
    cot_moved[-1], back_sums, far_hat = ahead((cot_moved[-1], back_sums, far_hat))
    grad, back_arrived, made = None, [], ()
    for at, n in parts:
        grad, sent = input_modes(cot_moved, grad, spec_weight, at, n, t)
        if back_arrived:
            made = (weight_grad(hat, far_hat, grad, far_grad, 0, n, (), t),)
            back_arrived[-1], sent, *made = ahead((back_arrived[-1], sent, *made))
        else:
            far_grad = lax.ppermute(grad, "dp", swap_pair)
        back_arrived.append(swap_slabs(sent))
    grad_spec = weight_grad(hat, far_hat, grad, far_grad, CHUNKS[0], GROUPS - CHUNKS[0], tuple(made), t)
    back = ()
    for k, (at, n) in enumerate(parts):
        if k == 1:
            back_arrived[k], back, grad_spec = ahead((back_arrived[k], back, grad_spec))
        back = (last(back_arrived[k], back_sums, at, n, back, t),)
    return (result[None], back[0][None], grad_spec)


def solution(mesh):
    in_specs = (
        P("dp", None, "slab", None, None),
        P("dp", None, "slab", None, None),
        P(None, None, "slab", None),
        P(),
    )
    out_specs = (
        P("dp", None, "slab", None, None),
        P("dp", None, "slab", None, None),
        P(None, None, "slab", None),
    )
    return jax.shard_map(
        on_device, mesh=mesh, in_specs=in_specs, out_specs=out_specs, check_vma=False
    )
```

```python
import functools
import math

import jax
import jax.numpy as jnp
import ml_dtypes
import numpy as np
from jax import lax
from jax.experimental import pallas as pl
from jax.experimental.pallas import tpu as pltpu
from jax.sharding import PartitionSpec as P

GX = 128
GY = 128
GZ = 128
KX = 32
KY = 32
KZ = 16


precise = lax.Precision.HIGHEST


def wave_tables(length, count, signed):
    positions = jnp.arange(length, dtype=jnp.int32)
    indices = jnp.arange(count, dtype=jnp.int32)
    if signed:
        freqs = jnp.where(indices < count // 2, indices, indices - count)
    else:
        freqs = indices
    phase = positions[:, None] * freqs[None, :] % length
    angle = phase.astype(jnp.float32) * (2.0 * math.pi / length)
    return (jnp.cos(angle), jnp.sin(angle))


def gelu_exact(values):
    return jax.nn.gelu(values, approximate=False)


def plane_spectrum(data, weight, z_cos, z_sin, y_cos, y_sin):
    chans, planes = (data.shape[0], data.shape[1])
    part_re = jnp.einsum("cxyz,zk->cxky", data, z_cos, precision=precise)
    part_im = -jnp.einsum("cxyz,zk->cxky", data, z_sin, precision=precise)
    mid_re = jnp.einsum("cxky,yj->cxjk", part_re, y_cos, precision=precise) + jnp.einsum(
        "cxky,yj->cxjk", part_im, y_sin, precision=precise
    )
    mid_im = jnp.einsum("cxky,yj->cxjk", part_im, y_cos, precision=precise) - jnp.einsum(
        "cxky,yj->cxjk", part_re, y_sin, precision=precise
    )
    stacked = jnp.stack([mid_re * weight, mid_im * weight])
    return stacked.reshape(2, chans, planes, KY * KZ)


def along_first(moved, x_cos, x_sin):
    line_re, line_im = (moved[0], moved[1])
    full_re = jnp.einsum("cxp,xi->cpi", line_re, x_cos, precision=precise) + jnp.einsum(
        "cxp,xi->cpi", line_im, x_sin, precision=precise
    )
    full_im = jnp.einsum("cxp,xi->cpi", line_im, x_cos, precision=precise) - jnp.einsum(
        "cxp,xi->cpi", line_re, x_sin, precision=precise
    )
    return (full_re, full_im)


def back_first(spec_re, spec_im, x_cos, x_sin):
    wide_re = jnp.einsum("cpi,xi->cxp", spec_re, x_cos, precision=precise) - jnp.einsum(
        "cpi,xi->cxp", spec_im, x_sin, precision=precise
    )
    wide_im = jnp.einsum("cpi,xi->cxp", spec_re, x_sin, precision=precise) + jnp.einsum(
        "cpi,xi->cxp", spec_im, x_cos, precision=precise
    )
    return jnp.stack([wide_re, wide_im])


def plane_inverse(arrived, weight, z_cos, z_sin, y_cos, y_sin):
    chans, planes = (arrived.shape[1], arrived.shape[2])
    shaped = arrived.reshape(2, chans, planes, KY, KZ)
    wide_re, wide_im = (shaped[0], shaped[1])
    plane_re = jnp.einsum("cxjk,yj->cxky", wide_re, y_cos, precision=precise) - jnp.einsum(
        "cxjk,yj->cxky", wide_im, y_sin, precision=precise
    )
    plane_im = jnp.einsum("cxjk,yj->cxky", wide_re, y_sin, precision=precise) + jnp.einsum(
        "cxjk,yj->cxky", wide_im, y_cos, precision=precise
    )
    plane_re = plane_re * weight[:, None]
    plane_im = plane_im * weight[:, None]
    return jnp.einsum("cxky,zk->cxyz", plane_re, z_cos, precision=precise) - jnp.einsum(
        "cxky,zk->cxyz", plane_im, z_sin, precision=precise
    )


def on_device_any(field, cotangent, spec_weight, bypass_weight):
    count = lax.axis_size("slab")
    pairs = KY * KZ // count
    chans = field.shape[1]
    z_cos, z_sin = wave_tables(GZ, KZ, False)
    y_cos, y_sin = wave_tables(GY, KY, True)
    x_cos, x_sin = wave_tables(GX, KX, True)
    kz_index = jnp.arange(KZ, dtype=jnp.int32)
    fold = jnp.where(kz_index == 0, 1.0, 2.0).astype(jnp.float32) / float(GX * GY * GZ)
    ones = jnp.ones((KZ,), jnp.float32)
    weights = spec_weight.reshape(2, chans, pairs, KX, chans)
    w_real = weights[0]
    w_imag = weights[1]
    source = field[0]
    local_spec = plane_spectrum(source, ones, z_cos, z_sin, y_cos, y_sin)
    moved = lax.all_to_all(local_spec, "slab", split_axis=3, concat_axis=2, tiled=True)
    hat_re, hat_im = along_first(moved, x_cos, x_sin)
    mix_re = jnp.einsum("cpi,cpio->opi", hat_re, w_real, precision=precise) - jnp.einsum(
        "cpi,cpio->opi", hat_im, w_imag, precision=precise
    )
    mix_im = jnp.einsum("cpi,cpio->opi", hat_re, w_imag, precision=precise) + jnp.einsum(
        "cpi,cpio->opi", hat_im, w_real, precision=precise
    )
    outgoing = back_first(mix_re, mix_im, x_cos, x_sin)
    arrived = lax.all_to_all(outgoing, "slab", split_axis=2, concat_axis=3, tiled=True)
    spectral = plane_inverse(arrived, fold, z_cos, z_sin, y_cos, y_sin)
    pre = spectral + jnp.einsum("co,cxyz->oxyz", bypass_weight, source, precision=precise)
    result, pullback = jax.vjp(gelu_exact, pre)
    grad_pre = pullback(cotangent[0])[0]
    fold_grid = jnp.broadcast_to(fold, (KY, KZ))
    cot_spec = plane_spectrum(grad_pre, fold_grid, z_cos, z_sin, y_cos, y_sin)
    cot_moved = lax.all_to_all(cot_spec, "slab", split_axis=3, concat_axis=2, tiled=True)
    grad_re, grad_im = along_first(cot_moved, x_cos, x_sin)
    own_real = jnp.einsum("cpi,opi->cpio", hat_re, grad_re, precision=precise) + jnp.einsum(
        "cpi,opi->cpio", hat_im, grad_im, precision=precise
    )
    own_imag = jnp.einsum("cpi,opi->cpio", hat_re, grad_im, precision=precise) - jnp.einsum(
        "cpi,opi->cpio", hat_im, grad_re, precision=precise
    )
    summed = lax.psum(jnp.stack([own_real, own_imag]), "dp")
    grad_spec = summed.reshape(2, chans, pairs, KX * chans)
    input_re = jnp.einsum("opi,cpio->cpi", grad_re, w_real, precision=precise) + jnp.einsum(
        "opi,cpio->cpi", grad_im, w_imag, precision=precise
    )
    input_im = jnp.einsum("opi,cpio->cpi", grad_im, w_real, precision=precise) - jnp.einsum(
        "opi,cpio->cpi", grad_re, w_imag, precision=precise
    )
    grad_out = back_first(input_re, input_im, x_cos, x_sin)
    grad_arrived = lax.all_to_all(grad_out, "slab", split_axis=2, concat_axis=3, tiled=True)
    back_field = plane_inverse(grad_arrived, ones, z_cos, z_sin, y_cos, y_sin)
    back_field = back_field + jnp.einsum(
        "co,oxyz->cxyz", bypass_weight, grad_pre, precision=precise
    )
    return (result[None], back_field[None], grad_spec)


CH = 32
PLANES = 8
PAIRS = 32
PEERS = 16
KYL = PAIRS // KZ
KYH = KY // KYL
QUAD = 4
GROUPS = CH // QUAD
TILE = QUAD * PAIRS
PER = 2
BLOCKS = QUAD * KYL
WIDE = BLOCKS * 2 * GZ
ROWS = PLANES * KYH
MODES_O = KX * CH

VMEM = 52 * 1024 * 1024

BF = jnp.bfloat16
F32 = jnp.float32


def split_table(table):
    high = table.astype(ml_dtypes.bfloat16)
    low = (table - high.astype(np.float64)).astype(ml_dtypes.bfloat16)
    return high, low


def phases(length, count, signed):
    freqs = np.arange(count)
    if signed:
        freqs = np.where(freqs < count // 2, freqs, freqs - count)
    phase = (np.arange(length)[:, None] * freqs[None, :]) % length
    angle = phase * (2.0 * np.pi / length)
    return np.cos(angle), np.sin(angle)


@functools.lru_cache(maxsize=None)
def host_tables():
    zc, zs = phases(GZ, KZ, False)
    yc, ys = phases(GY, KY, True)
    xc, xs = phases(GX, KX, True)
    fold = np.where(np.arange(KZ) == 0, 1.0, 2.0) / float(GX * GY * GZ)
    out = {}
    ycr = yc.T.reshape(KYH, KYL, GY).transpose(1, 0, 2)
    ysr = ys.T.reshape(KYH, KYL, GY).transpose(1, 0, 2)
    fwd = np.stack([ycr, -ysr], axis=1).reshape(2 * KY, GY)
    high, low = split_table(fwd)
    out["yf"] = np.block([[high, high], [low, low]])
    inv = np.stack([ycr, -ysr], axis=1).reshape(2 * KY, GY).T
    high, low = split_table(inv)
    out["yi"] = np.concatenate([high, high, low], axis=1)
    core = np.stack([np.stack([zc, -zs]), np.stack([zs, zc])])
    for name, scale in (("zf", np.ones(KZ)), ("zg", fold)):
        table = (core * scale).transpose(0, 2, 1, 3)[:, :, :, None, :]
        table = np.broadcast_to(table, (2, GZ, 2, BLOCKS, KZ))
        high, low = split_table(table.reshape(2 * GZ, 2 * TILE))
        out[name] = np.stack([high, low])
    core = np.stack([np.stack([zc, zs]), np.stack([-zs, zc])])
    for name, scale in (("zi", fold), ("zj", np.ones(KZ))):
        table = np.zeros((2, QUAD, KYL, KZ, QUAD, KYL, 2, GZ))
        for q in range(QUAD):
            for k in range(KYL):
                table[:, q, k, :, q, k, :, :] = (core * scale).transpose(0, 3, 1, 2)
        out[name + "h"], out[name + "l"] = split_table(table.reshape(2 * TILE, WIDE))
    core = np.stack([np.stack([xc, xs]), np.stack([-xs, xc])])
    table = core.reshape(2, 2, PEERS, PLANES, KX).transpose(0, 4, 2, 1, 3).reshape(2 * KX, 2 * GX)
    high, low = split_table(table)
    out["xfh"], out["xfl"] = high, low
    core = np.stack([np.stack([xc, -xs]), np.stack([xs, xc])])
    table = core.reshape(2, 2, PEERS, PLANES, KX).transpose(2, 0, 3, 1, 4).reshape(2 * GX, 2 * KX)
    high, low = split_table(table)
    out["xi"] = np.concatenate([high, high, low], axis=1)
    spread = np.repeat(np.eye(2 * KX), CH, axis=1).astype(ml_dtypes.bfloat16)
    out["spread"] = np.concatenate([spread, spread], axis=0)
    out["rep"] = np.repeat(np.eye(CH), 8, axis=0).astype(ml_dtypes.bfloat16)
    out["gather"] = np.concatenate([spread, spread], axis=0).T.copy()
    return out


def halves(values):
    high = values.astype(BF)
    return high, (values - high.astype(F32)).astype(BF)


def dot(left, right):
    return jnp.dot(left, right, preferred_element_type=F32)


def dot3(high, low, table_high, table_low):
    rows = high.shape[0]
    both = dot(jnp.concatenate([high, low], axis=0), table_high)
    return both[:rows] + both[rows:] + dot(high, table_low)


def lines_to_modes(pair, yf):
    high, low = halves(pair)
    both = dot(yf, jnp.concatenate([high, low], axis=0))
    return halves(both[: 2 * KY] + both[2 * KY :])


def call(body, us, grid, ins, outs, shapes, scratch, aliases=None, vmem=VMEM):
    return pl.pallas_call(
        body,
        grid=grid,
        in_specs=ins,
        out_specs=outs,
        out_shape=shapes,
        scratch_shapes=scratch,
        input_output_aliases=aliases or {},
        cost_estimate=pl.CostEstimate(flops=int(us * 1e9), bytes_accessed=int(us * 3e6), transcendentals=0),
        compiler_params=pltpu.CompilerParams(
            dimension_semantics=("arbitrary",), vmem_limit_bytes=vmem
        ),
    )


def whole(array):
    zeros = (0,) * array.ndim
    return pl.BlockSpec(array.shape, lambda step: zeros)


def store_modes(high, low, x, half, high_s, low_s):
    for j in range(2):
        for k in range(KYL):
            to = ((2 * half + j) * KYL + k) * ROWS + x * KYH
            for part in range(2):
                rows = slice((2 * k + part) * KYH, (2 * k + part + 1) * KYH)
                take = (rows, slice(j * GZ, (j + 1) * GZ))
                put = (slice(to, to + KYH), slice(part * GZ, (part + 1) * GZ))
                high_s[put] = high[take]
                low_s[put] = low[take]


def send_modes(high_s, low_s, table_ref, out_ref):
    full = dot3(high_s[...], low_s[...], table_ref[0], table_ref[1])
    owner = lax.broadcasted_iota(jnp.int32, (ROWS, 2 * TILE), 1) % TILE // KZ
    sums = full[:ROWS]
    for i in range(1, BLOCKS):
        sums = jnp.where(owner == i, full[i * ROWS : (i + 1) * ROWS], sums)
    for part in range(2):
        block = sums[:, part * TILE : (part + 1) * TILE].reshape(PLANES, KYH, TILE)
        out_ref[:, part * PLANES : (part + 1) * PLANES, :] = jnp.swapaxes(block, 0, 1)


def spectrum_body(f_ref, yf_ref, table_ref, out_ref, high_s, low_s):
    yf = yf_ref[...]
    for x in range(PLANES):
        for half in range(2):
            pair = jnp.concatenate([f_ref[2 * half, x], f_ref[2 * half + 1, x]], axis=1)
            high, low = lines_to_modes(pair, yf)
            store_modes(high, low, x, half, high_s, low_s)
    send_modes(high_s, low_s, table_ref, out_ref)


def channel_block(first):
    return pl.BlockSpec((QUAD, PLANES, GY, GZ), lambda g: (g + first, 0, 0, 0))


def moved_block(per=1):
    return pl.BlockSpec((PEERS, 2 * PLANES, per * TILE), lambda g: (0, 0, g))


def weight_block(at):
    return pl.BlockSpec((2, PER * QUAD, PAIRS, MODES_O), lambda g: (0, g + at // PER, 0, 0))


def hat_block(at):
    return pl.BlockSpec((2 * KX, PER * TILE), lambda g: (0, g + at // PER))


def moved_shape(groups):
    return jax.ShapeDtypeStruct((PEERS, 2 * PLANES, groups * TILE), F32)


def mode_scratch():
    return [pltpu.VMEM((BLOCKS * ROWS, 2 * GZ), BF), pltpu.VMEM((BLOCKS * ROWS, 2 * GZ), BF)]


def spectrum(field, first, count, t):
    tables = (t["yf"], t["zf"])
    return call(
        spectrum_body,
        2 * count,
        (count,),
        [channel_block(first)] + [whole(a) for a in tables],
        moved_block(),
        moved_shape(count),
        mode_scratch(),
        vmem=58 * 1024 * 1024,
    )(field, *tables)


def own_mask():
    rows = lax.broadcasted_iota(jnp.int32, (TILE, TILE), 0) % QUAD
    lanes = lax.broadcasted_iota(jnp.int32, (TILE, TILE), 1) // PAIRS
    return rows == lanes


def x_forward(moved, xfh, xfl):
    high, low = halves(moved)
    both = dot(jnp.concatenate([xfh, xfl], axis=0), high)
    return both[: 2 * KX] + both[2 * KX :] + dot(xfh, low)


def x_inverse(spec, xi):
    high, low = halves(spec)
    return dot(xi, jnp.concatenate([high, low, high], axis=0))


def spread_modes(spec, spread):
    turned = jnp.concatenate([spec, spec], axis=0).T
    high, low = halves(turned)
    lanes = lax.broadcasted_iota(jnp.int32, (TILE, 4 * KX), 1)
    return dot(jnp.where(lanes < 2 * KX, high, low), spread)


def mix_body(first, last, count, *refs):
    moved_ref, w_ref, xfh_ref, xfl_ref, spread_ref, xi_ref = refs[:6]
    refs = refs[6:]
    if not first:
        start_ref, refs = refs[0], refs[2:]
    hat_ref, refs = refs[0], refs[1:]
    if last:
        out_refs, (acc_s, turn_s) = refs[:-2], refs[-2:]
    else:
        (acc_s,) = refs
    step = pl.program_id(0)

    @pl.when(step == 0)
    def _():
        acc_s[...] = jnp.zeros_like(acc_s) if first else start_ref[...]

    hat = x_forward(moved_ref[...].reshape(2 * GX, PER * TILE), xfh_ref[...], xfl_ref[...])
    hat_ref[...] = hat
    acc_re, acc_im = acc_s[0], acc_s[1]
    for u in range(PER):
        wide = spread_modes(hat[:, u * TILE : (u + 1) * TILE], spread_ref[...])
        for q in range(QUAD):
            h_re = wide[q * PAIRS : (q + 1) * PAIRS, :MODES_O]
            h_im = wide[q * PAIRS : (q + 1) * PAIRS, MODES_O:]
            w_re, w_im = w_ref[0, u * QUAD + q], w_ref[1, u * QUAD + q]
            acc_re = acc_re + (h_re * w_re - h_im * w_im)
            acc_im = acc_im + (h_re * w_im + h_im * w_re)
    acc_s[0] = acc_re
    acc_s[1] = acc_im

    if last:

        @pl.when(step == count - 1)
        def _():
            mask = own_mask()
            for part in range(2):
                full = jnp.concatenate([acc_s[part]] * QUAD, axis=0)
                for k in range(MODES_O // TILE):
                    turned = full[:, k * TILE : (k + 1) * TILE].T
                    turn_s[pl.ds(part * MODES_O + k * TILE, TILE), :] = jnp.where(mask, turned, 0.0)
            xi = xi_ref[...]
            per = GROUPS // len(out_refs)
            for g in range(0, GROUPS, 2):
                tiles = []
                for h in range(g, g + 2):
                    parts = []
                    for part in range(2):
                        total = None
                        for q in range(QUAD):
                            rows = turn_s[pl.ds(part * MODES_O + h * QUAD + q, KX, stride=CH), :]
                            total = rows if total is None else total + rows
                        parts.append(total)
                    tiles.append(jnp.concatenate(parts, axis=0))
                wave = x_inverse(jnp.concatenate(tiles, axis=1), xi).reshape(PEERS, 2 * PLANES, 2 * TILE)
                for h in range(g, g + 2):
                    to = (h % per) * TILE
                    out_refs[h // per][:, :, to : to + TILE] = wave[:, :, (h - g) * TILE : (h - g + 1) * TILE]


def mix(moved, weights, so_far, at, count, chunks, t):
    first, last = not so_far, at + count == GROUPS
    tables = (t["xfh"], t["xfl"], t["spread"], t["xi"])
    hat = jax.ShapeDtypeStruct((2 * KX, CH * PAIRS), F32)
    acc = jax.ShapeDtypeStruct((2, PAIRS, MODES_O), F32)
    outs = [moved_shape(n) for n in chunks] if last else [acc]
    scratch = [pltpu.VMEM(acc.shape, F32), pltpu.VMEM((2 * MODES_O, TILE), F32)] if last else []
    before = [] if first else [whole(acc), pl.BlockSpec(memory_space=pl.ANY)]
    return call(
        functools.partial(mix_body, first, last, count // PER),
        5,
        (count // PER,),
        [moved_block(PER), weight_block(at)] + [whole(a) for a in tables] + before,
        [hat_block(at)] + [whole(a) for a in outs],
        [hat] + outs,
        scratch,
        aliases={} if first else {7: 0},
    )(moved, weights, *tables, *so_far)


def input_body(first, moved_refs, g_ref, w_ref, xfh_ref, xfl_ref, gather_ref, xi_ref, out_ref, turn_s):
    if first:

        @pl.when(pl.program_id(0) == 0)
        def _():
            lanes = lax.broadcasted_iota(jnp.int32, (KX, TILE), 1) // PAIRS
            per = GROUPS // len(moved_refs)
            for h in range(GROUPS):
                at = (h % per) * TILE
                tile = moved_refs[h // per][:, :, at : at + TILE].reshape(2 * GX, TILE)
                hat = x_forward(tile, xfh_ref[...], xfl_ref[...])
                for part in range(2):
                    rows = hat[part * KX : (part + 1) * KX]
                    for q in range(QUAD):
                        to = pl.ds(part * MODES_O + h * QUAD + q, KX, stride=CH)
                        turn_s[to, :] = jnp.where(lanes == q, rows, 0.0)
            for part in range(2):
                for k in range(MODES_O // TILE):
                    turned = turn_s[pl.ds(part * MODES_O + k * TILE, TILE), :].T
                    total = turned[:PAIRS]
                    for q in range(1, QUAD):
                        total = total + turned[q * PAIRS : (q + 1) * PAIRS]
                    g_ref[part, :, k * TILE : (k + 1) * TILE] = total

    g_re, g_im = g_ref[0], g_ref[1]
    rows_high, rows_low = [], []
    for c in range(PER * QUAD):
        w_re, w_im = w_ref[0, c], w_ref[1, c]
        full = jnp.concatenate([g_re * w_re + g_im * w_im, g_im * w_re - g_re * w_im], axis=1)
        high, low = halves(full)
        rows_high.append(high)
        rows_low.append(low)
    both = dot(jnp.concatenate(rows_high + rows_low, axis=0), gather_ref[...])
    both = both[: PER * TILE] + both[PER * TILE :]
    spec = jnp.concatenate([both[u * TILE : (u + 1) * TILE].T[: 2 * KX] for u in range(PER)], axis=1)
    out_ref[...] = x_inverse(spec, xi_ref[...]).reshape(PEERS, 2 * PLANES, PER * TILE)


def input_modes(moved, grad, weights, at, count, t):
    tables = (t["xfh"], t["xfl"], t["gather"], t["xi"])
    shape = jax.ShapeDtypeStruct((2, PAIRS, MODES_O), F32)
    first = grad is None
    if first:

        def body(*refs):
            n = len(moved)
            w, xfh, xfl, gather, xi, g, out, turn = refs[n:]
            input_body(True, refs[:n], g, w, xfh, xfl, gather, xi, out, turn)

        return call(
            body,
            7,
            (count // PER,),
            [whole(a) for a in moved] + [weight_block(at)] + [whole(a) for a in tables],
            [whole(shape), moved_block(PER)],
            [shape, moved_shape(count)],
            [pltpu.VMEM((2 * MODES_O, TILE), F32)],
        )(*moved, weights, *tables)

    def body(g, w, xfh, xfl, gather, xi, out):
        input_body(False, None, g, w, xfh, xfl, gather, xi, out, None)

    out = call(
        body,
        6,
        (count // PER,),
        [whole(shape), weight_block(at)] + [whole(a) for a in tables],
        moved_block(PER),
        moved_shape(count),
        [],
    )(grad, weights, *tables)
    return grad, out


def weight_grad_body(hat_ref, far_hat_ref, g_ref, far_g_ref, spread_ref, *refs):
    out_ref = refs[-1]
    spread = spread_ref[...]
    for u in range(PER):
        lanes = slice(u * TILE, (u + 1) * TILE)
        near = spread_modes(hat_ref[:, lanes], spread)
        far = spread_modes(far_hat_ref[:, lanes], spread)
        for q in range(QUAD):
            rows = slice(q * PAIRS, (q + 1) * PAIRS)
            n_re, n_im = near[rows, :MODES_O], near[rows, MODES_O:]
            f_re, f_im = far[rows, :MODES_O], far[rows, MODES_O:]
            c = u * QUAD + q
            out_ref[0, c] = n_re * g_ref[0] + n_im * g_ref[1] + f_re * far_g_ref[0] + f_im * far_g_ref[1]
            out_ref[1, c] = n_re * g_ref[1] - n_im * g_ref[0] + f_re * far_g_ref[1] - f_im * far_g_ref[0]


def weight_grad(hat, far_hat, grad, far_grad, at, count, so_far, t):
    return call(
        weight_grad_body,
        count,
        (count // PER,),
        [hat_block(at), hat_block(at), whole(grad), whole(far_grad), whole(t["spread"])]
        + [pl.BlockSpec(memory_space=pl.ANY)] * len(so_far),
        weight_block(at),
        jax.ShapeDtypeStruct((2, CH, PAIRS, MODES_O), F32),
        [],
        aliases={5 + i: i for i in range(len(so_far))},
    )(hat, far_hat, grad, far_grad, t["spread"], *so_far)


def gelu_parts(pre):
    bell = jnp.exp2(pre * pre * (-0.5 * math.log2(math.e)))
    rate = 0.3275911 * math.sqrt(0.5)
    t = 1.0 / (jnp.abs(pre) + 1.0 / rate)
    poly = 1.061405429 * 0.5 / rate**5
    for power, coefficient in zip((4, 3, 2, 1), (-1.453152027, 1.421413741, -0.284496736, 0.254829592)):
        poly = poly * t + coefficient * 0.5 / rate**power
    tail = poly * t * bell
    share = jnp.where(pre >= 0.0, 1.0 - tail, tail)
    return share, pre * bell * (1.0 / math.sqrt(2.0 * math.pi))


def arrive(arrived_ref, zih, zil):
    parts = []
    for part in range(2):
        block = arrived_ref[:, part * PLANES : (part + 1) * PLANES, :]
        parts.append(jnp.swapaxes(block, 0, 1).reshape(PLANES * KYH, TILE))
    high, low = halves(jnp.concatenate(parts, axis=1))
    return halves(dot3(high, low, zih, zil))


def inverse_pair(high, low, x, half, yi):
    stacks = []
    for source in (high, low):
        sides = []
        for j in range(2):
            lanes = (2 * half + j) * 2 * KYL * GZ
            pieces = [
                source[x * KYH : (x + 1) * KYH, lanes + k * GZ : lanes + (k + 1) * GZ] for k in range(2 * KYL)
            ]
            sides.append(jnp.concatenate(pieces, axis=0))
        stacks.append(jnp.concatenate(sides, axis=1))
    return dot(yi, jnp.concatenate([stacks[0], stacks[1], stacks[0]], axis=0))


def kron_halves(matrix, rep):
    rows = lax.broadcasted_iota(jnp.int32, (8 * CH, 8 * CH), 0) % 8
    lanes = lax.broadcasted_iota(jnp.int32, (8 * CH, 8 * CH), 1) % 8
    wide = []
    for half in halves(matrix):
        tall = dot(rep, half).astype(BF)
        full = lax.dot_general(tall, rep, (((1,), (1,)), ((), ())), preferred_element_type=F32)
        wide.append(jnp.where(rows == lanes, full, 0.0).astype(BF))
    return jnp.concatenate(wide, axis=0)


def channel_sum_body(data_ref, matrix_ref, rep_ref, *refs):
    out_ref, kron_s = refs[-2:]

    @pl.when(pl.program_id(0) == 0)
    def _():
        kron_s[...] = kron_halves(matrix_ref[...], rep_ref[...])

    for x in range(data_ref.shape[1]):
        for i in range(GY // 16):
            tiles = [data_ref[:, x, i * 16 + 8 * j : i * 16 + 8 * j + 8, :].reshape(8 * CH, GZ) for j in range(2)]
            high, low = halves(jnp.concatenate(tiles, axis=1))
            both = dot(kron_s[...], high)
            sums = both[: 8 * CH] + both[8 * CH :] + dot(kron_s[: 8 * CH], low)
            for j in range(2):
                at = slice(i * 16 + 8 * j, i * 16 + 8 * j + 8)
                out_ref[:, x, at, :] = sums[:, j * GZ : (j + 1) * GZ].reshape(CH, 8, GZ)


def channel_sum(data, matrix, first, count, step, so_far, t):
    block = pl.BlockSpec((CH, step, GY, GZ), lambda x: (0, x + first // step, 0, 0))
    return call(
        channel_sum_body,
        2 * count,
        (count // step,),
        [block, whole(matrix), whole(t["rep"])] + [pl.BlockSpec(memory_space=pl.ANY)] * len(so_far),
        block,
        jax.ShapeDtypeStruct(data.shape, F32),
        [pltpu.VMEM((16 * CH, 8 * CH), BF)],
        aliases={3 + i: i for i in range(len(so_far))},
    )(data, matrix, t["rep"], *so_far)


def middle_body(
    arrived_ref, sum_ref, cot_ref, yi_ref, zih_ref, zil_ref, yf_ref, zg_ref, *refs
):
    out_ref, grad_ref, spec_ref, high_s, low_s = refs[-5:]
    high, low = arrive(arrived_ref, zih_ref[...], zil_ref[...])
    yi, yf = yi_ref[...], yf_ref[...]
    for x in range(PLANES):
        for half in range(2):
            waves = inverse_pair(high, low, x, half, yi)
            grads = []
            for j in range(2):
                c = 2 * half + j
                pre = waves[:, j * GZ : (j + 1) * GZ] + sum_ref[c, x]
                share, slope = gelu_parts(pre)
                out_ref[c, x] = pre * share
                grad = cot_ref[c, x] * (share + slope)
                grad_ref[c, x] = grad
                grads.append(grad)
            store_modes(*lines_to_modes(jnp.concatenate(grads, axis=1), yf), x, half, high_s, low_s)
    send_modes(high_s, low_s, zg_ref, spec_ref)


def middle(arrived, sums, cotangent, first, count, so_far, t):
    tables = (t["yi"], t["zih"], t["zil"], t["yf"], t["zg"])
    block = channel_block(first)
    shape = jax.ShapeDtypeStruct(sums.shape, F32)
    n = 3 + len(tables)
    return call(
        middle_body,
        5 * count,
        (count,),
        [moved_block(), block, block] + [whole(a) for a in tables] + [pl.BlockSpec(memory_space=pl.ANY)] * len(so_far),
        [block, block, moved_block()],
        [shape, shape, moved_shape(count)],
        mode_scratch(),
        aliases={n + i: i for i in range(len(so_far))},
    )(arrived, sums, cotangent, *tables, *so_far)


def last_body(arrived_ref, sum_ref, yi_ref, zjh_ref, zjl_ref, *refs):
    out_ref = refs[-1]
    high, low = arrive(arrived_ref, zjh_ref[...], zjl_ref[...])
    yi = yi_ref[...]
    for x in range(PLANES):
        for half in range(2):
            waves = inverse_pair(high, low, x, half, yi)
            for j in range(2):
                c = 2 * half + j
                out_ref[c, x] = waves[:, j * GZ : (j + 1) * GZ] + sum_ref[c, x]


def last(arrived, sums, first, count, so_far, t):
    tables = (t["yi"], t["zjh"], t["zjl"])
    block = channel_block(first)
    n = 2 + len(tables)
    return call(
        last_body,
        2.5 * count,
        (count,),
        [moved_block(), block] + [whole(a) for a in tables] + [pl.BlockSpec(memory_space=pl.ANY)] * len(so_far),
        block,
        jax.ShapeDtypeStruct(sums.shape, F32),
        [],
        aliases={n + i: i for i in range(len(so_far))},
    )(arrived, sums, *tables, *so_far)


def swap_slabs(array):
    return lax.all_to_all(array, "slab", split_axis=0, concat_axis=0, tiled=True)


CHUNKS = (4, 4)
STARTS = tuple(sum(CHUNKS[:k]) for k in range(len(CHUNKS)))


def on_device(field, cotangent, spec_weight, bypass_weight):
    shape = (field.shape[1], field.shape[2], spec_weight.shape[2], lax.axis_size("slab"), lax.axis_size("dp"))
    if shape != (CH, PLANES, PAIRS, PEERS, 2):
        return on_device_any(field, cotangent, spec_weight, bypass_weight)
    t = {name: jnp.asarray(table) for name, table in host_tables().items()}
    source, other = field[0], cotangent[0]
    swap_pair = [(0, 1), (1, 0)]
    parts = list(zip(STARTS, CHUNKS))
    ahead = lax.optimization_barrier

    turned = bypass_weight.T
    moved, sums = [], ()
    for at, n in parts:
        sent = spectrum(source, at, n, t)
        if moved:
            sums = (channel_sum(source, turned, 0, 2, 1, (), t),)
            moved[-1], sent, *sums = ahead((moved[-1], sent, *sums))
        moved.append(swap_slabs(sent))
    sums = (channel_sum(source, turned, 2, 4, 1, tuple(sums), t),)
    moved[-1], *sums = ahead((moved[-1], *sums))
    hat, state = None, ()
    for arrived, (at, n) in zip(moved, parts):
        hat, *state = mix(arrived, spec_weight, (*state, hat) if state else (), at, n, CHUNKS, t)
    far_hat = lax.ppermute(hat, "dp", swap_pair)
    sums = channel_sum(source, turned, 6, 2, 1, tuple(sums), t)
    so_far, cot_moved, arrived = (), [], []
    for sent in state:
        if arrived:
            arrived[-1], sums, sent = ahead((arrived[-1], sums, sent))
        arrived.append(swap_slabs(sent))
    for k, (at, n) in enumerate(parts):
        *so_far, sent = middle(arrived[k], sums, other, at, n, so_far, t)
        if k == 0:
            arrived[-1], sent = ahead((arrived[-1], sent))
        else:
            cot_moved[-1], sent = ahead((cot_moved[-1], sent))
        cot_moved.append(swap_slabs(sent))
    result, grad_pre = so_far
    back_sums = channel_sum(grad_pre, bypass_weight, 0, 6, 2, (), t)
    cot_moved[-1], back_sums, far_hat = ahead((cot_moved[-1], back_sums, far_hat))
    grad, back_arrived = None, []
    for at, n in parts:
        grad, sent = input_modes(cot_moved, grad, spec_weight, at, n, t)
        if back_arrived:
            back_sums = channel_sum(grad_pre, bypass_weight, 6, 2, 1, (back_sums,), t)
            back_arrived[-1], sent, back_sums = ahead((back_arrived[-1], sent, back_sums))
        else:
            far_grad = lax.ppermute(grad, "dp", swap_pair)
        back_arrived.append(swap_slabs(sent))
    grad_spec = weight_grad(hat, far_hat, grad, far_grad, 0, GROUPS, (), t)
    back = ()
    for k, (at, n) in enumerate(parts):
        if k == 1:
            back_arrived[k], back, grad_spec = ahead((back_arrived[k], back, grad_spec))
        back = (last(back_arrived[k], back_sums, at, n, back, t),)
    return (result[None], back[0][None], grad_spec)


def solution(mesh):
    in_specs = (
        P("dp", None, "slab", None, None),
        P("dp", None, "slab", None, None),
        P(None, None, "slab", None),
        P(),
    )
    out_specs = (
        P("dp", None, "slab", None, None),
        P("dp", None, "slab", None, None),
        P(None, None, "slab", None),
    )
    return jax.shard_map(
        on_device, mesh=mesh, in_specs=in_specs, out_specs=out_specs, check_vma=False
    )
```

```python
import functools
import math

import jax
import jax.numpy as jnp
import ml_dtypes
import numpy as np
from jax import lax
from jax.experimental import pallas as pl
from jax.experimental.pallas import tpu as pltpu
from jax.sharding import PartitionSpec as P

GX = 128
GY = 128
GZ = 128
KX = 32
KY = 32
KZ = 16


precise = lax.Precision.HIGHEST


def wave_tables(length, count, signed):
    positions = jnp.arange(length, dtype=jnp.int32)
    indices = jnp.arange(count, dtype=jnp.int32)
    if signed:
        freqs = jnp.where(indices < count // 2, indices, indices - count)
    else:
        freqs = indices
    phase = positions[:, None] * freqs[None, :] % length
    angle = phase.astype(jnp.float32) * (2.0 * math.pi / length)
    return (jnp.cos(angle), jnp.sin(angle))


def gelu_exact(values):
    return jax.nn.gelu(values, approximate=False)


def plane_spectrum(data, weight, z_cos, z_sin, y_cos, y_sin):
    chans, planes = (data.shape[0], data.shape[1])
    part_re = jnp.einsum("cxyz,zk->cxky", data, z_cos, precision=precise)
    part_im = -jnp.einsum("cxyz,zk->cxky", data, z_sin, precision=precise)
    mid_re = jnp.einsum("cxky,yj->cxjk", part_re, y_cos, precision=precise) + jnp.einsum(
        "cxky,yj->cxjk", part_im, y_sin, precision=precise
    )
    mid_im = jnp.einsum("cxky,yj->cxjk", part_im, y_cos, precision=precise) - jnp.einsum(
        "cxky,yj->cxjk", part_re, y_sin, precision=precise
    )
    stacked = jnp.stack([mid_re * weight, mid_im * weight])
    return stacked.reshape(2, chans, planes, KY * KZ)


def along_first(moved, x_cos, x_sin):
    line_re, line_im = (moved[0], moved[1])
    full_re = jnp.einsum("cxp,xi->cpi", line_re, x_cos, precision=precise) + jnp.einsum(
        "cxp,xi->cpi", line_im, x_sin, precision=precise
    )
    full_im = jnp.einsum("cxp,xi->cpi", line_im, x_cos, precision=precise) - jnp.einsum(
        "cxp,xi->cpi", line_re, x_sin, precision=precise
    )
    return (full_re, full_im)


def back_first(spec_re, spec_im, x_cos, x_sin):
    wide_re = jnp.einsum("cpi,xi->cxp", spec_re, x_cos, precision=precise) - jnp.einsum(
        "cpi,xi->cxp", spec_im, x_sin, precision=precise
    )
    wide_im = jnp.einsum("cpi,xi->cxp", spec_re, x_sin, precision=precise) + jnp.einsum(
        "cpi,xi->cxp", spec_im, x_cos, precision=precise
    )
    return jnp.stack([wide_re, wide_im])


def plane_inverse(arrived, weight, z_cos, z_sin, y_cos, y_sin):
    chans, planes = (arrived.shape[1], arrived.shape[2])
    shaped = arrived.reshape(2, chans, planes, KY, KZ)
    wide_re, wide_im = (shaped[0], shaped[1])
    plane_re = jnp.einsum("cxjk,yj->cxky", wide_re, y_cos, precision=precise) - jnp.einsum(
        "cxjk,yj->cxky", wide_im, y_sin, precision=precise
    )
    plane_im = jnp.einsum("cxjk,yj->cxky", wide_re, y_sin, precision=precise) + jnp.einsum(
        "cxjk,yj->cxky", wide_im, y_cos, precision=precise
    )
    plane_re = plane_re * weight[:, None]
    plane_im = plane_im * weight[:, None]
    return jnp.einsum("cxky,zk->cxyz", plane_re, z_cos, precision=precise) - jnp.einsum(
        "cxky,zk->cxyz", plane_im, z_sin, precision=precise
    )


def on_device_any(field, cotangent, spec_weight, bypass_weight):
    count = lax.axis_size("slab")
    pairs = KY * KZ // count
    chans = field.shape[1]
    z_cos, z_sin = wave_tables(GZ, KZ, False)
    y_cos, y_sin = wave_tables(GY, KY, True)
    x_cos, x_sin = wave_tables(GX, KX, True)
    kz_index = jnp.arange(KZ, dtype=jnp.int32)
    fold = jnp.where(kz_index == 0, 1.0, 2.0).astype(jnp.float32) / float(GX * GY * GZ)
    ones = jnp.ones((KZ,), jnp.float32)
    weights = spec_weight.reshape(2, chans, pairs, KX, chans)
    w_real = weights[0]
    w_imag = weights[1]
    source = field[0]
    local_spec = plane_spectrum(source, ones, z_cos, z_sin, y_cos, y_sin)
    moved = lax.all_to_all(local_spec, "slab", split_axis=3, concat_axis=2, tiled=True)
    hat_re, hat_im = along_first(moved, x_cos, x_sin)
    mix_re = jnp.einsum("cpi,cpio->opi", hat_re, w_real, precision=precise) - jnp.einsum(
        "cpi,cpio->opi", hat_im, w_imag, precision=precise
    )
    mix_im = jnp.einsum("cpi,cpio->opi", hat_re, w_imag, precision=precise) + jnp.einsum(
        "cpi,cpio->opi", hat_im, w_real, precision=precise
    )
    outgoing = back_first(mix_re, mix_im, x_cos, x_sin)
    arrived = lax.all_to_all(outgoing, "slab", split_axis=2, concat_axis=3, tiled=True)
    spectral = plane_inverse(arrived, fold, z_cos, z_sin, y_cos, y_sin)
    pre = spectral + jnp.einsum("co,cxyz->oxyz", bypass_weight, source, precision=precise)
    result, pullback = jax.vjp(gelu_exact, pre)
    grad_pre = pullback(cotangent[0])[0]
    fold_grid = jnp.broadcast_to(fold, (KY, KZ))
    cot_spec = plane_spectrum(grad_pre, fold_grid, z_cos, z_sin, y_cos, y_sin)
    cot_moved = lax.all_to_all(cot_spec, "slab", split_axis=3, concat_axis=2, tiled=True)
    grad_re, grad_im = along_first(cot_moved, x_cos, x_sin)
    own_real = jnp.einsum("cpi,opi->cpio", hat_re, grad_re, precision=precise) + jnp.einsum(
        "cpi,opi->cpio", hat_im, grad_im, precision=precise
    )
    own_imag = jnp.einsum("cpi,opi->cpio", hat_re, grad_im, precision=precise) - jnp.einsum(
        "cpi,opi->cpio", hat_im, grad_re, precision=precise
    )
    summed = lax.psum(jnp.stack([own_real, own_imag]), "dp")
    grad_spec = summed.reshape(2, chans, pairs, KX * chans)
    input_re = jnp.einsum("opi,cpio->cpi", grad_re, w_real, precision=precise) + jnp.einsum(
        "opi,cpio->cpi", grad_im, w_imag, precision=precise
    )
    input_im = jnp.einsum("opi,cpio->cpi", grad_im, w_real, precision=precise) - jnp.einsum(
        "opi,cpio->cpi", grad_re, w_imag, precision=precise
    )
    grad_out = back_first(input_re, input_im, x_cos, x_sin)
    grad_arrived = lax.all_to_all(grad_out, "slab", split_axis=2, concat_axis=3, tiled=True)
    back_field = plane_inverse(grad_arrived, ones, z_cos, z_sin, y_cos, y_sin)
    back_field = back_field + jnp.einsum(
        "co,oxyz->cxyz", bypass_weight, grad_pre, precision=precise
    )
    return (result[None], back_field[None], grad_spec)


CH = 32
PLANES = 8
PAIRS = 32
PEERS = 16
KYL = PAIRS // KZ
KYH = KY // KYL
QUAD = 4
GROUPS = CH // QUAD
TILE = QUAD * PAIRS
PER = 2
BLOCKS = QUAD * KYL
WIDE = BLOCKS * 2 * GZ
ROWS = PLANES * KYH
MODES_O = KX * CH

VMEM = 52 * 1024 * 1024

BF = jnp.bfloat16
F32 = jnp.float32


def split_table(table):
    high = table.astype(ml_dtypes.bfloat16)
    low = (table - high.astype(np.float64)).astype(ml_dtypes.bfloat16)
    return high, low


def phases(length, count, signed):
    freqs = np.arange(count)
    if signed:
        freqs = np.where(freqs < count // 2, freqs, freqs - count)
    phase = (np.arange(length)[:, None] * freqs[None, :]) % length
    angle = phase * (2.0 * np.pi / length)
    return np.cos(angle), np.sin(angle)


@functools.lru_cache(maxsize=None)
def host_tables():
    zc, zs = phases(GZ, KZ, False)
    yc, ys = phases(GY, KY, True)
    xc, xs = phases(GX, KX, True)
    fold = np.where(np.arange(KZ) == 0, 1.0, 2.0) / float(GX * GY * GZ)
    out = {}
    ycr = yc.T.reshape(KYH, KYL, GY).transpose(1, 0, 2)
    ysr = ys.T.reshape(KYH, KYL, GY).transpose(1, 0, 2)
    fwd = np.stack([ycr, -ysr], axis=1).reshape(2 * KY, GY)
    high, low = split_table(fwd)
    out["yf"] = np.block([[high, high], [low, low]])
    inv = np.stack([ycr, -ysr], axis=1).reshape(2 * KY, GY).T
    high, low = split_table(inv)
    out["yi"] = np.concatenate([high, high, low], axis=1)
    core = np.stack([np.stack([zc, -zs]), np.stack([zs, zc])])
    for name, scale in (("zf", np.ones(KZ)), ("zg", fold)):
        table = (core * scale).transpose(0, 2, 1, 3)[:, :, :, None, :]
        table = np.broadcast_to(table, (2, GZ, 2, BLOCKS, KZ))
        high, low = split_table(table.reshape(2 * GZ, 2 * TILE))
        out[name] = np.stack([high, low])
    core = np.stack([np.stack([zc, zs]), np.stack([-zs, zc])])
    for name, scale in (("zi", fold), ("zj", np.ones(KZ))):
        table = np.zeros((2, QUAD, KYL, KZ, QUAD, KYL, 2, GZ))
        for q in range(QUAD):
            for k in range(KYL):
                table[:, q, k, :, q, k, :, :] = (core * scale).transpose(0, 3, 1, 2)
        out[name + "h"], out[name + "l"] = split_table(table.reshape(2 * TILE, WIDE))
    core = np.stack([np.stack([xc, xs]), np.stack([-xs, xc])])
    table = core.reshape(2, 2, PEERS, PLANES, KX).transpose(0, 4, 2, 1, 3).reshape(2 * KX, 2 * GX)
    high, low = split_table(table)
    out["xfh"], out["xfl"] = high, low
    core = np.stack([np.stack([xc, -xs]), np.stack([xs, xc])])
    table = core.reshape(2, 2, PEERS, PLANES, KX).transpose(2, 0, 3, 1, 4).reshape(2 * GX, 2 * KX)
    high, low = split_table(table)
    out["xi"] = np.concatenate([high, high, low], axis=1)
    spread = np.repeat(np.eye(2 * KX), CH, axis=1).astype(ml_dtypes.bfloat16)
    out["spread"] = np.concatenate([spread, spread], axis=0)
    out["rep"] = np.repeat(np.eye(CH), 8, axis=0).astype(ml_dtypes.bfloat16)
    out["gather"] = np.concatenate([spread, spread], axis=0).T.copy()
    return out


def halves(values):
    high = values.astype(BF)
    return high, (values - high.astype(F32)).astype(BF)


def dot(left, right):
    return jnp.dot(left, right, preferred_element_type=F32)


def lines_to_modes(pair, yf):
    high, low = halves(pair)
    both = dot(yf, jnp.concatenate([high, low], axis=0))
    return halves(both[: 2 * KY] + both[2 * KY :])


def call(body, us, grid, ins, outs, shapes, scratch, aliases=None, vmem=VMEM):
    return pl.pallas_call(
        body,
        grid=grid,
        in_specs=ins,
        out_specs=outs,
        out_shape=shapes,
        scratch_shapes=scratch,
        input_output_aliases=aliases or {},
        cost_estimate=pl.CostEstimate(flops=int(us * 1e9), bytes_accessed=int(us * 3e6), transcendentals=0),
        compiler_params=pltpu.CompilerParams(
            dimension_semantics=("arbitrary",), vmem_limit_bytes=vmem
        ),
    )


def whole(array):
    zeros = (0,) * array.ndim
    return pl.BlockSpec(array.shape, lambda step: zeros)


def store_modes(high, low, x, half, high_s, low_s):
    for j in range(2):
        for k in range(KYL):
            to = ((2 * half + j) * KYL + k) * ROWS + x * KYH
            for part in range(2):
                rows = slice((2 * k + part) * KYH, (2 * k + part + 1) * KYH)
                take = (rows, slice(j * GZ, (j + 1) * GZ))
                put = (slice(to, to + KYH), slice(part * GZ, (part + 1) * GZ))
                high_s[put] = high[take]
                low_s[put] = low[take]


def send_modes(high_s, low_s, table_ref, out_ref):
    high, low = high_s[...], low_s[...]
    full = dot(high, table_ref[0]) + dot(low, table_ref[0]) + dot(high, table_ref[1])
    owner = lax.broadcasted_iota(jnp.int32, (ROWS, 2 * TILE), 1) % TILE // KZ
    sums = full[:ROWS]
    for i in range(1, BLOCKS):
        sums = jnp.where(owner == i, full[i * ROWS : (i + 1) * ROWS], sums)
    for part in range(2):
        block = sums[:, part * TILE : (part + 1) * TILE].reshape(PLANES, KYH, TILE)
        out_ref[:, part * PLANES : (part + 1) * PLANES, :] = jnp.swapaxes(block, 0, 1)


def spectrum_body(f_ref, yf_ref, table_ref, out_ref, high_s, low_s):
    yf = yf_ref[...]
    for x in range(PLANES):
        for half in range(2):
            pair = jnp.concatenate([f_ref[2 * half, x], f_ref[2 * half + 1, x]], axis=1)
            high, low = lines_to_modes(pair, yf)
            store_modes(high, low, x, half, high_s, low_s)
    send_modes(high_s, low_s, table_ref, out_ref)


def channel_block(first):
    return pl.BlockSpec((QUAD, PLANES, GY, GZ), lambda g: (g + first, 0, 0, 0))


def moved_block(per=1):
    return pl.BlockSpec((PEERS, 2 * PLANES, per * TILE), lambda g: (0, 0, g))


def weight_block(at):
    return pl.BlockSpec((2, PER * QUAD, PAIRS, MODES_O), lambda g: (0, g + at // PER, 0, 0))


def hat_block(at):
    return pl.BlockSpec((2 * KX, PER * TILE), lambda g: (0, g + at // PER))


def moved_shape(groups):
    return jax.ShapeDtypeStruct((PEERS, 2 * PLANES, groups * TILE), F32)


def mode_scratch():
    return [pltpu.VMEM((BLOCKS * ROWS, 2 * GZ), BF), pltpu.VMEM((BLOCKS * ROWS, 2 * GZ), BF)]


def spectrum(field, first, count, t):
    tables = (t["yf"], t["zf"])
    return call(
        spectrum_body,
        2 * count,
        (count,),
        [channel_block(first)] + [whole(a) for a in tables],
        moved_block(),
        moved_shape(count),
        mode_scratch(),
        vmem=58 * 1024 * 1024,
    )(field, *tables)


def own_mask():
    rows = lax.broadcasted_iota(jnp.int32, (TILE, TILE), 0) % QUAD
    lanes = lax.broadcasted_iota(jnp.int32, (TILE, TILE), 1) // PAIRS
    return rows == lanes


def x_forward(moved, xfh, xfl):
    high, low = halves(moved)
    both = dot(jnp.concatenate([xfh, xfl], axis=0), high)
    return both[: 2 * KX] + both[2 * KX :] + dot(xfh, low)


def x_inverse(spec, xi):
    high, low = halves(spec)
    return dot(xi, jnp.concatenate([high, low, high], axis=0))


def spread_modes(spec, spread):
    turned = jnp.concatenate([spec, spec], axis=0).T
    high, low = halves(turned)
    lanes = lax.broadcasted_iota(jnp.int32, (TILE, 4 * KX), 1)
    return dot(jnp.where(lanes < 2 * KX, high, low), spread)


def mix_body(first, last, count, *refs):
    moved_ref, w_ref, xfh_ref, xfl_ref, spread_ref, xi_ref = refs[:6]
    refs = refs[6:]
    if not first:
        start_ref, refs = refs[0], refs[2:]
    hat_ref, refs = refs[0], refs[1:]
    if last:
        out_refs, (acc_s, turn_s) = refs[:-2], refs[-2:]
    else:
        (acc_s,) = refs
    step = pl.program_id(0)

    @pl.when(step == 0)
    def _():
        acc_s[...] = jnp.zeros_like(acc_s) if first else start_ref[...]

    hat = x_forward(moved_ref[...].reshape(2 * GX, PER * TILE), xfh_ref[...], xfl_ref[...])
    hat_ref[...] = hat
    acc_re, acc_im = acc_s[0], acc_s[1]
    for u in range(PER):
        wide = spread_modes(hat[:, u * TILE : (u + 1) * TILE], spread_ref[...])
        for q in range(QUAD):
            h_re = wide[q * PAIRS : (q + 1) * PAIRS, :MODES_O]
            h_im = wide[q * PAIRS : (q + 1) * PAIRS, MODES_O:]
            w_re, w_im = w_ref[0, u * QUAD + q], w_ref[1, u * QUAD + q]
            acc_re = acc_re + (h_re * w_re - h_im * w_im)
            acc_im = acc_im + (h_re * w_im + h_im * w_re)
    acc_s[0] = acc_re
    acc_s[1] = acc_im

    if last:

        @pl.when(step == count - 1)
        def _():
            mask = own_mask()
            for part in range(2):
                full = jnp.concatenate([acc_s[part]] * QUAD, axis=0)
                for k in range(MODES_O // TILE):
                    turned = full[:, k * TILE : (k + 1) * TILE].T
                    turn_s[pl.ds(part * MODES_O + k * TILE, TILE), :] = jnp.where(mask, turned, 0.0)
            xi = xi_ref[...]
            per = GROUPS // len(out_refs)
            for g in range(0, GROUPS, 2):
                tiles = []
                for h in range(g, g + 2):
                    parts = []
                    for part in range(2):
                        total = None
                        for q in range(QUAD):
                            rows = turn_s[pl.ds(part * MODES_O + h * QUAD + q, KX, stride=CH), :]
                            total = rows if total is None else total + rows
                        parts.append(total)
                    tiles.append(jnp.concatenate(parts, axis=0))
                wave = x_inverse(jnp.concatenate(tiles, axis=1), xi).reshape(PEERS, 2 * PLANES, 2 * TILE)
                for h in range(g, g + 2):
                    to = (h % per) * TILE
                    out_refs[h // per][:, :, to : to + TILE] = wave[:, :, (h - g) * TILE : (h - g + 1) * TILE]


def mix(moved, weights, so_far, at, count, chunks, t):
    first, last = not so_far, at + count == GROUPS
    tables = (t["xfh"], t["xfl"], t["spread"], t["xi"])
    hat = jax.ShapeDtypeStruct((2 * KX, CH * PAIRS), F32)
    acc = jax.ShapeDtypeStruct((2, PAIRS, MODES_O), F32)
    outs = [moved_shape(n) for n in chunks] if last else [acc]
    scratch = [pltpu.VMEM(acc.shape, F32), pltpu.VMEM((2 * MODES_O, TILE), F32)] if last else []
    before = [] if first else [whole(acc), pl.BlockSpec(memory_space=pl.ANY)]
    return call(
        functools.partial(mix_body, first, last, count // PER),
        5,
        (count // PER,),
        [moved_block(PER), weight_block(at)] + [whole(a) for a in tables] + before,
        [hat_block(at)] + [whole(a) for a in outs],
        [hat] + outs,
        scratch,
        aliases={} if first else {7: 0},
        vmem=48 * 1024 * 1024,
    )(moved, weights, *tables, *so_far)


def input_body(first, moved_refs, g_ref, w_ref, xfh_ref, xfl_ref, gather_ref, xi_ref, out_ref, turn_s):
    if first:

        @pl.when(pl.program_id(0) == 0)
        def _():
            lanes = lax.broadcasted_iota(jnp.int32, (KX, TILE), 1) // PAIRS
            per = GROUPS // len(moved_refs)
            for h in range(GROUPS):
                at = (h % per) * TILE
                tile = moved_refs[h // per][:, :, at : at + TILE].reshape(2 * GX, TILE)
                hat = x_forward(tile, xfh_ref[...], xfl_ref[...])
                for part in range(2):
                    rows = hat[part * KX : (part + 1) * KX]
                    for q in range(QUAD):
                        to = pl.ds(part * MODES_O + h * QUAD + q, KX, stride=CH)
                        turn_s[to, :] = jnp.where(lanes == q, rows, 0.0)
            for part in range(2):
                for k in range(MODES_O // TILE):
                    turned = turn_s[pl.ds(part * MODES_O + k * TILE, TILE), :].T
                    total = turned[:PAIRS]
                    for q in range(1, QUAD):
                        total = total + turned[q * PAIRS : (q + 1) * PAIRS]
                    g_ref[part, :, k * TILE : (k + 1) * TILE] = total

    g_re, g_im = g_ref[0], g_ref[1]
    rows_high, rows_low = [], []
    for c in range(PER * QUAD):
        w_re, w_im = w_ref[0, c], w_ref[1, c]
        full = jnp.concatenate([g_re * w_re + g_im * w_im, g_im * w_re - g_re * w_im], axis=1)
        high, low = halves(full)
        rows_high.append(high)
        rows_low.append(low)
    both = dot(jnp.concatenate(rows_high + rows_low, axis=0), gather_ref[...])
    both = both[: PER * TILE] + both[PER * TILE :]
    spec = jnp.concatenate([both[u * TILE : (u + 1) * TILE].T[: 2 * KX] for u in range(PER)], axis=1)
    out_ref[...] = x_inverse(spec, xi_ref[...]).reshape(PEERS, 2 * PLANES, PER * TILE)


def input_modes(moved, grad, weights, at, count, t):
    tables = (t["xfh"], t["xfl"], t["gather"], t["xi"])
    shape = jax.ShapeDtypeStruct((2, PAIRS, MODES_O), F32)
    first = grad is None
    if first:

        def body(*refs):
            n = len(moved)
            w, xfh, xfl, gather, xi, g, out, turn = refs[n:]
            input_body(True, refs[:n], g, w, xfh, xfl, gather, xi, out, turn)

        return call(
            body,
            7,
            (count // PER,),
            [whole(a) for a in moved] + [weight_block(at)] + [whole(a) for a in tables],
            [whole(shape), moved_block(PER)],
            [shape, moved_shape(count)],
            [pltpu.VMEM((2 * MODES_O, TILE), F32)],
        )(*moved, weights, *tables)

    def body(g, w, xfh, xfl, gather, xi, out):
        input_body(False, None, g, w, xfh, xfl, gather, xi, out, None)

    out = call(
        body,
        6,
        (count // PER,),
        [whole(shape), weight_block(at)] + [whole(a) for a in tables],
        moved_block(PER),
        moved_shape(count),
        [],
    )(grad, weights, *tables)
    return grad, out


def weight_grad_body(hat_ref, far_hat_ref, g_ref, far_g_ref, spread_ref, *refs):
    out_ref = refs[-1]
    spread = spread_ref[...]
    for u in range(PER):
        lanes = slice(u * TILE, (u + 1) * TILE)
        near = spread_modes(hat_ref[:, lanes], spread)
        far = spread_modes(far_hat_ref[:, lanes], spread)
        for q in range(QUAD):
            rows = slice(q * PAIRS, (q + 1) * PAIRS)
            n_re, n_im = near[rows, :MODES_O], near[rows, MODES_O:]
            f_re, f_im = far[rows, :MODES_O], far[rows, MODES_O:]
            c = u * QUAD + q
            out_ref[0, c] = n_re * g_ref[0] + n_im * g_ref[1] + f_re * far_g_ref[0] + f_im * far_g_ref[1]
            out_ref[1, c] = n_re * g_ref[1] - n_im * g_ref[0] + f_re * far_g_ref[1] - f_im * far_g_ref[0]


def weight_grad(hat, far_hat, grad, far_grad, at, count, so_far, t):
    return call(
        weight_grad_body,
        count,
        (count // PER,),
        [hat_block(at), hat_block(at), whole(grad), whole(far_grad), whole(t["spread"])]
        + [pl.BlockSpec(memory_space=pl.ANY)] * len(so_far),
        weight_block(at),
        jax.ShapeDtypeStruct((2, CH, PAIRS, MODES_O), F32),
        [],
        aliases={5 + i: i for i in range(len(so_far))},
    )(hat, far_hat, grad, far_grad, t["spread"], *so_far)


def gelu_parts(pre):
    bell = jnp.exp2(pre * pre * (-0.5 * math.log2(math.e)))
    rate = 0.3275911 * math.sqrt(0.5)
    t = 1.0 / (jnp.abs(pre) + 1.0 / rate)
    poly = 1.061405429 * 0.5 / rate**5
    for power, coefficient in zip((4, 3, 2, 1), (-1.453152027, 1.421413741, -0.284496736, 0.254829592)):
        poly = poly * t + coefficient * 0.5 / rate**power
    tail = poly * t * bell
    share = jnp.where(pre >= 0.0, 1.0 - tail, tail)
    return share, pre * bell * (1.0 / math.sqrt(2.0 * math.pi))


def arrive(arrived_ref, zih, zil):
    parts = []
    for part in range(2):
        block = arrived_ref[:, part * PLANES : (part + 1) * PLANES, :]
        parts.append(jnp.swapaxes(block, 0, 1).reshape(PLANES * KYH, TILE))
    high, low = halves(jnp.concatenate(parts, axis=1))
    tables = jnp.concatenate([zih, zih, zil], axis=0)
    return halves(dot(jnp.concatenate([high, low, high], axis=1), tables))


def inverse_pair(high, low, x, half, yi):
    stacks = []
    for source in (high, low):
        sides = []
        for j in range(2):
            lanes = (2 * half + j) * 2 * KYL * GZ
            pieces = [
                source[x * KYH : (x + 1) * KYH, lanes + k * GZ : lanes + (k + 1) * GZ] for k in range(2 * KYL)
            ]
            sides.append(jnp.concatenate(pieces, axis=0))
        stacks.append(jnp.concatenate(sides, axis=1))
    return dot(yi, jnp.concatenate([stacks[0], stacks[1], stacks[0]], axis=0))


def kron_halves(matrix, rep):
    rows = lax.broadcasted_iota(jnp.int32, (8 * CH, 8 * CH), 0) % 8
    lanes = lax.broadcasted_iota(jnp.int32, (8 * CH, 8 * CH), 1) % 8
    wide = []
    for half in halves(matrix):
        tall = dot(rep, half).astype(BF)
        full = lax.dot_general(tall, rep, (((1,), (1,)), ((), ())), preferred_element_type=F32)
        wide.append(jnp.where(rows == lanes, full, 0.0).astype(BF))
    return jnp.concatenate(wide, axis=0)


def channel_sum_body(data_ref, matrix_ref, rep_ref, *refs):
    out_ref, kron_s = refs[-2:]

    @pl.when(pl.program_id(0) == 0)
    def _():
        kron_s[...] = kron_halves(matrix_ref[...], rep_ref[...])

    for x in range(data_ref.shape[1]):
        for i in range(GY // 16):
            tiles = [data_ref[:, x, i * 16 + 8 * j : i * 16 + 8 * j + 8, :].reshape(8 * CH, GZ) for j in range(2)]
            high, low = halves(jnp.concatenate(tiles, axis=1))
            both = dot(kron_s[...], high)
            sums = both[: 8 * CH] + both[8 * CH :] + dot(kron_s[: 8 * CH], low)
            for j in range(2):
                at = slice(i * 16 + 8 * j, i * 16 + 8 * j + 8)
                out_ref[:, x, at, :] = sums[:, j * GZ : (j + 1) * GZ].reshape(CH, 8, GZ)


def channel_sum(data, matrix, first, count, step, so_far, t):
    block = pl.BlockSpec((CH, step, GY, GZ), lambda x: (0, x + first // step, 0, 0))
    return call(
        channel_sum_body,
        2 * count,
        (count // step,),
        [block, whole(matrix), whole(t["rep"])] + [pl.BlockSpec(memory_space=pl.ANY)] * len(so_far),
        block,
        jax.ShapeDtypeStruct(data.shape, F32),
        [pltpu.VMEM((16 * CH, 8 * CH), BF)],
        aliases={3 + i: i for i in range(len(so_far))},
    )(data, matrix, t["rep"], *so_far)


def middle_body(
    arrived_ref, sum_ref, cot_ref, yi_ref, zih_ref, zil_ref, yf_ref, zg_ref, *refs
):
    out_ref, grad_ref, spec_ref, high_s, low_s = refs[-5:]
    high, low = arrive(arrived_ref, zih_ref[...], zil_ref[...])
    yi, yf = yi_ref[...], yf_ref[...]
    for x in range(PLANES):
        for half in range(2):
            waves = inverse_pair(high, low, x, half, yi)
            grads = []
            for j in range(2):
                c = 2 * half + j
                pre = waves[:, j * GZ : (j + 1) * GZ] + sum_ref[c, x]
                share, slope = gelu_parts(pre)
                out_ref[c, x] = pre * share
                grad = cot_ref[c, x] * (share + slope)
                grad_ref[c, x] = grad
                grads.append(grad)
            store_modes(*lines_to_modes(jnp.concatenate(grads, axis=1), yf), x, half, high_s, low_s)
    send_modes(high_s, low_s, zg_ref, spec_ref)


def middle(arrived, sums, cotangent, first, count, so_far, t):
    tables = (t["yi"], t["zih"], t["zil"], t["yf"], t["zg"])
    block = channel_block(first)
    shape = jax.ShapeDtypeStruct(sums.shape, F32)
    n = 3 + len(tables)
    return call(
        middle_body,
        5 * count,
        (count,),
        [moved_block(), block, block] + [whole(a) for a in tables] + [pl.BlockSpec(memory_space=pl.ANY)] * len(so_far),
        [block, block, moved_block()],
        [shape, shape, moved_shape(count)],
        mode_scratch(),
        aliases={n + i: i for i in range(len(so_far))},
    )(arrived, sums, cotangent, *tables, *so_far)


def last_body(arrived_ref, sum_ref, yi_ref, zjh_ref, zjl_ref, *refs):
    out_ref = refs[-1]
    high, low = arrive(arrived_ref, zjh_ref[...], zjl_ref[...])
    yi = yi_ref[...]
    for x in range(PLANES):
        for half in range(2):
            waves = inverse_pair(high, low, x, half, yi)
            for j in range(2):
                c = 2 * half + j
                out_ref[c, x] = waves[:, j * GZ : (j + 1) * GZ] + sum_ref[c, x]


def last(arrived, sums, first, count, so_far, t):
    tables = (t["yi"], t["zjh"], t["zjl"])
    block = channel_block(first)
    n = 2 + len(tables)
    return call(
        last_body,
        2.5 * count,
        (count,),
        [moved_block(), block] + [whole(a) for a in tables] + [pl.BlockSpec(memory_space=pl.ANY)] * len(so_far),
        block,
        jax.ShapeDtypeStruct(sums.shape, F32),
        [],
        aliases={n + i: i for i in range(len(so_far))},
    )(arrived, sums, *tables, *so_far)


def swap_slabs(array):
    return lax.all_to_all(array, "slab", split_axis=0, concat_axis=0, tiled=True)


CHUNKS = (4, 4)
STARTS = tuple(sum(CHUNKS[:k]) for k in range(len(CHUNKS)))


def on_device(field, cotangent, spec_weight, bypass_weight):
    shape = (field.shape[1], field.shape[2], spec_weight.shape[2], lax.axis_size("slab"), lax.axis_size("dp"))
    if shape != (CH, PLANES, PAIRS, PEERS, 2):
        return on_device_any(field, cotangent, spec_weight, bypass_weight)
    t = {name: jnp.asarray(table) for name, table in host_tables().items()}
    source, other = field[0], cotangent[0]
    swap_pair = [(0, 1), (1, 0)]
    parts = list(zip(STARTS, CHUNKS))
    ahead = lax.optimization_barrier

    turned = bypass_weight.T
    moved, sums = [], ()
    for at, n in parts:
        sent = spectrum(source, at, n, t)
        if moved:
            sums = (channel_sum(source, turned, 0, 2, 1, (), t),)
            moved[-1], sent, *sums = ahead((moved[-1], sent, *sums))
        moved.append(swap_slabs(sent))
    sums = (channel_sum(source, turned, 2, 4, 1, tuple(sums), t),)
    moved[-1], *sums = ahead((moved[-1], *sums))
    hat, state = None, ()
    for arrived, (at, n) in zip(moved, parts):
        hat, *state = mix(arrived, spec_weight, (*state, hat) if state else (), at, n, CHUNKS, t)
    far_hat = lax.ppermute(hat, "dp", swap_pair)
    sums = channel_sum(source, turned, 6, 2, 1, tuple(sums), t)
    so_far, cot_moved, arrived = (), [], []
    for sent in state:
        if arrived:
            arrived[-1], sums, sent = ahead((arrived[-1], sums, sent))
        arrived.append(swap_slabs(sent))
    for k, (at, n) in enumerate(parts):
        *so_far, sent = middle(arrived[k], sums, other, at, n, so_far, t)
        if k == 0:
            arrived[-1], sent = ahead((arrived[-1], sent))
        else:
            cot_moved[-1], sent = ahead((cot_moved[-1], sent))
        cot_moved.append(swap_slabs(sent))
    result, grad_pre = so_far
    back_sums = channel_sum(grad_pre, bypass_weight, 0, 6, 2, (), t)
    cot_moved[-1], back_sums, far_hat = ahead((cot_moved[-1], back_sums, far_hat))
    grad, back_arrived = None, []
    for at, n in parts:
        grad, sent = input_modes(cot_moved, grad, spec_weight, at, n, t)
        if back_arrived:
            back_sums = channel_sum(grad_pre, bypass_weight, 6, 2, 1, (back_sums,), t)
            back_arrived[-1], sent, back_sums = ahead((back_arrived[-1], sent, back_sums))
        else:
            far_grad = lax.ppermute(grad, "dp", swap_pair)
        back_arrived.append(swap_slabs(sent))
    grad_spec = weight_grad(hat, far_hat, grad, far_grad, 0, GROUPS, (), t)
    back = ()
    for k, (at, n) in enumerate(parts):
        if k == 1:
            back_arrived[k], back, grad_spec = ahead((back_arrived[k], back, grad_spec))
        back = (last(back_arrived[k], back_sums, at, n, back, t),)
    return (result[None], back[0][None], grad_spec)


def solution(mesh):
    in_specs = (
        P("dp", None, "slab", None, None),
        P("dp", None, "slab", None, None),
        P(None, None, "slab", None),
        P(),
    )
    out_specs = (
        P("dp", None, "slab", None, None),
        P("dp", None, "slab", None, None),
        P(None, None, "slab", None),
    )
    return jax.shard_map(
        on_device, mesh=mesh, in_specs=in_specs, out_specs=out_specs, check_vma=False
    )
```

```python
import functools
import math

import jax
import jax.numpy as jnp
import ml_dtypes
import numpy as np
from jax import lax
from jax.experimental import pallas as pl
from jax.experimental.pallas import tpu as pltpu
from jax.sharding import PartitionSpec as P

GX = 128
GY = 128
GZ = 128
KX = 32
KY = 32
KZ = 16


precise = lax.Precision.HIGHEST


def wave_tables(length, count, signed):
    positions = jnp.arange(length, dtype=jnp.int32)
    indices = jnp.arange(count, dtype=jnp.int32)
    if signed:
        freqs = jnp.where(indices < count // 2, indices, indices - count)
    else:
        freqs = indices
    phase = positions[:, None] * freqs[None, :] % length
    angle = phase.astype(jnp.float32) * (2.0 * math.pi / length)
    return (jnp.cos(angle), jnp.sin(angle))


def gelu_exact(values):
    return jax.nn.gelu(values, approximate=False)


def plane_spectrum(data, weight, z_cos, z_sin, y_cos, y_sin):
    chans, planes = (data.shape[0], data.shape[1])
    part_re = jnp.einsum("cxyz,zk->cxky", data, z_cos, precision=precise)
    part_im = -jnp.einsum("cxyz,zk->cxky", data, z_sin, precision=precise)
    mid_re = jnp.einsum("cxky,yj->cxjk", part_re, y_cos, precision=precise) + jnp.einsum(
        "cxky,yj->cxjk", part_im, y_sin, precision=precise
    )
    mid_im = jnp.einsum("cxky,yj->cxjk", part_im, y_cos, precision=precise) - jnp.einsum(
        "cxky,yj->cxjk", part_re, y_sin, precision=precise
    )
    stacked = jnp.stack([mid_re * weight, mid_im * weight])
    return stacked.reshape(2, chans, planes, KY * KZ)


def along_first(moved, x_cos, x_sin):
    line_re, line_im = (moved[0], moved[1])
    full_re = jnp.einsum("cxp,xi->cpi", line_re, x_cos, precision=precise) + jnp.einsum(
        "cxp,xi->cpi", line_im, x_sin, precision=precise
    )
    full_im = jnp.einsum("cxp,xi->cpi", line_im, x_cos, precision=precise) - jnp.einsum(
        "cxp,xi->cpi", line_re, x_sin, precision=precise
    )
    return (full_re, full_im)


def back_first(spec_re, spec_im, x_cos, x_sin):
    wide_re = jnp.einsum("cpi,xi->cxp", spec_re, x_cos, precision=precise) - jnp.einsum(
        "cpi,xi->cxp", spec_im, x_sin, precision=precise
    )
    wide_im = jnp.einsum("cpi,xi->cxp", spec_re, x_sin, precision=precise) + jnp.einsum(
        "cpi,xi->cxp", spec_im, x_cos, precision=precise
    )
    return jnp.stack([wide_re, wide_im])


def plane_inverse(arrived, weight, z_cos, z_sin, y_cos, y_sin):
    chans, planes = (arrived.shape[1], arrived.shape[2])
    shaped = arrived.reshape(2, chans, planes, KY, KZ)
    wide_re, wide_im = (shaped[0], shaped[1])
    plane_re = jnp.einsum("cxjk,yj->cxky", wide_re, y_cos, precision=precise) - jnp.einsum(
        "cxjk,yj->cxky", wide_im, y_sin, precision=precise
    )
    plane_im = jnp.einsum("cxjk,yj->cxky", wide_re, y_sin, precision=precise) + jnp.einsum(
        "cxjk,yj->cxky", wide_im, y_cos, precision=precise
    )
    plane_re = plane_re * weight[:, None]
    plane_im = plane_im * weight[:, None]
    return jnp.einsum("cxky,zk->cxyz", plane_re, z_cos, precision=precise) - jnp.einsum(
        "cxky,zk->cxyz", plane_im, z_sin, precision=precise
    )


def on_device_any(field, cotangent, spec_weight, bypass_weight):
    count = lax.axis_size("slab")
    pairs = KY * KZ // count
    chans = field.shape[1]
    z_cos, z_sin = wave_tables(GZ, KZ, False)
    y_cos, y_sin = wave_tables(GY, KY, True)
    x_cos, x_sin = wave_tables(GX, KX, True)
    kz_index = jnp.arange(KZ, dtype=jnp.int32)
    fold = jnp.where(kz_index == 0, 1.0, 2.0).astype(jnp.float32) / float(GX * GY * GZ)
    ones = jnp.ones((KZ,), jnp.float32)
    weights = spec_weight.reshape(2, chans, pairs, KX, chans)
    w_real = weights[0]
    w_imag = weights[1]
    source = field[0]
    local_spec = plane_spectrum(source, ones, z_cos, z_sin, y_cos, y_sin)
    moved = lax.all_to_all(local_spec, "slab", split_axis=3, concat_axis=2, tiled=True)
    hat_re, hat_im = along_first(moved, x_cos, x_sin)
    mix_re = jnp.einsum("cpi,cpio->opi", hat_re, w_real, precision=precise) - jnp.einsum(
        "cpi,cpio->opi", hat_im, w_imag, precision=precise
    )
    mix_im = jnp.einsum("cpi,cpio->opi", hat_re, w_imag, precision=precise) + jnp.einsum(
        "cpi,cpio->opi", hat_im, w_real, precision=precise
    )
    outgoing = back_first(mix_re, mix_im, x_cos, x_sin)
    arrived = lax.all_to_all(outgoing, "slab", split_axis=2, concat_axis=3, tiled=True)
    spectral = plane_inverse(arrived, fold, z_cos, z_sin, y_cos, y_sin)
    pre = spectral + jnp.einsum("co,cxyz->oxyz", bypass_weight, source, precision=precise)
    result, pullback = jax.vjp(gelu_exact, pre)
    grad_pre = pullback(cotangent[0])[0]
    fold_grid = jnp.broadcast_to(fold, (KY, KZ))
    cot_spec = plane_spectrum(grad_pre, fold_grid, z_cos, z_sin, y_cos, y_sin)
    cot_moved = lax.all_to_all(cot_spec, "slab", split_axis=3, concat_axis=2, tiled=True)
    grad_re, grad_im = along_first(cot_moved, x_cos, x_sin)
    own_real = jnp.einsum("cpi,opi->cpio", hat_re, grad_re, precision=precise) + jnp.einsum(
        "cpi,opi->cpio", hat_im, grad_im, precision=precise
    )
    own_imag = jnp.einsum("cpi,opi->cpio", hat_re, grad_im, precision=precise) - jnp.einsum(
        "cpi,opi->cpio", hat_im, grad_re, precision=precise
    )
    summed = lax.psum(jnp.stack([own_real, own_imag]), "dp")
    grad_spec = summed.reshape(2, chans, pairs, KX * chans)
    input_re = jnp.einsum("opi,cpio->cpi", grad_re, w_real, precision=precise) + jnp.einsum(
        "opi,cpio->cpi", grad_im, w_imag, precision=precise
    )
    input_im = jnp.einsum("opi,cpio->cpi", grad_im, w_real, precision=precise) - jnp.einsum(
        "opi,cpio->cpi", grad_re, w_imag, precision=precise
    )
    grad_out = back_first(input_re, input_im, x_cos, x_sin)
    grad_arrived = lax.all_to_all(grad_out, "slab", split_axis=2, concat_axis=3, tiled=True)
    back_field = plane_inverse(grad_arrived, ones, z_cos, z_sin, y_cos, y_sin)
    back_field = back_field + jnp.einsum(
        "co,oxyz->cxyz", bypass_weight, grad_pre, precision=precise
    )
    return (result[None], back_field[None], grad_spec)


CH = 32
PLANES = 8
PAIRS = 32
PEERS = 16
KYL = PAIRS // KZ
KYH = KY // KYL
QUAD = 4
GROUPS = CH // QUAD
TILE = QUAD * PAIRS
PER = 2
BLOCKS = QUAD * KYL
WIDE = BLOCKS * 2 * GZ
ROWS = PLANES * KYH
MODES_O = KX * CH

VMEM = 52 * 1024 * 1024

BF = jnp.bfloat16
F32 = jnp.float32


def split_table(table):
    high = table.astype(ml_dtypes.bfloat16)
    low = (table - high.astype(np.float64)).astype(ml_dtypes.bfloat16)
    return high, low


def phases(length, count, signed):
    freqs = np.arange(count)
    if signed:
        freqs = np.where(freqs < count // 2, freqs, freqs - count)
    phase = (np.arange(length)[:, None] * freqs[None, :]) % length
    angle = phase * (2.0 * np.pi / length)
    return np.cos(angle), np.sin(angle)


@functools.lru_cache(maxsize=None)
def host_tables():
    zc, zs = phases(GZ, KZ, False)
    yc, ys = phases(GY, KY, True)
    xc, xs = phases(GX, KX, True)
    fold = np.where(np.arange(KZ) == 0, 1.0, 2.0) / float(GX * GY * GZ)
    out = {}
    ycr = yc.T.reshape(KYH, KYL, GY).transpose(1, 0, 2)
    ysr = ys.T.reshape(KYH, KYL, GY).transpose(1, 0, 2)
    fwd = np.stack([ycr, -ysr], axis=1).reshape(2 * KY, GY)
    high, low = split_table(fwd)
    out["yf"] = np.block([[high, high], [low, low]])
    inv = np.stack([ycr, -ysr], axis=1).reshape(2 * KY, GY).T
    high, low = split_table(inv)
    out["yi"] = np.concatenate([high, high, low], axis=1)
    core = np.stack([np.stack([zc, -zs]), np.stack([zs, zc])])
    for name, scale in (("zf", np.ones(KZ)), ("zg", fold)):
        table = (core * scale).transpose(0, 2, 1, 3)[:, :, :, None, :]
        table = np.broadcast_to(table, (2, GZ, 2, BLOCKS, KZ))
        high, low = split_table(table.reshape(2 * GZ, 2 * TILE))
        out[name] = np.stack([high, low])
    core = np.stack([np.stack([zc, zs]), np.stack([-zs, zc])])
    for name, scale in (("zi", fold), ("zj", np.ones(KZ))):
        table = np.zeros((2, QUAD, KYL, KZ, QUAD, KYL, 2, GZ))
        for q in range(QUAD):
            for k in range(KYL):
                table[:, q, k, :, q, k, :, :] = (core * scale).transpose(0, 3, 1, 2)
        out[name + "h"], out[name + "l"] = split_table(table.reshape(2 * TILE, WIDE))
    core = np.stack([np.stack([xc, xs]), np.stack([-xs, xc])])
    table = core.reshape(2, 2, PEERS, PLANES, KX).transpose(0, 4, 2, 1, 3).reshape(2 * KX, 2 * GX)
    high, low = split_table(table)
    out["xfh"], out["xfl"] = high, low
    core = np.stack([np.stack([xc, -xs]), np.stack([xs, xc])])
    table = core.reshape(2, 2, PEERS, PLANES, KX).transpose(2, 0, 3, 1, 4).reshape(2 * GX, 2 * KX)
    high, low = split_table(table)
    out["xi"] = np.concatenate([high, high, low], axis=1)
    spread = np.repeat(np.eye(2 * KX), CH, axis=1).astype(ml_dtypes.bfloat16)
    out["spread"] = np.concatenate([spread, spread], axis=0)
    out["rep"] = np.repeat(np.eye(CH), 8, axis=0).astype(ml_dtypes.bfloat16)
    out["gather"] = np.concatenate([spread, spread], axis=0).T.copy()
    return out


def halves(values):
    high = values.astype(BF)
    return high, (values - high.astype(F32)).astype(BF)


def dot(left, right):
    return jnp.dot(left, right, preferred_element_type=F32)


def lines_to_modes(pair, yf):
    high, low = halves(pair)
    both = dot(yf, jnp.concatenate([high, low], axis=0))
    return halves(both[: 2 * KY] + both[2 * KY :])


def call(body, us, grid, ins, outs, shapes, scratch, aliases=None, vmem=VMEM):
    return pl.pallas_call(
        body,
        grid=grid,
        in_specs=ins,
        out_specs=outs,
        out_shape=shapes,
        scratch_shapes=scratch,
        input_output_aliases=aliases or {},
        cost_estimate=pl.CostEstimate(flops=int(us * 1e9), bytes_accessed=int(us * 3e6), transcendentals=0),
        compiler_params=pltpu.CompilerParams(
            dimension_semantics=("arbitrary",), vmem_limit_bytes=vmem
        ),
    )


def whole(array):
    zeros = (0,) * array.ndim
    return pl.BlockSpec(array.shape, lambda step: zeros)


def store_modes(high, low, x, half, high_s, low_s):
    for j in range(2):
        for k in range(KYL):
            to = ((2 * half + j) * KYL + k) * ROWS + x * KYH
            for part in range(2):
                rows = slice((2 * k + part) * KYH, (2 * k + part + 1) * KYH)
                take = (rows, slice(j * GZ, (j + 1) * GZ))
                put = (slice(to, to + KYH), slice(part * GZ, (part + 1) * GZ))
                high_s[put] = high[take]
                low_s[put] = low[take]


def send_modes(high_s, low_s, table_ref, out_ref):
    high, low = high_s[...], low_s[...]
    full = dot(high, table_ref[0]) + dot(low, table_ref[0]) + dot(high, table_ref[1])
    owner = lax.broadcasted_iota(jnp.int32, (ROWS, 2 * TILE), 1) % TILE // KZ
    sums = full[:ROWS]
    for i in range(1, BLOCKS):
        sums = jnp.where(owner == i, full[i * ROWS : (i + 1) * ROWS], sums)
    for part in range(2):
        block = sums[:, part * TILE : (part + 1) * TILE].reshape(PLANES, KYH, TILE)
        out_ref[:, part * PLANES : (part + 1) * PLANES, :] = jnp.swapaxes(block, 0, 1)


def spectrum_body(f_ref, yf_ref, table_ref, out_ref, high_s, low_s):
    yf = yf_ref[...]
    for x in range(PLANES):
        for half in range(2):
            pair = jnp.concatenate([f_ref[2 * half, x], f_ref[2 * half + 1, x]], axis=1)
            high, low = lines_to_modes(pair, yf)
            store_modes(high, low, x, half, high_s, low_s)
    send_modes(high_s, low_s, table_ref, out_ref)


def channel_block(first):
    return pl.BlockSpec((QUAD, PLANES, GY, GZ), lambda g: (g + first, 0, 0, 0))


def moved_block(per=1):
    return pl.BlockSpec((PEERS, 2 * PLANES, per * TILE), lambda g: (0, 0, g))


def weight_block(at):
    return pl.BlockSpec((2, PER * QUAD, PAIRS, MODES_O), lambda g: (0, g + at // PER, 0, 0))


def hat_block(at):
    return pl.BlockSpec((2 * KX, PER * TILE), lambda g: (0, g + at // PER))


def moved_shape(groups):
    return jax.ShapeDtypeStruct((PEERS, 2 * PLANES, groups * TILE), F32)


def mode_scratch():
    return [pltpu.VMEM((BLOCKS * ROWS, 2 * GZ), BF), pltpu.VMEM((BLOCKS * ROWS, 2 * GZ), BF)]


def spectrum(field, first, count, t):
    tables = (t["yf"], t["zf"])
    return call(
        spectrum_body,
        2 * count,
        (count,),
        [channel_block(first)] + [whole(a) for a in tables],
        moved_block(),
        moved_shape(count),
        mode_scratch(),
        vmem=58 * 1024 * 1024,
    )(field, *tables)


def own_mask():
    rows = lax.broadcasted_iota(jnp.int32, (TILE, TILE), 0) % QUAD
    lanes = lax.broadcasted_iota(jnp.int32, (TILE, TILE), 1) // PAIRS
    return rows == lanes


def x_forward(moved, xfh, xfl):
    high, low = halves(moved)
    both = dot(jnp.concatenate([xfh, xfl], axis=0), high)
    return both[: 2 * KX] + both[2 * KX :] + dot(xfh, low)


def x_inverse(spec, xi):
    high, low = halves(spec)
    return dot(xi, jnp.concatenate([high, low, high], axis=0))


def spread_modes(spec, spread):
    turned = jnp.concatenate([spec, spec], axis=0).T
    high, low = halves(turned)
    lanes = lax.broadcasted_iota(jnp.int32, (TILE, 4 * KX), 1)
    return dot(jnp.where(lanes < 2 * KX, high, low), spread)


def mix_body(first, last, count, *refs):
    moved_ref, w_ref, xfh_ref, xfl_ref, spread_ref, xi_ref = refs[:6]
    refs = refs[6:]
    if not first:
        start_ref, refs = refs[0], refs[2:]
    hat_ref, refs = refs[0], refs[1:]
    if last:
        out_refs, (acc_s, turn_s) = refs[:-2], refs[-2:]
    else:
        (acc_s,) = refs
    step = pl.program_id(0)

    @pl.when(step == 0)
    def _():
        acc_s[...] = jnp.zeros_like(acc_s) if first else start_ref[...]

    hat = x_forward(moved_ref[...].reshape(2 * GX, PER * TILE), xfh_ref[...], xfl_ref[...])
    hat_ref[...] = hat
    acc_re, acc_im = acc_s[0], acc_s[1]
    for u in range(PER):
        wide = spread_modes(hat[:, u * TILE : (u + 1) * TILE], spread_ref[...])
        for q in range(QUAD):
            h_re = wide[q * PAIRS : (q + 1) * PAIRS, :MODES_O]
            h_im = wide[q * PAIRS : (q + 1) * PAIRS, MODES_O:]
            w_re, w_im = w_ref[0, u * QUAD + q], w_ref[1, u * QUAD + q]
            acc_re = acc_re + (h_re * w_re - h_im * w_im)
            acc_im = acc_im + (h_re * w_im + h_im * w_re)
    acc_s[0] = acc_re
    acc_s[1] = acc_im

    if last:

        @pl.when(step == count - 1)
        def _():
            mask = own_mask()
            for part in range(2):
                full = jnp.concatenate([acc_s[part]] * QUAD, axis=0)
                for k in range(MODES_O // TILE):
                    turned = full[:, k * TILE : (k + 1) * TILE].T
                    turn_s[pl.ds(part * MODES_O + k * TILE, TILE), :] = jnp.where(mask, turned, 0.0)
            xi = xi_ref[...]
            per = GROUPS // len(out_refs)
            for g in range(0, GROUPS, 2):
                tiles = []
                for h in range(g, g + 2):
                    parts = []
                    for part in range(2):
                        total = None
                        for q in range(QUAD):
                            rows = turn_s[pl.ds(part * MODES_O + h * QUAD + q, KX, stride=CH), :]
                            total = rows if total is None else total + rows
                        parts.append(total)
                    tiles.append(jnp.concatenate(parts, axis=0))
                wave = x_inverse(jnp.concatenate(tiles, axis=1), xi).reshape(PEERS, 2 * PLANES, 2 * TILE)
                for h in range(g, g + 2):
                    to = (h % per) * TILE
                    out_refs[h // per][:, :, to : to + TILE] = wave[:, :, (h - g) * TILE : (h - g + 1) * TILE]


def mix(moved, weights, so_far, at, count, chunks, t):
    first, last = not so_far, at + count == GROUPS
    tables = (t["xfh"], t["xfl"], t["spread"], t["xi"])
    hat = jax.ShapeDtypeStruct((2 * KX, CH * PAIRS), F32)
    acc = jax.ShapeDtypeStruct((2, PAIRS, MODES_O), F32)
    outs = [moved_shape(n) for n in chunks] if last else [acc]
    scratch = [pltpu.VMEM(acc.shape, F32), pltpu.VMEM((2 * MODES_O, TILE), F32)] if last else []
    before = [] if first else [whole(acc), pl.BlockSpec(memory_space=pl.ANY)]
    return call(
        functools.partial(mix_body, first, last, count // PER),
        5,
        (count // PER,),
        [moved_block(PER), weight_block(at)] + [whole(a) for a in tables] + before,
        [hat_block(at)] + [whole(a) for a in outs],
        [hat] + outs,
        scratch,
        aliases={} if first else {7: 0},
        vmem=48 * 1024 * 1024,
    )(moved, weights, *tables, *so_far)


def input_body(first, moved_refs, g_ref, w_ref, xfh_ref, xfl_ref, gather_ref, xi_ref, out_ref, turn_s):
    if first:

        @pl.when(pl.program_id(0) == 0)
        def _():
            lanes = lax.broadcasted_iota(jnp.int32, (KX, TILE), 1) // PAIRS
            per = GROUPS // len(moved_refs)
            for h in range(GROUPS):
                at = (h % per) * TILE
                tile = moved_refs[h // per][:, :, at : at + TILE].reshape(2 * GX, TILE)
                hat = x_forward(tile, xfh_ref[...], xfl_ref[...])
                for part in range(2):
                    rows = hat[part * KX : (part + 1) * KX]
                    for q in range(QUAD):
                        to = pl.ds(part * MODES_O + h * QUAD + q, KX, stride=CH)
                        turn_s[to, :] = jnp.where(lanes == q, rows, 0.0)
            for part in range(2):
                for k in range(MODES_O // TILE):
                    turned = turn_s[pl.ds(part * MODES_O + k * TILE, TILE), :].T
                    total = turned[:PAIRS]
                    for q in range(1, QUAD):
                        total = total + turned[q * PAIRS : (q + 1) * PAIRS]
                    g_ref[part, :, k * TILE : (k + 1) * TILE] = total

    g_re, g_im = g_ref[0], g_ref[1]
    rows_high, rows_low = [], []
    for c in range(PER * QUAD):
        w_re, w_im = w_ref[0, c], w_ref[1, c]
        full = jnp.concatenate([g_re * w_re + g_im * w_im, g_im * w_re - g_re * w_im], axis=1)
        high, low = halves(full)
        rows_high.append(high)
        rows_low.append(low)
    both = dot(jnp.concatenate(rows_high + rows_low, axis=0), gather_ref[...])
    both = both[: PER * TILE] + both[PER * TILE :]
    spec = jnp.concatenate([both[u * TILE : (u + 1) * TILE].T[: 2 * KX] for u in range(PER)], axis=1)
    out_ref[...] = x_inverse(spec, xi_ref[...]).reshape(PEERS, 2 * PLANES, PER * TILE)


def input_modes(moved, grad, weights, at, count, t):
    tables = (t["xfh"], t["xfl"], t["gather"], t["xi"])
    shape = jax.ShapeDtypeStruct((2, PAIRS, MODES_O), F32)
    first = grad is None
    if first:

        def body(*refs):
            n = len(moved)
            w, xfh, xfl, gather, xi, g, out, turn = refs[n:]
            input_body(True, refs[:n], g, w, xfh, xfl, gather, xi, out, turn)

        return call(
            body,
            7,
            (count // PER,),
            [whole(a) for a in moved] + [weight_block(at)] + [whole(a) for a in tables],
            [whole(shape), moved_block(PER)],
            [shape, moved_shape(count)],
            [pltpu.VMEM((2 * MODES_O, TILE), F32)],
        )(*moved, weights, *tables)

    def body(g, w, xfh, xfl, gather, xi, out):
        input_body(False, None, g, w, xfh, xfl, gather, xi, out, None)

    out = call(
        body,
        6,
        (count // PER,),
        [whole(shape), weight_block(at)] + [whole(a) for a in tables],
        moved_block(PER),
        moved_shape(count),
        [],
    )(grad, weights, *tables)
    return grad, out


def weight_grad_body(hat_ref, far_hat_ref, g_ref, far_g_ref, spread_ref, *refs):
    out_ref = refs[-1]
    spread = spread_ref[...]
    for u in range(PER):
        lanes = slice(u * TILE, (u + 1) * TILE)
        near = spread_modes(hat_ref[:, lanes], spread)
        far = spread_modes(far_hat_ref[:, lanes], spread)
        for q in range(QUAD):
            rows = slice(q * PAIRS, (q + 1) * PAIRS)
            n_re, n_im = near[rows, :MODES_O], near[rows, MODES_O:]
            f_re, f_im = far[rows, :MODES_O], far[rows, MODES_O:]
            c = u * QUAD + q
            out_ref[0, c] = n_re * g_ref[0] + n_im * g_ref[1] + f_re * far_g_ref[0] + f_im * far_g_ref[1]
            out_ref[1, c] = n_re * g_ref[1] - n_im * g_ref[0] + f_re * far_g_ref[1] - f_im * far_g_ref[0]


def weight_grad(hat, far_hat, grad, far_grad, at, count, so_far, t):
    return call(
        weight_grad_body,
        count,
        (count // PER,),
        [hat_block(at), hat_block(at), whole(grad), whole(far_grad), whole(t["spread"])]
        + [pl.BlockSpec(memory_space=pl.ANY)] * len(so_far),
        weight_block(at),
        jax.ShapeDtypeStruct((2, CH, PAIRS, MODES_O), F32),
        [],
        aliases={5 + i: i for i in range(len(so_far))},
    )(hat, far_hat, grad, far_grad, t["spread"], *so_far)


def gelu_parts(pre):
    bell = jnp.exp2(pre * pre * (-0.5 * math.log2(math.e)))
    rate = 0.3275911 * math.sqrt(0.5)
    t = 1.0 / (jnp.abs(pre) + 1.0 / rate)
    poly = 1.061405429 * 0.5 / rate**5
    for power, coefficient in zip((4, 3, 2, 1), (-1.453152027, 1.421413741, -0.284496736, 0.254829592)):
        poly = poly * t + coefficient * 0.5 / rate**power
    tail = poly * t * bell
    share = jnp.where(pre >= 0.0, 1.0 - tail, tail)
    return share, pre * bell * (1.0 / math.sqrt(2.0 * math.pi))


def arrive(arrived_ref, zih, zil):
    parts = []
    for part in range(2):
        block = arrived_ref[:, part * PLANES : (part + 1) * PLANES, :]
        parts.append(jnp.swapaxes(block, 0, 1).reshape(PLANES * KYH, TILE))
    high, low = halves(jnp.concatenate(parts, axis=1))
    tables = jnp.concatenate([zih, zih, zil], axis=0)
    return halves(dot(jnp.concatenate([high, low, high], axis=1), tables))


def inverse_pair(high, low, x, half, yi):
    stacks = []
    for source in (high, low):
        sides = []
        for j in range(2):
            lanes = (2 * half + j) * 2 * KYL * GZ
            pieces = [
                source[x * KYH : (x + 1) * KYH, lanes + k * GZ : lanes + (k + 1) * GZ] for k in range(2 * KYL)
            ]
            sides.append(jnp.concatenate(pieces, axis=0))
        stacks.append(jnp.concatenate(sides, axis=1))
    return dot(yi, jnp.concatenate([stacks[0], stacks[1], stacks[0]], axis=0))


def kron_halves(matrix, rep):
    rows = lax.broadcasted_iota(jnp.int32, (8 * CH, 8 * CH), 0) % 8
    lanes = lax.broadcasted_iota(jnp.int32, (8 * CH, 8 * CH), 1) % 8
    wide = []
    for half in halves(matrix):
        tall = dot(rep, half).astype(BF)
        full = lax.dot_general(tall, rep, (((1,), (1,)), ((), ())), preferred_element_type=F32)
        wide.append(jnp.where(rows == lanes, full, 0.0).astype(BF))
    return jnp.concatenate(wide, axis=0)


def channel_sum_body(data_ref, matrix_ref, rep_ref, *refs):
    out_ref, kron_s = refs[-2:]

    @pl.when(pl.program_id(0) == 0)
    def _():
        kron_s[...] = kron_halves(matrix_ref[...], rep_ref[...])

    for x in range(data_ref.shape[1]):
        for i in range(GY // 16):
            tiles = [data_ref[:, x, i * 16 + 8 * j : i * 16 + 8 * j + 8, :].reshape(8 * CH, GZ) for j in range(2)]
            high, low = halves(jnp.concatenate(tiles, axis=1))
            both = dot(kron_s[...], high)
            sums = both[: 8 * CH] + both[8 * CH :] + dot(kron_s[: 8 * CH], low)
            for j in range(2):
                at = slice(i * 16 + 8 * j, i * 16 + 8 * j + 8)
                out_ref[:, x, at, :] = sums[:, j * GZ : (j + 1) * GZ].reshape(CH, 8, GZ)


def channel_sum(data, matrix, first, count, step, so_far, t):
    block = pl.BlockSpec((CH, step, GY, GZ), lambda x: (0, x + first // step, 0, 0))
    return call(
        channel_sum_body,
        2 * count,
        (count // step,),
        [block, whole(matrix), whole(t["rep"])] + [pl.BlockSpec(memory_space=pl.ANY)] * len(so_far),
        block,
        jax.ShapeDtypeStruct(data.shape, F32),
        [pltpu.VMEM((16 * CH, 8 * CH), BF)],
        aliases={3 + i: i for i in range(len(so_far))},
    )(data, matrix, t["rep"], *so_far)


def middle_body(
    arrived_ref, sum_ref, cot_ref, yi_ref, zih_ref, zil_ref, yf_ref, zg_ref, *refs
):
    out_ref, grad_ref, spec_ref, high_s, low_s = refs[-5:]
    high, low = arrive(arrived_ref, zih_ref[...], zil_ref[...])
    yi, yf = yi_ref[...], yf_ref[...]
    for x in range(PLANES):
        for half in range(2):
            waves = inverse_pair(high, low, x, half, yi)
            grads = []
            for j in range(2):
                c = 2 * half + j
                pre = waves[:, j * GZ : (j + 1) * GZ] + sum_ref[c, x]
                share, slope = gelu_parts(pre)
                out_ref[c, x] = pre * share
                grad = cot_ref[c, x] * (share + slope)
                grad_ref[c, x] = grad
                grads.append(grad)
            store_modes(*lines_to_modes(jnp.concatenate(grads, axis=1), yf), x, half, high_s, low_s)
    send_modes(high_s, low_s, zg_ref, spec_ref)


def middle(arrived, sums, cotangent, first, count, so_far, t):
    tables = (t["yi"], t["zih"], t["zil"], t["yf"], t["zg"])
    block = channel_block(first)
    shape = jax.ShapeDtypeStruct(sums.shape, F32)
    n = 3 + len(tables)
    return call(
        middle_body,
        5 * count,
        (count,),
        [moved_block(), block, block] + [whole(a) for a in tables] + [pl.BlockSpec(memory_space=pl.ANY)] * len(so_far),
        [block, block, moved_block()],
        [shape, shape, moved_shape(count)],
        mode_scratch(),
        aliases={n + i: i for i in range(len(so_far))},
    )(arrived, sums, cotangent, *tables, *so_far)


def last_body(arrived_ref, sum_ref, yi_ref, zjh_ref, zjl_ref, *refs):
    out_ref = refs[-1]
    high, low = arrive(arrived_ref, zjh_ref[...], zjl_ref[...])
    yi = yi_ref[...]
    for x in range(PLANES):
        for half in range(2):
            waves = inverse_pair(high, low, x, half, yi)
            for j in range(2):
                c = 2 * half + j
                out_ref[c, x] = waves[:, j * GZ : (j + 1) * GZ] + sum_ref[c, x]


def last(arrived, sums, first, count, so_far, t):
    tables = (t["yi"], t["zjh"], t["zjl"])
    block = channel_block(first)
    n = 2 + len(tables)
    return call(
        last_body,
        2.5 * count,
        (count,),
        [moved_block(), block] + [whole(a) for a in tables] + [pl.BlockSpec(memory_space=pl.ANY)] * len(so_far),
        block,
        jax.ShapeDtypeStruct(sums.shape, F32),
        [],
        aliases={n + i: i for i in range(len(so_far))},
    )(arrived, sums, *tables, *so_far)


def swap_slabs(array):
    return lax.all_to_all(array, "slab", split_axis=0, concat_axis=0, tiled=True)


CHUNKS = (4, 4)
STARTS = tuple(sum(CHUNKS[:k]) for k in range(len(CHUNKS)))


def on_device(field, cotangent, spec_weight, bypass_weight):
    shape = (field.shape[1], field.shape[2], spec_weight.shape[2], lax.axis_size("slab"), lax.axis_size("dp"))
    if shape != (CH, PLANES, PAIRS, PEERS, 2):
        return on_device_any(field, cotangent, spec_weight, bypass_weight)
    t = {name: jnp.asarray(table) for name, table in host_tables().items()}
    source, other = field[0], cotangent[0]
    swap_pair = [(0, 1), (1, 0)]
    parts = list(zip(STARTS, CHUNKS))
    ahead = lax.optimization_barrier

    turned = bypass_weight.T
    moved, sums = [], ()
    for at, n in parts:
        sent = spectrum(source, at, n, t)
        if moved:
            sums = (channel_sum(source, turned, 0, 2, 1, (), t),)
            moved[-1], sent, *sums = ahead((moved[-1], sent, *sums))
        moved.append(swap_slabs(sent))
    sums = (channel_sum(source, turned, 2, 4, 1, tuple(sums), t),)
    moved[-1], *sums = ahead((moved[-1], *sums))
    hat, state = None, ()
    for arrived, (at, n) in zip(moved, parts):
        hat, *state = mix(arrived, spec_weight, (*state, hat) if state else (), at, n, CHUNKS, t)
    far_hat = lax.ppermute(hat, "dp", swap_pair)
    sums = channel_sum(source, turned, 6, 2, 1, tuple(sums), t)
    so_far, cot_moved, arrived = (), [], []
    for sent in state:
        if arrived:
            arrived[-1], sums, sent = ahead((arrived[-1], sums, sent))
        arrived.append(swap_slabs(sent))
    for k, (at, n) in enumerate(parts):
        *so_far, sent = middle(arrived[k], sums, other, at, n, so_far, t)
        if k == 0:
            arrived[-1], sent = ahead((arrived[-1], sent))
        else:
            cot_moved[-1], sent = ahead((cot_moved[-1], sent))
        cot_moved.append(swap_slabs(sent))
    result, grad_pre = so_far
    back_sums = channel_sum(grad_pre, bypass_weight, 0, 6, 2, (), t)
    cot_moved[-1], back_sums, far_hat = ahead((cot_moved[-1], back_sums, far_hat))
    grad, back_arrived = None, []
    for at, n in parts:
        grad, sent = input_modes(cot_moved, grad, spec_weight, at, n, t)
        if back_arrived:
            back_sums = channel_sum(grad_pre, bypass_weight, 6, 2, 1, (back_sums,), t)
            made = weight_grad(hat, far_hat, grad, far_grad, 0, PER, (), t)
            back_arrived[-1], sent, back_sums, made = ahead((back_arrived[-1], sent, back_sums, made))
        else:
            far_grad = lax.ppermute(grad, "dp", swap_pair)
        back_arrived.append(swap_slabs(sent))
    grad_spec = weight_grad(hat, far_hat, grad, far_grad, PER, GROUPS - PER, (made,), t)
    back = ()
    for k, (at, n) in enumerate(parts):
        if k == 1:
            back_arrived[k], back, grad_spec = ahead((back_arrived[k], back, grad_spec))
        back = (last(back_arrived[k], back_sums, at, n, back, t),)
    return (result[None], back[0][None], grad_spec)


def solution(mesh):
    in_specs = (
        P("dp", None, "slab", None, None),
        P("dp", None, "slab", None, None),
        P(None, None, "slab", None),
        P(),
    )
    out_specs = (
        P("dp", None, "slab", None, None),
        P("dp", None, "slab", None, None),
        P(None, None, "slab", None),
    )
    return jax.shard_map(
        on_device, mesh=mesh, in_specs=in_specs, out_specs=out_specs, check_vma=False
    )
```
